32 devices in a mesh: band: 16 (over z, y, core), strip: 2 (over x).
Axes of the slice: x: 2, y: 2, z: 4, core: 2. Of those that a mesh axis runs over, the one named last changes fastest.
Arguments:
- activations: bfloat16 [16, 320, 12, 128], P('band', None, 'strip'), may hold values from -6 to 6
- out_grad: bfloat16 [16, 320, 12, 128], P('band', None, 'strip'), may hold values from -6 to 6
- kernel: bfloat16 [320, 9, 320], P('band', None, 'strip'), may hold values from -0.109375 to 0.109375
Outputs:
- input_grad: bfloat16 [16, 320, 12, 128], P('band', None, 'strip')
- kernel_grad: float32 [320, 9, 320], P('band', None, 'strip')
The draws below stay inside these ranges and needn't reach their ends.
All inputs are finite; a program needn't handle non-finite values.
Results may differ from the reference program's by a relative error of at most 0.001.
Values may be sent and summed in bfloat16 or wider, within the bound.
No kernel may reach another device: no remote copies, remote signals or barrier semaphores. Data moves between devices by JAX's collectives and lax.ppermute only.
A program may use at most 64 MiB of HBM per device.

```python
import math
import jax
import jax.numpy as jnp
from jax import lax

CH = 320
TAPS = 9
WIDTH = 128
IMAGES = 16
HEIGHT = 12


def with_spikes(result, rng, source, target, blocks, factor):
    def block_of(dim):
        return (jnp.arange(result.shape[dim]) // (result.shape[dim] // blocks)).reshape((-1,) + (1,) * (result.ndim - 1 - dim))

    first = jax.random.permutation(rng, blocks)[block_of(target)]
    second = (block_of(target) + blocks // 2) % blocks
    return jnp.where((block_of(source) == first) | (block_of(source) == second), factor * result, result)


def block_scale(own_key, dims, shards, least, largest):
    def one(axis_at, parts):
        heights = jax.random.uniform(jax.random.fold_in(jax.random.fold_in(own_key, 6), axis_at), (parts,), jnp.float32, least / len(shards), largest / len(shards))
        return jnp.repeat(jnp.exp(heights), dims[axis_at] // parts).reshape((-1,) + (1,) * (len(dims) - axis_at - 1))

    loudness = one(*shards[0])
    for cut in shards[1:]:
        loudness = loudness * one(*cut)
    return loudness


def centred(own_key, shape, width, bound, split=(), held_as=jnp.bfloat16):
    factor_of = block_scale(own_key, shape, split, -0.22, 0.18) if split else 1.0
    result = jax.random.normal(own_key, shape, jnp.float32) * width * factor_of
    return jnp.minimum(jnp.maximum(result, -bound), bound).astype(held_as)


def bell_draw_with(own_key, dims, scale, reach, pieces, heavy, kind=jnp.bfloat16):
    result = scale * jax.random.normal(own_key, dims, jnp.float32)
    if pieces:
        result = result * block_scale(own_key, dims, pieces, -0.22, 0.18)
    return jnp.clip(with_spikes(result, jax.random.fold_in(own_key, 3), *heavy), -reach, reach).astype(kind)


def setup_inputs(seed: int = 0) -> dict:
    arg_keys = jax.random.split(jax.random.key(seed), 4)
    return {
        "activations": bell_draw_with(arg_keys[0], (IMAGES, CH, HEIGHT, WIDTH), 1.0, 6.0, ((0, 16), (2, 2)), (0, 1, 16, 2.0)),
        "out_grad": bell_draw_with(arg_keys[1], (IMAGES, CH, HEIGHT, WIDTH), 1.0, 6.0, ((0, 16), (2, 2)), (2, 1, 2, 2.0)),
        "kernel": centred(arg_keys[2], (CH, TAPS, CH), (9 * CH) ** -0.5, 0.109375, ((0, 16), (2, 2))),
    }


OFFSETS = ((-1, -1), (-1, 0), (-1, 1), (0, -1), (0, 0), (0, 1), (1, -1), (1, 0), (1, 1))

def reference(activations, out_grad, kernel):
    images = activations.shape[0]
    channels = activations.shape[1]
    height = activations.shape[2]
    row_len = activations.shape[3]
    grad_scale = 1.0 / math.sqrt(images * height * row_len)

    def per_image(summed, fields):
        act_image, grad_image = fields
        grad_padded = jnp.pad(grad_image, ((0, 0), (1, 1), (1, 1)))
        act_flat = act_image.reshape(channels, height * row_len)
        image_grad = jnp.zeros((channels, height * row_len), jnp.float32)
        for tap_index, (row_step, col_step) in enumerate(OFFSETS):
            shifted = grad_padded[:, 1 - row_step:1 - row_step + height, 1 - col_step:1 - col_step + row_len]
            shifted = shifted.reshape(channels, height * row_len)
            image_grad = image_grad + jnp.dot(kernel[:, tap_index, :], shifted, preferred_element_type=jnp.float32)
            partial_value = jnp.dot(act_flat, shifted.T, preferred_element_type=jnp.float32)
            summed = summed.at[:, tap_index, :].add(partial_value)
        return (summed, image_grad.reshape(channels, height, row_len).astype(jnp.bfloat16))
    start_sum = jnp.zeros((channels, 9, channels), jnp.float32)
    kernel_sum, input_grad = lax.scan(per_image, start_sum, (activations, out_grad))
    return (input_grad, kernel_sum * grad_scale)
```

```python
import functools
import math

import jax
import jax.numpy as jnp
from jax import lax
from jax.experimental import pallas as pl
from jax.experimental.pallas import tpu as pltpu
from jax.sharding import PartitionSpec as P

AXES = ("band", "strip")
TAP_STEPS = (-1, 0, 1)
LANES = 128
TOP_POWER = 2.0**15.5
LEAST_PEAK = 1e-30
VMEM_BYTES = 40 * 2**20


def padded_lanes(count):
    return (count // LANES + 1) * LANES


def swap(value, sizes, band_mask, strip_mask, other_masks=None):
    bands, strips = sizes
    pairs = []
    for b in range(bands):
        for s in range(strips):
            masks = (band_mask, strip_mask)
            if other_masks is not None and b % 2:
                masks = other_masks
            pairs.append((b * strips + s, (b ^ masks[0]) * strips + (s ^ masks[1])))
    return lax.ppermute(value, AXES, pairs)


def call(kernel, out_shape, operands, scratch=(), flops=0):
    moved = sum(x.size * x.dtype.itemsize for x in operands)
    return pl.pallas_call(
        kernel,
        out_shape=out_shape,
        in_specs=[pl.BlockSpec(memory_space=pltpu.VMEM)] * len(operands),
        out_specs=jax.tree.map(lambda _: pl.BlockSpec(memory_space=pltpu.VMEM), out_shape),
        scratch_shapes=list(scratch),
        compiler_params=pltpu.CompilerParams(vmem_limit_bytes=VMEM_BYTES),
        cost_estimate=pl.CostEstimate(flops=flops, bytes_accessed=2 * moved, transcendentals=0),
    )(*operands)


def encoded(peak, value, used):
    lane = lax.broadcasted_iota(jnp.int32, value.shape, value.ndim - 1)
    ratio = value * (TOP_POWER / peak)
    square = ratio * ratio
    power = ratio * jnp.abs(ratio) * square * (square * square)
    return jnp.where(lane < used, power, peak).astype(jnp.bfloat16)


def decoded(message):
    power = message.astype(jnp.float32)
    peak = power[0:1, message.shape[1] - 1 : message.shape[1]]
    root = jnp.sqrt(jnp.sqrt(jnp.sqrt(jnp.abs(power))))
    return jnp.where(power < 0, -root, root) * (peak * (1.0 / TOP_POWER))


def peak_of(value, used):
    lane = lax.broadcasted_iota(jnp.int32, value.shape, value.ndim - 1)
    largest = jnp.max(jnp.where(lane < used, jnp.abs(value), 0.0))
    largest = jnp.maximum(largest * (1.0 + 2.0**-6), LEAST_PEAK)
    return jnp.full((1, 1), largest, jnp.float32).astype(jnp.bfloat16).astype(jnp.float32)


class Plan:
    def __init__(self, images, channels, rows, width, bands, strips):
        self.images, self.channels, self.rows, self.width = images, channels, rows, width
        self.bands, self.strips = bands, strips
        self.sizes = (bands, strips)
        self.depth = channels // bands
        self.cols = channels // strips
        self.blocks = bands // 2
        self.half = channels // 2
        self.strip_bits = strips.bit_length() - 1
        self.band_bits = bands.bit_length() - 1
        assert bands == 1 << self.band_bits and strips == 1 << self.strip_bits
        assert self.band_bits >= 2 and self.strip_bits >= 1
        self.top_strip = 1 << (self.strip_bits - 1)
        self.rest_strip = [1 << k for k in reversed(range(self.strip_bits - 1))]
        self.rest_band = [1 << k for k in range(2, self.band_bits)]
        self.inner = self.blocks // 2
        self.half_used = len(TAP_STEPS) * self.half
        self.half_lanes = padded_lanes(self.half_used)
        self.used = len(TAP_STEPS) * self.cols
        self.lanes = padded_lanes(self.used)
        self.block_rows = len(TAP_STEPS) * self.depth

    def block_of(self, slot, low):
        bits = self.band_bits - 2
        turned = sum(((slot >> k) & 1) << (bits - 1 - k) for k in range(bits))
        return turned * 2 + low

    def slot_of(self, difference):
        bits = self.band_bits - 2
        return sum(((difference >> (k + 1)) & 1) << (bits - 1 - k) for k in range(bits))


def place(plan):
    band, strip = lax.axis_index("band"), lax.axis_index("strip")
    core = band % 2
    low = (band // 2) % 2
    high = strip // plan.top_strip
    return band, strip, core, low, high


def grad_row(plan, grad_ref, top_ref, bottom_ref, image, row, start, strip):
    if row < 0:
        piece = top_ref[image, pl.ds(start, plan.half), :]
        return jnp.where(strip > 0, piece, jnp.zeros_like(piece))
    if row >= plan.rows:
        piece = bottom_ref[image, pl.ds(start, plan.half), :]
        return jnp.where(strip < plan.strips - 1, piece, jnp.zeros_like(piece))
    return grad_ref[image, row, pl.ds(start, plan.half), :]


def moved(value, step):
    width = value.shape[-1]
    if step == 0:
        return value
    lane = lax.broadcasted_iota(jnp.int32, value.shape, value.ndim - 1)
    turned = pltpu.roll(value, (-step) % width, value.ndim - 1)
    inside = lane < width - step if step > 0 else lane >= -step
    return jnp.where(inside, turned, 0.0)


def terms_kernel(plan, sends, act0, act1, grad0, grad1, top0, top1, bottom0, bottom1, out, left, right):
    _, strip, core, low, high = place(plan)
    mine = jnp.where(core == 0, high, low)
    first = 1 - mine if sends else mine
    sources = ((act0, grad0, top0, bottom0), (act1, grad1, top1, bottom1))
    chunks = [(d, n, h) for d in range(2) for n in range(plan.images) for h in range(plan.rows)]
    depth, width = plan.depth, plan.width
    for at, (d, n, h) in enumerate(chunks):
        cells = sources[d][0][n, h].astype(jnp.float32)
        blocks = []
        for m in range(plan.blocks):
            begin = 2 * m * depth
            blocks.append(
                jnp.where(
                    core == 0,
                    cells[begin : begin + depth],
                    cells[begin + depth : begin + 2 * depth],
                )
            )
        for y in range(2):
            pieces = []
            for slot in range(plan.inner):
                for step in TAP_STEPS:
                    pieces.append(moved(blocks[plan.block_of(slot, y)], step))
            left[y, :, at * width : (at + 1) * width] = jnp.concatenate(pieces, axis=0).astype(jnp.bfloat16)
    for q in range(2):
        y = jnp.where(core == 0, q, first)
        x = jnp.where(core == 0, first, q)
        start = pl.multiple_of(x * plan.half, 16)
        for at, (d, n, h) in enumerate(chunks):
            _, grad, top, bottom = sources[d]
            for r, row_step in enumerate(TAP_STEPS):
                right[r * plan.half : (r + 1) * plan.half, at * width : (at + 1) * width] = grad_row(
                    plan, grad, top, bottom, n, h - row_step, start, strip
                )
        total = lax.dot_general(
            left[y], right[...], (((1,), (1,)), ((), ())), preferred_element_type=jnp.float32
        )
        spare = plan.half_lanes - plan.half_used
        total = jnp.concatenate([total, jnp.zeros((total.shape[0], spare), jnp.float32)], axis=1)
        if sends:
            out[q] = encoded(peak_of(total, plan.half_used), total, plan.half_used)
        else:
            out[q] = total


def turn_kernel(plan, keep, message, send, kept):
    _, _, core, low, high = place(plan)
    mine = jnp.where(core == 0, low, high)
    total = keep[1 - mine] + decoded(message[1 - mine])
    send[...] = encoded(peak_of(total, plan.half_used), total, plan.half_used)
    kept[...] = keep[mine] + decoded(message[mine])


def halve_kernel(plan, mask, used, keep, message, send, kept):
    band = lax.axis_index("band")
    side = (band // mask) % 2
    total = keep[...] + decoded(message[...])
    rows = total.shape[0] // 2
    lower, upper = total[:rows], total[rows:]
    given = jnp.where(side == 0, upper, lower)
    send[...] = encoded(peak_of(given, used), given, used)
    kept[...] = jnp.where(side == 0, lower, upper)


def last_kernel(plan, scale, keep, message, out):
    total = (keep[...] + decoded(message[...])) * scale
    depth, cols = plan.depth, plan.cols
    for r in range(len(TAP_STEPS)):
        for c in range(len(TAP_STEPS)):
            out[r * len(TAP_STEPS) + c] = total[c * depth : (c + 1) * depth, r * cols : (r + 1) * cols]


def pack_kernel(plan, kernel, out):
    rows = []
    for c in range(len(TAP_STEPS)):
        pieces = [kernel[r * len(TAP_STEPS) + c].astype(jnp.float32) for r in range(len(TAP_STEPS))]
        pieces.append(jnp.zeros((plan.depth, plan.lanes - plan.used), jnp.float32))
        rows.append(jnp.concatenate(pieces, axis=1))
    out[...] = jnp.concatenate(rows, axis=0).astype(jnp.bfloat16)


def cells_kernel(plan, own, other, grad0, grad1, top0, top1, bottom0, bottom1, out0, out1, left, right):
    band, strip, core, low, high = place(plan)
    depth, width, half, lanes = plan.depth, plan.width, plan.half, plan.half_lanes
    steps = len(TAP_STEPS)
    for x in range(2):
        rows = [[] for _ in TAP_STEPS]
        for m in range(plan.blocks):
            difference = m ^ (band // 2)
            by_row, by_col = difference % 2, x ^ high
            one = jnp.where(core == 0, by_row, by_col)
            two = jnp.where(core == 0, by_col, by_row)
            slot = one * plan.inner + plan.slot_of(difference)
            block = jnp.where(two == 0, own[slot], other[slot]).astype(jnp.float32)
            for c in range(steps):
                rows[c].append(block[c * depth : (c + 1) * depth])
        for c in range(steps):
            left[c * half : (c + 1) * half, x * lanes : (x + 1) * lanes] = jnp.concatenate(
                rows[c], axis=0
            ).astype(jnp.bfloat16)
    sources = ((grad0, top0, bottom0), (grad1, top1, bottom1))
    chunks = [(d, n, h) for d in range(2) for n in range(plan.images) for h in range(plan.rows)]
    for at, (d, n, h) in enumerate(chunks):
        grad, top, bottom = sources[d]
        for x in range(2):
            for r, row_step in enumerate(TAP_STEPS):
                begin = x * lanes + r * half
                right[begin : begin + half, at * width : (at + 1) * width] = grad_row(
                    plan, grad, top, bottom, n, h - row_step, x * half, strip
                )
            begin = x * lanes + steps * half
            right[begin : (x + 1) * lanes, at * width : (at + 1) * width] = jnp.zeros(
                (lanes - steps * half, width), jnp.bfloat16
            )
    group = 2
    for begin in range(0, len(chunks), group):
        part = chunks[begin : begin + group]
        product = jnp.dot(
            left[...],
            right[:, begin * width : (begin + len(part)) * width],
            preferred_element_type=jnp.float32,
        )
        for k, (d, n, h) in enumerate(part):
            total = None
            for c, col_step in enumerate(TAP_STEPS):
                term = moved(product[c * half : (c + 1) * half, k * width : (k + 1) * width], -col_step)
                total = term if total is None else total + term
            (out0, out1)[d][n, h] = total.astype(jnp.bfloat16)


def weave_kernel(plan, mine, theirs, out):
    core = lax.axis_index("band") % 2
    depth = plan.depth
    for n in range(plan.images):
        for h in range(plan.rows):
            a, b = mine[n, h].astype(jnp.float32), theirs[n, h].astype(jnp.float32)
            even, odd = jnp.where(core == 0, a, b), jnp.where(core == 0, b, a)
            pieces = []
            for m in range(plan.blocks):
                pieces += [even[m * depth : (m + 1) * depth], odd[m * depth : (m + 1) * depth]]
            out[n, h] = jnp.concatenate(pieces, axis=0).astype(jnp.bfloat16)


def whole_kernel(plan, kernel):
    sizes, f32 = plan.sizes, jnp.float32
    shape = jax.ShapeDtypeStruct((plan.block_rows, plan.lanes), jnp.bfloat16)
    packed = call(functools.partial(pack_kernel, plan), shape, [kernel])[None]
    for mask in reversed(plan.rest_band):
        packed = jnp.concatenate([packed, swap(packed, sizes, mask, 0)], axis=0)
    if plan.rest_strip:
        packed = packed[None]
        for mask in reversed(plan.rest_strip):
            packed = jnp.concatenate([packed, swap(packed, sizes, 0, mask)], axis=0)
        count = packed.shape[0]
        order = jnp.arange(count) ^ (lax.axis_index("strip") % count)
        packed = jnp.take(packed, order, axis=0)[..., : plan.used]
        packed = packed.reshape(count, plan.inner, plan.block_rows, len(TAP_STEPS), plan.cols)
        packed = packed.transpose(1, 2, 3, 0, 4).reshape(plan.inner, plan.block_rows, plan.half_used)
        packed = jnp.pad(packed, ((0, 0), (0, 0), (0, plan.half_lanes - plan.half_used)))
    by_row, by_col = (2, 0), (0, plan.top_strip)
    packed = jnp.concatenate([packed, swap(packed, sizes, *by_row, other_masks=by_col)], axis=0)
    return packed, swap(packed, sizes, *by_col, other_masks=by_row)


def narrowed(plan, total):
    rows = total.shape[0]
    total = total[:, : plan.half_used].reshape(rows, len(TAP_STEPS), plan.half)
    for mask in plan.rest_strip:
        side = (lax.axis_index("strip") // mask) % 2
        parts = total.reshape(rows, len(TAP_STEPS), 2, total.shape[2] // 2)
        kept = jnp.where(side == 0, parts[:, :, 0], parts[:, :, 1])
        given = jnp.where(side == 0, parts[:, :, 1], parts[:, :, 0])
        total = kept + swap(given, plan.sizes, 0, mask)
    total = total.reshape(rows, plan.used)
    return jnp.pad(total, ((0, 0), (0, plan.lanes - plan.used)))


def kernel_terms(plan, cells, scale):
    sizes, f32 = plan.sizes, jnp.float32
    rows, lanes = plan.inner * plan.block_rows, plan.half_lanes
    depth = 2 * plan.images * plan.rows * plan.width
    scratch = [
        pltpu.VMEM((2, rows, depth), jnp.bfloat16),
        pltpu.VMEM((plan.half_used, depth), jnp.bfloat16),
    ]
    flops = 4 * rows * plan.half_used * depth
    send = call(
        functools.partial(terms_kernel, plan, True),
        jax.ShapeDtypeStruct((2, rows, lanes), jnp.bfloat16), cells, scratch, flops,
    )
    keep = call(
        functools.partial(terms_kernel, plan, False),
        jax.ShapeDtypeStruct((2, rows, lanes), f32), cells, scratch, flops,
    )
    by_row, by_col = (2, 0), (0, plan.top_strip)
    come = swap(send, sizes, *by_col, other_masks=by_row)
    send, keep = call(
        functools.partial(turn_kernel, plan),
        (jax.ShapeDtypeStruct((rows, lanes), jnp.bfloat16), jax.ShapeDtypeStruct((rows, lanes), f32)),
        [keep, come],
    )
    come = swap(send, sizes, *by_row, other_masks=by_col)
    if plan.rest_strip:
        total = keep[:, :] + decoded(come)
        keep = narrowed(plan, total)
        come = jnp.zeros(keep.shape, jnp.bfloat16)
    for mask in plan.rest_band:
        rows //= 2
        send, keep = call(
            functools.partial(halve_kernel, plan, mask, plan.used),
            (
                jax.ShapeDtypeStruct((rows, plan.lanes), jnp.bfloat16),
                jax.ShapeDtypeStruct((rows, plan.lanes), f32),
            ),
            [keep, come],
        )
        come = swap(send, sizes, mask, 0)
    return call(
        functools.partial(last_kernel, plan, scale),
        jax.ShapeDtypeStruct((len(TAP_STEPS) ** 2, plan.depth, plan.cols), f32),
        [keep, come],
    )


def borders(plan, grad):
    strip = lax.axis_index("strip")
    first, last = grad[:, 0], grad[:, plan.rows - 1]
    if plan.strips == 2:
        come = swap(jnp.where(strip == 0, last, first), plan.sizes, 0, 1)
        return [come]
    ends = plan.strips - 1
    return [
        lax.ppermute(last, "strip", [(i, i + 1) for i in range(ends)]),
        lax.ppermute(first, "strip", [(i + 1, i) for i in range(ends)]),
    ]


def body(activations, out_grad, kernel):
    images, channels, rows, width = activations.shape
    bands, strips = lax.axis_size("band"), lax.axis_size("strip")
    plan = Plan(images, channels, rows, width, bands, strips)
    scale = 1.0 / math.sqrt(images * bands * rows * strips * width)
    act = activations.transpose(0, 2, 1, 3)
    grad = out_grad.transpose(0, 2, 1, 3)
    edges = borders(plan, grad)
    act1 = swap(act, plan.sizes, 1, 0)
    grad1 = swap(grad, plan.sizes, 1, 0)
    edges1 = [swap(edge, plan.sizes, 1, 0) for edge in edges]
    near = [grad, grad1, edges[0], edges1[0], edges[-1], edges1[-1]]
    kernel_grad = kernel_terms(plan, [act, act1, *near], scale)
    packed = whole_kernel(plan, kernel.transpose(1, 0, 2))
    depth = 2 * images * rows * width
    shape = jax.ShapeDtypeStruct((images, rows, plan.half, width), jnp.bfloat16)
    mine, given = call(
        functools.partial(cells_kernel, plan),
        (shape, shape),
        [*packed, *near],
        [
            pltpu.VMEM((len(TAP_STEPS) * plan.half, 2 * plan.half_lanes), jnp.bfloat16),
            pltpu.VMEM((2 * plan.half_lanes, depth), jnp.bfloat16),
        ],
        2 * len(TAP_STEPS) * plan.half * 2 * plan.half_lanes * depth,
    )
    theirs = swap(given, plan.sizes, 1, 0)
    input_grad = call(
        functools.partial(weave_kernel, plan),
        jax.ShapeDtypeStruct((images, rows, channels, width), jnp.bfloat16),
        [mine, theirs],
    )
    return input_grad.transpose(0, 2, 1, 3), kernel_grad.transpose(1, 0, 2)


def solution(mesh):
    in_specs = (
        P("band", None, "strip", None),
        P("band", None, "strip", None),
        P("band", None, "strip"),
    )
    out_specs = (P("band", None, "strip", None), P("band", None, "strip"))
    return jax.shard_map(body, mesh=mesh, in_specs=in_specs, out_specs=out_specs, check_vma=False)
```

```python
import functools
import math

import jax
import jax.numpy as jnp
from jax import lax
from jax.experimental import pallas as pl
from jax.experimental.pallas import tpu as pltpu
from jax.sharding import PartitionSpec as P

AXES = ("band", "strip")
TAP_STEPS = (-1, 0, 1)
LANES = 128
TOP_POWER = 2.0**15.5
LEAST_PEAK = 1e-30
VMEM_BYTES = 40 * 2**20
LAST_FLOPS = 10**10


def padded_lanes(count):
    return (count // LANES + 1) * LANES


def swap(value, sizes, band_mask, strip_mask, other_masks=None):
    bands, strips = sizes
    pairs = []
    for b in range(bands):
        for s in range(strips):
            masks = (band_mask, strip_mask)
            if other_masks is not None and b % 2:
                masks = other_masks
            pairs.append((b * strips + s, (b ^ masks[0]) * strips + (s ^ masks[1])))
    return lax.ppermute(value, AXES, pairs)


def call(kernel, out_shape, operands, scratch=(), flops=0, far=0):
    moved = sum(x.size * x.dtype.itemsize for x in operands)
    spaces = [pl.ANY] * far + [pltpu.VMEM] * (len(operands) - far)
    return pl.pallas_call(
        kernel,
        out_shape=out_shape,
        in_specs=[pl.BlockSpec(memory_space=space) for space in spaces],
        out_specs=jax.tree.map(lambda _: pl.BlockSpec(memory_space=pltpu.VMEM), out_shape),
        scratch_shapes=list(scratch),
        compiler_params=pltpu.CompilerParams(vmem_limit_bytes=VMEM_BYTES),
        cost_estimate=pl.CostEstimate(flops=flops, bytes_accessed=2 * moved, transcendentals=0),
    )(*operands)


def encoded(peak, value, used):
    lane = lax.broadcasted_iota(jnp.int32, value.shape, value.ndim - 1)
    ratio = value * (TOP_POWER / peak)
    square = ratio * ratio
    power = ratio * jnp.abs(ratio) * square * (square * square)
    return jnp.where(lane < used, power, peak).astype(jnp.bfloat16)


def decoded(message):
    power = message.astype(jnp.float32)
    peak = power[0:1, message.shape[1] - 1 : message.shape[1]]
    root = jnp.sqrt(jnp.sqrt(jnp.sqrt(jnp.abs(power))))
    return jnp.where(power < 0, -root, root) * (peak * (1.0 / TOP_POWER))


def peak_of(value, used):
    lane = lax.broadcasted_iota(jnp.int32, value.shape, value.ndim - 1)
    largest = jnp.max(jnp.where(lane < used, jnp.abs(value), 0.0))
    largest = jnp.maximum(largest * (1.0 + 2.0**-6), LEAST_PEAK)
    return jnp.full((1, 1), largest, jnp.float32).astype(jnp.bfloat16).astype(jnp.float32)


class Plan:
    def __init__(self, images, channels, rows, width, bands, strips):
        self.images, self.channels, self.rows, self.width = images, channels, rows, width
        self.bands, self.strips = bands, strips
        self.sizes = (bands, strips)
        self.depth = channels // bands
        self.cols = channels // strips
        self.blocks = bands // 2
        self.half = channels // 2
        self.strip_bits = strips.bit_length() - 1
        self.band_bits = bands.bit_length() - 1
        assert bands == 1 << self.band_bits and strips == 1 << self.strip_bits
        assert self.band_bits >= 2 and self.strip_bits >= 1
        self.top_strip = 1 << (self.strip_bits - 1)
        self.rest_strip = [1 << k for k in reversed(range(self.strip_bits - 1))]
        self.rest_band = [1 << k for k in range(2, self.band_bits)]
        self.inner = self.blocks // 2
        self.half_used = len(TAP_STEPS) * self.half
        self.half_lanes = padded_lanes(self.half_used)
        self.used = len(TAP_STEPS) * self.cols
        self.lanes = padded_lanes(self.used)
        self.block_rows = len(TAP_STEPS) * self.depth

    def block_of(self, slot, low):
        bits = self.band_bits - 2
        turned = sum(((slot >> k) & 1) << (bits - 1 - k) for k in range(bits))
        return turned * 2 + low

    def slot_of(self, difference):
        return (difference // 2) % self.inner


def place(plan):
    band, strip = lax.axis_index("band"), lax.axis_index("strip")
    core = band % 2
    low = (band // 2) % 2
    high = strip // plan.top_strip
    return band, strip, core, low, high


def grad_row(plan, grad_ref, top_ref, bottom_ref, image, row, start, strip):
    if row < 0:
        piece = top_ref[image, pl.ds(start, plan.half), :]
        return jnp.where(strip > 0, piece, jnp.zeros_like(piece))
    if row >= plan.rows:
        piece = bottom_ref[image, pl.ds(start, plan.half), :]
        return jnp.where(strip < plan.strips - 1, piece, jnp.zeros_like(piece))
    return grad_ref[image, row, pl.ds(start, plan.half), :]


def moved(value, step):
    width = value.shape[-1]
    if step == 0:
        return value
    lane = lax.broadcasted_iota(jnp.int32, value.shape, value.ndim - 1)
    turned = pltpu.roll(value, (-step) % width, value.ndim - 1)
    inside = lane < width - step if step > 0 else lane >= -step
    return jnp.where(inside, turned, 0.0)


def near_kernel(far0, far1, near0, near1, sems):
    copies = [pltpu.make_async_copy(far0, near0, sems.at[0]), pltpu.make_async_copy(far1, near1, sems.at[1])]
    for copy in copies:
        copy.start()
    for copy in copies:
        copy.wait()


def terms_kernel(plan, sends, act0, grad0, act1, grad1, top0, top1, bottom0, bottom1, out, left, right):
    _, strip, core, low, high = place(plan)
    mine = jnp.where(core == 0, high, low)
    first = 1 - mine if sends else mine
    sources = ((act0, grad0, top0, bottom0), (act1, grad1, top1, bottom1))
    chunks = [(d, n, h) for d in range(2) for n in range(plan.images) for h in range(plan.rows)]
    depth, width = plan.depth, plan.width
    for at, (d, n, h) in enumerate(chunks):
        cells = sources[d][0][n, h].astype(jnp.float32)
        blocks = []
        for m in range(plan.blocks):
            begin = 2 * m * depth
            blocks.append(
                jnp.where(
                    core == 0,
                    cells[begin : begin + depth],
                    cells[begin + depth : begin + 2 * depth],
                )
            )
        for y in range(2):
            pieces = []
            for slot in range(plan.inner):
                for step in TAP_STEPS:
                    pieces.append(moved(blocks[plan.block_of(slot, y)], step))
            left[y, :, at * width : (at + 1) * width] = jnp.concatenate(pieces, axis=0).astype(jnp.bfloat16)
    for q in range(2):
        y = jnp.where(core == 0, q, first)
        x = jnp.where(core == 0, first, q)
        start = pl.multiple_of(x * plan.half, 16)
        for at, (d, n, h) in enumerate(chunks):
            _, grad, top, bottom = sources[d]
            for r, row_step in enumerate(TAP_STEPS):
                right[r * plan.half : (r + 1) * plan.half, at * width : (at + 1) * width] = grad_row(
                    plan, grad, top, bottom, n, h - row_step, start, strip
                )
        total = lax.dot_general(
            left[y], right[...], (((1,), (1,)), ((), ())), preferred_element_type=jnp.float32
        )
        spare = plan.half_lanes - plan.half_used
        total = jnp.concatenate([total, jnp.zeros((total.shape[0], spare), jnp.float32)], axis=1)
        if sends:
            out[q] = encoded(peak_of(total, plan.half_used), total, plan.half_used)
        else:
            out[q] = total


def turn_kernel(plan, sends, keep, message, out):
    _, _, core, low, high = place(plan)
    mine = jnp.where(core == 0, low, high)
    if sends:
        total = keep[1 - mine] + decoded(message[1 - mine])
        out[...] = encoded(peak_of(total, plan.half_used), total, plan.half_used)
    else:
        out[...] = keep[mine] + decoded(message[mine])


def halve_kernel(plan, mask, used, sends, keep, message, out):
    side = (lax.axis_index("band") // mask) % 2
    total = keep[...] + decoded(message[...])
    rows = total.shape[0] // 2
    lower, upper = total[:rows], total[rows:]
    if sends:
        given = jnp.where(side == 0, upper, lower)
        out[...] = encoded(peak_of(given, used), given, used)
    else:
        out[...] = jnp.where(side == 0, lower, upper)


def last_kernel(plan, scale, keep, message, out):
    total = (keep[...] + decoded(message[...])) * scale
    depth, cols = plan.depth, plan.cols
    for r in range(len(TAP_STEPS)):
        for c in range(len(TAP_STEPS)):
            out[r * len(TAP_STEPS) + c] = total[c * depth : (c + 1) * depth, r * cols : (r + 1) * cols]


def pack_kernel(plan, kernel, out):
    rows = []
    for c in range(len(TAP_STEPS)):
        pieces = [kernel[r * len(TAP_STEPS) + c].astype(jnp.float32) for r in range(len(TAP_STEPS))]
        pieces.append(jnp.zeros((plan.depth, plan.lanes - plan.used), jnp.float32))
        rows.append(jnp.concatenate(pieces, axis=1))
    out[...] = jnp.concatenate(rows, axis=0).astype(jnp.bfloat16)


def cells_kernel(plan, own, other, grad0, grad1, top0, top1, bottom0, bottom1, out0, out1, left, right):
    band, strip, core, low, high = place(plan)
    depth, width, half, lanes = plan.depth, plan.width, plan.half, plan.half_lanes
    steps = len(TAP_STEPS)
    for x in range(2):
        rows = [[] for _ in TAP_STEPS]
        for m in range(plan.blocks):
            difference = m ^ (band // 2)
            by_row, by_col = difference % 2, x ^ high
            one = jnp.where(core == 0, by_row, by_col)
            two = jnp.where(core == 0, by_col, by_row)
            slot = one * plan.inner + plan.slot_of(difference)
            block = jnp.where(two == 0, own[slot], other[slot]).astype(jnp.float32)
            for c in range(steps):
                rows[c].append(block[c * depth : (c + 1) * depth])
        for c in range(steps):
            left[c * half : (c + 1) * half, x * lanes : (x + 1) * lanes] = jnp.concatenate(
                rows[c], axis=0
            ).astype(jnp.bfloat16)
    sources = ((grad0, top0, bottom0), (grad1, top1, bottom1))
    chunks = [(d, n, h) for d in range(2) for n in range(plan.images) for h in range(plan.rows)]
    for at, (d, n, h) in enumerate(chunks):
        grad, top, bottom = sources[d]
        for x in range(2):
            for r, row_step in enumerate(TAP_STEPS):
                begin = x * lanes + r * half
                right[begin : begin + half, at * width : (at + 1) * width] = grad_row(
                    plan, grad, top, bottom, n, h - row_step, x * half, strip
                )
            begin = x * lanes + steps * half
            right[begin : (x + 1) * lanes, at * width : (at + 1) * width] = jnp.zeros(
                (lanes - steps * half, width), jnp.bfloat16
            )
    group = 2
    for begin in range(0, len(chunks), group):
        part = chunks[begin : begin + group]
        product = jnp.dot(
            left[...],
            right[:, begin * width : (begin + len(part)) * width],
            preferred_element_type=jnp.float32,
        )
        for k, (d, n, h) in enumerate(part):
            total = None
            for c, col_step in enumerate(TAP_STEPS):
                term = moved(product[c * half : (c + 1) * half, k * width : (k + 1) * width], -col_step)
                total = term if total is None else total + term
            (out0, out1)[d][n, h] = total.astype(jnp.bfloat16)


def weave_kernel(plan, mine, theirs, out):
    core = lax.axis_index("band") % 2
    depth = plan.depth
    for n in range(plan.images):
        for h in range(plan.rows):
            a, b = mine[n, h].astype(jnp.float32), theirs[n, h].astype(jnp.float32)
            even, odd = jnp.where(core == 0, a, b), jnp.where(core == 0, b, a)
            pieces = []
            for m in range(plan.blocks):
                pieces += [even[m * depth : (m + 1) * depth], odd[m * depth : (m + 1) * depth]]
            out[n, h] = jnp.concatenate(pieces, axis=0).astype(jnp.bfloat16)


def after(value, *others):
    return lax.optimization_barrier((value, *others))[0]


def joined(packed, come, start):
    return after(jnp.concatenate([packed, after(come, start)], axis=0), start)


def first_kernel(plan, kernel):
    shape = jax.ShapeDtypeStruct((plan.block_rows, plan.lanes), jnp.bfloat16)
    packed = call(functools.partial(pack_kernel, plan), shape, [kernel])[None]
    return [packed] + [swap(packed, plan.sizes, mask, 0) for mask in plan.rest_band[:1]]


def whole_kernel(plan, packed, starts):
    sizes = plan.sizes
    starts = list(starts)
    packed = joined(*packed, starts.pop(0)) if len(packed) > 1 else packed[0]
    for mask in plan.rest_band[1:]:
        packed = joined(packed, swap(packed, sizes, mask, 0), starts.pop(0))
    if plan.rest_strip:
        packed = packed[None]
        for mask in reversed(plan.rest_strip):
            packed = jnp.concatenate([packed, swap(packed, sizes, 0, mask)], axis=0)
        count = packed.shape[0]
        order = jnp.arange(count) ^ (lax.axis_index("strip") % count)
        packed = jnp.take(packed, order, axis=0)[..., : plan.used]
        packed = packed.reshape(count, plan.inner, plan.block_rows, len(TAP_STEPS), plan.cols)
        packed = packed.transpose(1, 2, 3, 0, 4).reshape(plan.inner, plan.block_rows, plan.half_used)
        packed = jnp.pad(packed, ((0, 0), (0, 0), (0, plan.half_lanes - plan.half_used)))
    by_row, by_col = (2, 0), (0, plan.top_strip)
    packed = joined(packed, swap(packed, sizes, *by_row, other_masks=by_col), starts.pop(0))
    return packed, swap(packed, sizes, *by_col, other_masks=by_row)


def narrowed(plan, total):
    rows = total.shape[0]
    total = total[:, : plan.half_used].reshape(rows, len(TAP_STEPS), plan.half)
    for mask in plan.rest_strip:
        side = (lax.axis_index("strip") // mask) % 2
        parts = total.reshape(rows, len(TAP_STEPS), 2, total.shape[2] // 2)
        kept = jnp.where(side == 0, parts[:, :, 0], parts[:, :, 1])
        given = jnp.where(side == 0, parts[:, :, 1], parts[:, :, 0])
        total = kept + swap(given, plan.sizes, 0, mask)
    total = total.reshape(rows, plan.used)
    return jnp.pad(total, ((0, 0), (0, plan.lanes - plan.used)))


def kernel_terms(plan, cells, scale):
    sizes, f32 = plan.sizes, jnp.float32
    rows, lanes = plan.inner * plan.block_rows, plan.half_lanes
    depth = 2 * plan.images * plan.rows * plan.width
    scratch = [
        pltpu.VMEM((2, rows, depth), jnp.bfloat16),
        pltpu.VMEM((plan.half_used, depth), jnp.bfloat16),
    ]
    flops = 4 * rows * plan.half_used * depth
    steps = []

    def done(value):
        steps.append(value)
        return value

    shape = (2, rows, lanes)
    send = call(
        functools.partial(terms_kernel, plan, True),
        jax.ShapeDtypeStruct(shape, jnp.bfloat16), cells, scratch, flops,
    )
    keep = done(call(
        functools.partial(terms_kernel, plan, False),
        jax.ShapeDtypeStruct(shape, f32), [*cells[:4], after(cells[4], send), *cells[5:]], scratch, flops,
    ))
    by_row, by_col = (2, 0), (0, plan.top_strip)
    come = swap(send, sizes, *by_col, other_masks=by_row)
    shape = (rows, lanes)
    turn = functools.partial(turn_kernel, plan)
    send = call(functools.partial(turn, True), jax.ShapeDtypeStruct(shape, jnp.bfloat16), [keep, come])
    keep = done(call(functools.partial(turn, False), jax.ShapeDtypeStruct(shape, f32), [after(keep, send), come]))
    come = swap(send, sizes, *by_row, other_masks=by_col)
    if plan.rest_strip:
        keep = narrowed(plan, keep + decoded(come))
        come = jnp.zeros(keep.shape, jnp.bfloat16)
    for mask in plan.rest_band:
        rows //= 2
        shape = (rows, plan.lanes)
        halve = functools.partial(halve_kernel, plan, mask, plan.used)
        send = call(functools.partial(halve, True), jax.ShapeDtypeStruct(shape, jnp.bfloat16), [keep, come])
        keep = done(call(functools.partial(halve, False), jax.ShapeDtypeStruct(shape, f32), [after(keep, send), come]))
        come = swap(send, sizes, mask, 0)
    total = call(
        functools.partial(last_kernel, plan, scale),
        jax.ShapeDtypeStruct((len(TAP_STEPS) ** 2, plan.depth, plan.cols), f32),
        [keep, come],
        flops=LAST_FLOPS,
    )
    return total, steps


def borders(plan, grad):
    strip = lax.axis_index("strip")
    first, last = grad[:, 0], grad[:, plan.rows - 1]
    if plan.strips == 2:
        come = swap(jnp.where(strip == 0, last, first), plan.sizes, 0, 1)
        return [come]
    ends = plan.strips - 1
    return [
        lax.ppermute(last, "strip", [(i, i + 1) for i in range(ends)]),
        lax.ppermute(first, "strip", [(i + 1, i) for i in range(ends)]),
    ]


def body(activations, out_grad, kernel):
    images, channels, rows, width = activations.shape
    bands, strips = lax.axis_size("band"), lax.axis_size("strip")
    plan = Plan(images, channels, rows, width, bands, strips)
    scale = 1.0 / math.sqrt(images * bands * rows * strips * width)
    act = activations.transpose(0, 2, 1, 3)
    grad = out_grad.transpose(0, 2, 1, 3)
    edges = borders(plan, grad)
    act1 = swap(act, plan.sizes, 1, 0)
    grad1 = swap(grad, plan.sizes, 1, 0)
    shape = jax.ShapeDtypeStruct(act.shape, act.dtype)
    act0, grad0 = call(near_kernel, (shape, shape), [act, grad], [pltpu.SemaphoreType.DMA((2,))], far=2)
    edges = [after(edge, act0, grad0) for edge in edges]
    edges1 = [swap(edge, plan.sizes, 1, 0) for edge in edges]
    near = [grad1, edges[0], edges1[0], edges[-1], edges1[-1]]
    packed = first_kernel(plan, kernel.transpose(1, 0, 2))
    near[2] = after(near[2], packed[-1])
    kernel_grad, steps = kernel_terms(plan, [act0, grad0, act1, *near], scale)
    packed = whole_kernel(plan, packed, steps + [steps[-1]] * plan.band_bits)
    packed = (after(packed[0], steps[-1]), packed[1])
    depth = 2 * images * rows * width
    shape = jax.ShapeDtypeStruct((images, rows, plan.half, width), jnp.bfloat16)
    mine, given = call(
        functools.partial(cells_kernel, plan),
        (shape, shape),
        [*packed, grad0, *near],
        [
            pltpu.VMEM((len(TAP_STEPS) * plan.half, 2 * plan.half_lanes), jnp.bfloat16),
            pltpu.VMEM((2 * plan.half_lanes, depth), jnp.bfloat16),
        ],
    )
    theirs = swap(given, plan.sizes, 1, 0)
    input_grad = call(
        functools.partial(weave_kernel, plan),
        jax.ShapeDtypeStruct((images, rows, channels, width), jnp.bfloat16),
        [mine, theirs],
    )
    return input_grad.transpose(0, 2, 1, 3), kernel_grad.transpose(1, 0, 2)


def solution(mesh):
    in_specs = (
        P("band", None, "strip", None),
        P("band", None, "strip", None),
        P("band", None, "strip"),
    )
    out_specs = (P("band", None, "strip", None), P("band", None, "strip"))
    return jax.shard_map(body, mesh=mesh, in_specs=in_specs, out_specs=out_specs, check_vma=False)
```

```python
import functools
import math

import jax
import jax.numpy as jnp
from jax import lax
from jax.experimental import pallas as pl
from jax.experimental.pallas import tpu as pltpu
from jax.sharding import PartitionSpec as P

AXES = ("band", "strip")
TAP_STEPS = (-1, 0, 1)
LANES = 128
TOP_POWER = 2.0**15.5
LEAST_PEAK = 1e-30
VMEM_BYTES = 40 * 2**20
PACK_FLOPS = 10**10
LAST_FLOPS = 10**10


def padded_lanes(count):
    return (count // LANES + 1) * LANES


def swap(value, sizes, *masks):
    bands, strips = sizes
    pairs = []
    for b in range(bands):
        for s in range(strips):
            masks_here = masks[b % len(masks)]
            pairs.append((b * strips + s, (b ^ masks_here[0]) * strips + (s ^ masks_here[1])))
    return lax.ppermute(value, AXES, pairs)


def call(kernel, out_shape, operands, scratch=(), flops=0):
    return pl.pallas_call(
        kernel,
        out_shape=out_shape,
        in_specs=[pl.BlockSpec(memory_space=pltpu.VMEM)] * len(operands),
        out_specs=jax.tree.map(lambda _: pl.BlockSpec(memory_space=pltpu.VMEM), out_shape),
        scratch_shapes=list(scratch),
        compiler_params=pltpu.CompilerParams(vmem_limit_bytes=VMEM_BYTES),
        cost_estimate=pl.CostEstimate(flops=flops, bytes_accessed=0, transcendentals=0),
    )(*operands)


def encoded(peak, value, used):
    lane = lax.broadcasted_iota(jnp.int32, value.shape, value.ndim - 1)
    ratio = value * (TOP_POWER / peak)
    square = ratio * ratio
    power = ratio * jnp.abs(ratio) * square * (square * square)
    return jnp.where(lane < used, power, peak).astype(jnp.bfloat16)


def decoded(message):
    power = message.astype(jnp.float32)
    peak = power[0:1, message.shape[1] - 1 : message.shape[1]]
    root = jnp.sqrt(jnp.sqrt(jnp.sqrt(jnp.abs(power))))
    return jnp.where(power < 0, -root, root) * (peak * (1.0 / TOP_POWER))


def peak_of(value, used):
    lane = lax.broadcasted_iota(jnp.int32, value.shape, value.ndim - 1)
    largest = jnp.max(jnp.where(lane < used, jnp.abs(value), 0.0))
    largest = jnp.maximum(largest * (1.0 + 2.0**-6), LEAST_PEAK)
    return jnp.full((1, 1), largest, jnp.float32).astype(jnp.bfloat16).astype(jnp.float32)


class Plan:
    def __init__(self, images, channels, rows, width, bands, strips):
        self.images, self.channels, self.rows, self.width = images, channels, rows, width
        self.bands, self.strips = bands, strips
        self.sizes = (bands, strips)
        self.depth = channels // bands
        self.cols = channels // strips
        self.blocks = bands // 2
        self.half = channels // 2
        self.strip_bits = strips.bit_length() - 1
        self.band_bits = bands.bit_length() - 1
        assert bands == 1 << self.band_bits and strips == 1 << self.strip_bits
        assert self.band_bits >= 3 and self.strip_bits >= 1
        self.top_strip = 1 << (self.strip_bits - 1)
        self.rest_strip = [1 << k for k in reversed(range(self.strip_bits - 1))]
        self.rest_band = [1 << k for k in range(3, self.band_bits)]
        self.inner = self.blocks // 4
        self.half_used = len(TAP_STEPS) * self.half
        self.half_lanes = padded_lanes(self.half_used)
        self.used = len(TAP_STEPS) * self.cols
        self.lanes = padded_lanes(self.used)
        self.block_rows = len(TAP_STEPS) * self.depth
        self.part_rows = self.inner * self.block_rows
        self.cells = 2 * images * rows * width
        by_row, by_next, by_col = (2, 0), (4, 0), (0, self.top_strip)
        self.term_masks = ((by_col, by_row), (by_row, by_next), (by_next, by_col))
        self.gather_masks = ((by_next, by_col), (by_row, by_next), (by_col, by_row))

    def block_of(self, slot, by_next, by_row):
        bits = self.band_bits - 3
        turned = sum(((slot >> k) & 1) << (bits - 1 - k) for k in range(bits))
        return turned * 4 + by_next * 2 + by_row

    def chunks(self):
        return [(d, n, h) for d in range(2) for n in range(self.images) for h in range(self.rows)]


def place(plan):
    band, strip = lax.axis_index("band"), lax.axis_index("strip")
    return band % 2, (band // 2) % 2, (band // 4) % 2, strip // plan.top_strip


def mine(plan):
    core, by_row, by_next, by_col = place(plan)
    order = ((by_col, by_row, by_next), (by_row, by_next, by_col))
    return [jnp.where(core == 0, a, b) for a, b in zip(*order)]


def part_at(plan, bits):
    core = lax.axis_index("band") % 2
    first, second, third = bits
    order = ((second, third, first), (first, second, third))
    return [jnp.where(core == 0, a, b) for a, b in zip(*order)]


def grad_row(plan, grad_ref, top_ref, bottom_ref, image, row, start, strip):
    if row < 0:
        piece = top_ref[image, pl.ds(start, plan.half), :]
        return jnp.where(strip > 0, piece, jnp.zeros_like(piece))
    if row >= plan.rows:
        piece = bottom_ref[image, pl.ds(start, plan.half), :]
        return jnp.where(strip < plan.strips - 1, piece, jnp.zeros_like(piece))
    return grad_ref[image, row, pl.ds(start, plan.half), :]


def moved(value, step):
    width = value.shape[-1]
    if step == 0:
        return value
    lane = lax.broadcasted_iota(jnp.int32, value.shape, value.ndim - 1)
    turned = pltpu.roll(value, (-step) % width, value.ndim - 1)
    inside = lane < width - step if step > 0 else lane >= -step
    return jnp.where(inside, turned, 0.0)


def acts_kernel(plan, act0, act1, out):
    core = lax.axis_index("band") % 2
    depth, width = plan.depth, plan.width
    for at, (d, n, h) in enumerate(plan.chunks()):
        cells = (act0, act1)[d][n, h].astype(jnp.float32)
        shifted = []
        for m in range(plan.blocks):
            begin = 2 * m * depth
            even, odd = cells[begin : begin + depth], cells[begin + depth : begin + 2 * depth]
            block = jnp.where(core == 0, even, odd)
            shifted.append([moved(block, step) for step in TAP_STEPS])
        for y in range(2):
            for z in range(2):
                pieces = []
                for slot in range(plan.inner):
                    pieces += shifted[plan.block_of(slot, z, y)]
                out[y, z, :, at * width : (at + 1) * width] = jnp.concatenate(pieces, axis=0).astype(jnp.bfloat16)


def grads_kernel(plan, grad0, grad1, top0, top1, bottom0, bottom1, out):
    strip = lax.axis_index("strip")
    half, width = plan.half, plan.width
    sources = ((grad0, top0, bottom0), (grad1, top1, bottom1))
    for at, (d, n, h) in enumerate(plan.chunks()):
        cells = slice(at * width, (at + 1) * width)
        for x in range(2):
            for r, row_step in enumerate(TAP_STEPS):
                out[x, r * half : (r + 1) * half, cells] = grad_row(
                    plan, *sources[d], n, h - row_step, x * half, strip
                )
            out[x, plan.half_used :, cells] = jnp.zeros((plan.half_lanes - plan.half_used, width), jnp.bfloat16)


def part_terms(plan, acts, grads, bits):
    y, z, x = part_at(plan, bits)
    return lax.dot_general(acts[y, z], grads[x], (((1,), (1,)), ((), ())), preferred_element_type=jnp.float32)


def send_kernel(plan, same, acts, grads, out):
    first, second, third = mine(plan)
    for k in range(2):
        total = part_terms(plan, acts, grads, (1 - first, second if same else 1 - second, third if k else 1 - third))
        out[k] = encoded(peak_of(total, plan.half_used), total, plan.half_used)


def keep_kernel(plan, acts, grads, out):
    first, second, third = mine(plan)
    for j in range(2):
        for k in range(2):
            out[j, k] = part_terms(plan, acts, grads, (first, second if j else 1 - second, third if k else 1 - third))


def turn_kernel(plan, same, keep, message, out):
    for k in range(2):
        total = keep[1 if same else 0, k] + decoded(message[k])
        out[k] = total if same else encoded(peak_of(total, plan.half_used), total, plan.half_used)


def part_kernel(plan, same, keep, message, out):
    k = 1 if same else 0
    total = keep[k] + decoded(message[k])
    out[...] = total if same else encoded(peak_of(total, plan.half_used), total, plan.half_used)


def halve_kernel(plan, mask, used, same, keep, message, out):
    side = (lax.axis_index("band") // mask) % 2
    total = keep[...] + decoded(message[...])
    rows = total.shape[0] // 2
    lower, upper = total[:rows], total[rows:]
    if same:
        out[...] = jnp.where(side == 0, lower, upper)
    else:
        given = jnp.where(side == 0, upper, lower)
        out[...] = encoded(peak_of(given, used), given, used)


def last_kernel(plan, scale, keep, message, out):
    total = (keep[...] + decoded(message[...])) * scale
    depth, cols = plan.depth, plan.cols
    for r in range(len(TAP_STEPS)):
        for c in range(len(TAP_STEPS)):
            out[r * len(TAP_STEPS) + c] = total[c * depth : (c + 1) * depth, r * cols : (r + 1) * cols]


def pack_kernel(plan, kernel, out):
    rows = []
    for c in range(len(TAP_STEPS)):
        pieces = [kernel[r * len(TAP_STEPS) + c].astype(jnp.float32) for r in range(len(TAP_STEPS))]
        pieces.append(jnp.zeros((plan.depth, plan.lanes - plan.used), jnp.float32))
        rows.append(jnp.concatenate(pieces, axis=1))
    out[...] = jnp.concatenate(rows, axis=0).astype(jnp.bfloat16)


def cells_kernel(plan, own, other, grads, out0, out1, left):
    core, row_bit, next_bit, col_bit = place(plan)
    rest = lax.axis_index("band") // 8
    depth, width, half, lanes = plan.depth, plan.width, plan.half, plan.half_lanes
    steps = len(TAP_STEPS)
    for x in range(2):
        rows = [[] for _ in TAP_STEPS]
        for m in range(plan.blocks):
            row, behind, col = (m % 2) ^ row_bit, (m // 2 % 2) ^ next_bit, x ^ col_bit
            one = jnp.where(core == 0, behind, col)
            two = jnp.where(core == 0, row, behind)
            three = jnp.where(core == 0, col, row)
            slot = (two * 2 + one) * plan.inner + ((m // 4) ^ rest)
            block = jnp.where(three == 0, own[slot], other[slot]).astype(jnp.float32)
            for c in range(steps):
                rows[c].append(block[c * depth : (c + 1) * depth])
        for c in range(steps):
            left[c * half : (c + 1) * half, x * lanes : (x + 1) * lanes] = jnp.concatenate(
                rows[c], axis=0
            ).astype(jnp.bfloat16)
    group = 2
    chunks = plan.chunks()
    for begin in range(0, len(chunks), group):
        part = chunks[begin : begin + group]
        product = jnp.dot(
            left[...],
            grads[:, begin * width : (begin + len(part)) * width],
            preferred_element_type=jnp.float32,
        )
        for k, (d, n, h) in enumerate(part):
            total = None
            for c, col_step in enumerate(TAP_STEPS):
                term = moved(product[c * half : (c + 1) * half, k * width : (k + 1) * width], -col_step)
                total = term if total is None else total + term
            (out0, out1)[d][n, h] = total.astype(jnp.bfloat16)


def weave_kernel(plan, own, theirs, out):
    core = lax.axis_index("band") % 2
    depth = plan.depth
    for n in range(plan.images):
        for h in range(plan.rows):
            a, b = own[n, h].astype(jnp.float32), theirs[n, h].astype(jnp.float32)
            even, odd = jnp.where(core == 0, a, b), jnp.where(core == 0, b, a)
            pieces = []
            for m in range(plan.blocks):
                pieces += [even[m * depth : (m + 1) * depth], odd[m * depth : (m + 1) * depth]]
            out[n, h] = jnp.concatenate(pieces, axis=0).astype(jnp.bfloat16)


def after(value, *others):
    return lax.optimization_barrier((value, *others))[0]


def joined(packed, come, start):
    return after(jnp.concatenate([packed, after(come, start)], axis=0), start)


def first_kernel(plan, kernel):
    shape = jax.ShapeDtypeStruct((plan.block_rows, plan.lanes), jnp.bfloat16)
    packed = call(functools.partial(pack_kernel, plan), shape, [kernel], flops=PACK_FLOPS)[None]
    return [packed] + [swap(packed, plan.sizes, (mask, 0)) for mask in plan.rest_band[:1]]


def whole_kernel(plan, packed, starts):
    sizes = plan.sizes
    starts = list(starts)
    packed = joined(*packed, starts.pop(0)) if len(packed) > 1 else packed[0]
    for mask in plan.rest_band[1:]:
        packed = jnp.concatenate([packed, swap(packed, sizes, (mask, 0))], axis=0)
    if plan.rest_strip:
        packed = packed[None]
        for mask in reversed(plan.rest_strip):
            packed = jnp.concatenate([packed, swap(packed, sizes, (0, mask))], axis=0)
        count = packed.shape[0]
        order = jnp.arange(count) ^ (lax.axis_index("strip") % count)
        packed = jnp.take(packed, order, axis=0)[..., : plan.used]
        packed = packed.reshape(count, plan.inner, plan.block_rows, len(TAP_STEPS), plan.cols)
        packed = packed.transpose(1, 2, 3, 0, 4).reshape(plan.inner, plan.block_rows, plan.half_used)
        packed = jnp.pad(packed, ((0, 0), (0, 0), (0, plan.half_lanes - plan.half_used)))
    for masks in plan.gather_masks[:-1]:
        packed = joined(packed, swap(packed, sizes, *masks), starts.pop(0))
    return packed, swap(packed, sizes, *plan.gather_masks[-1])


def narrowed(plan, total):
    rows = total.shape[0]
    total = total[:, : plan.half_used].reshape(rows, len(TAP_STEPS), plan.half)
    for mask in plan.rest_strip:
        side = (lax.axis_index("strip") // mask) % 2
        parts = total.reshape(rows, len(TAP_STEPS), 2, total.shape[2] // 2)
        kept = jnp.where(side == 0, parts[:, :, 0], parts[:, :, 1])
        given = jnp.where(side == 0, parts[:, :, 1], parts[:, :, 0])
        total = kept + swap(given, plan.sizes, (0, mask))
    total = total.reshape(rows, plan.used)
    return jnp.pad(total, ((0, 0), (0, plan.lanes - plan.used)))


def kernel_terms(plan, acts, grads, gathered, scale):
    sizes, f32 = plan.sizes, jnp.float32
    rows, lanes = plan.part_rows, plan.half_lanes
    flops = 0

    def run(kernel, shape, kind, operands, flops=0):
        return call(kernel, jax.ShapeDtypeStruct(shape, kind), operands, flops=flops)

    part = functools.partial
    b16 = jnp.bfloat16
    shape = (2, rows, lanes)
    send0 = run(part(send_kernel, plan, False), shape, b16, [acts, grads], flops)
    send1 = run(part(send_kernel, plan, True), shape, b16, [after(acts, send0, gathered), grads], flops)
    keep = run(part(keep_kernel, plan), (2, *shape), f32, [after(acts, send1), grads], 2 * flops)
    steps = [send1, keep]
    come0 = swap(send0, sizes, *plan.term_masks[0])
    come1 = swap(send1, sizes, *plan.term_masks[0])
    send = run(part(turn_kernel, plan, False), shape, b16, [keep, come0])
    come = swap(send, sizes, *plan.term_masks[1])
    keep = run(part(turn_kernel, plan, True), shape, f32, [after(keep, send), come1])
    steps.append(keep)
    shape = shape[1:]
    send = run(part(part_kernel, plan, False), shape, b16, [keep, come])
    keep = run(part(part_kernel, plan, True), shape, f32, [after(keep, send), come])
    steps.append(keep)
    come = swap(send, sizes, *plan.term_masks[2])
    if plan.rest_strip:
        keep = narrowed(plan, keep + decoded(come))
        come = jnp.zeros(keep.shape, b16)
    for mask in plan.rest_band:
        rows //= 2
        shape = (rows, plan.lanes)
        halve = part(halve_kernel, plan, mask, plan.used)
        send = run(part(halve, False), shape, b16, [keep, come])
        keep = run(part(halve, True), shape, f32, [after(keep, send), come])
        steps.append(keep)
        come = swap(send, sizes, (mask, 0))
    total = call(
        part(last_kernel, plan, scale),
        jax.ShapeDtypeStruct((len(TAP_STEPS) ** 2, plan.depth, plan.cols), f32),
        [keep, come],
        flops=LAST_FLOPS,
    )
    return total, steps


def borders(plan, grad):
    strip = lax.axis_index("strip")
    first, last = grad[:, 0], grad[:, plan.rows - 1]
    if plan.strips == 2:
        come = swap(jnp.where(strip == 0, last, first), plan.sizes, (0, 1))
        return [come]
    ends = plan.strips - 1
    return [
        lax.ppermute(last, "strip", [(i, i + 1) for i in range(ends)]),
        lax.ppermute(first, "strip", [(i + 1, i) for i in range(ends)]),
    ]


def body(activations, out_grad, kernel):
    images, channels, rows, width = activations.shape
    bands, strips = lax.axis_size("band"), lax.axis_size("strip")
    plan = Plan(images, channels, rows, width, bands, strips)
    scale = 1.0 / math.sqrt(images * bands * rows * strips * width)
    act = activations.transpose(0, 2, 1, 3)
    grad = out_grad.transpose(0, 2, 1, 3)
    edges = borders(plan, grad)
    act1 = swap(act, plan.sizes, (1, 0))
    grad1 = swap(grad, plan.sizes, (1, 0))
    packed = first_kernel(plan, kernel.transpose(1, 0, 2))
    shape = (2, 2, plan.part_rows, plan.cells)
    acts = call(functools.partial(acts_kernel, plan), jax.ShapeDtypeStruct(shape, act.dtype), [act, act1])
    edges = [after(edge, acts) for edge in edges]
    edges1 = [swap(edge, plan.sizes, (1, 0)) for edge in edges]
    shape = (2, plan.half_lanes, plan.cells)
    grads = call(
        functools.partial(grads_kernel, plan),
        jax.ShapeDtypeStruct(shape, grad.dtype),
        [grad, grad1, edges[0], edges1[0], edges[-1], edges1[-1]],
    )
    kernel_grad, steps = kernel_terms(plan, acts, grads, packed[-1], scale)
    packed = whole_kernel(plan, packed, steps + [steps[-1]] * plan.band_bits)
    shape = jax.ShapeDtypeStruct((images, rows, plan.half, width), jnp.bfloat16)
    own, given = call(
        functools.partial(cells_kernel, plan),
        (shape, shape),
        [after(packed[0], steps[-1]), packed[1], grads.reshape(2 * plan.half_lanes, plan.cells)],
        [pltpu.VMEM((len(TAP_STEPS) * plan.half, 2 * plan.half_lanes), jnp.bfloat16)],
    )
    theirs = swap(given, plan.sizes, (1, 0))
    input_grad = call(
        functools.partial(weave_kernel, plan),
        jax.ShapeDtypeStruct((images, rows, channels, width), jnp.bfloat16),
        [own, theirs],
    )
    return input_grad.transpose(0, 2, 1, 3), kernel_grad.transpose(1, 0, 2)


def solution(mesh):
    in_specs = (
        P("band", None, "strip", None),
        P("band", None, "strip", None),
        P("band", None, "strip"),
    )
    out_specs = (P("band", None, "strip", None), P("band", None, "strip"))
    return jax.shard_map(body, mesh=mesh, in_specs=in_specs, out_specs=out_specs, check_vma=False)
```

```python
import functools
import math

import jax
import jax.numpy as jnp
from jax import lax
from jax.experimental import pallas as pl
from jax.experimental.pallas import tpu as pltpu
from jax.sharding import PartitionSpec as P

AXES = ("band", "strip")
TAP_STEPS = (-1, 0, 1)
LANES = 128
TOP_POWER = 2.0**15.5
LEAST_POWER = 2.0**-126
LEAST_PEAK = 1e-30
VMEM_BYTES = 40 * 2**20
HINTS = {
    "edge": 8.0,
    "pack": 8.0,
    "acts": 0.6,
    "grads": 0.5,
    "send0": 1.4,
    "send1": 1.4,
    "keep0": 1.0,
    "keep1": 1.0,
    "turn0": 0.9,
    "turn1": 0.6,
    "part0": 0.5,
    "part1": 0.3,
    "halve0": 0.5,
    "halve1": 3.0,
    "last": 8.0,
    "cells": 1.8,
    "weave": 0.9,
}
GATHER_STEPS = ("send1", "turn1", "part1")
CELLS_STEP = "halve1"
FLOPS_PER_US = 1.15e9


def padded_lanes(count):
    return (count // LANES + 1) * LANES


def swap(value, sizes, *masks):
    bands, strips = sizes
    pairs = []
    for b in range(bands):
        for s in range(strips):
            masks_here = masks[b % len(masks)]
            pairs.append((b * strips + s, (b ^ masks_here[0]) * strips + (s ^ masks_here[1])))
    return lax.ppermute(value, AXES, pairs)


def call(name, kernel, out_shape, operands, scratch=()):
    return pl.pallas_call(
        kernel,
        out_shape=out_shape,
        in_specs=[pl.BlockSpec(memory_space=pltpu.VMEM)] * len(operands),
        out_specs=jax.tree.map(lambda _: pl.BlockSpec(memory_space=pltpu.VMEM), out_shape),
        scratch_shapes=list(scratch),
        compiler_params=pltpu.CompilerParams(vmem_limit_bytes=VMEM_BYTES),
        cost_estimate=pl.CostEstimate(
            flops=int(HINTS[name] * FLOPS_PER_US), bytes_accessed=0, transcendentals=0
        ),
        name=name,
    )(*operands)


def encoded(peak, value, used):
    lane = lax.broadcasted_iota(jnp.int32, value.shape, value.ndim - 1)
    ratio = value * (TOP_POWER / peak)
    square = ratio * ratio
    power = ratio * jnp.abs(ratio) * square * (square * square)
    return jnp.where(lane < used, power, peak).astype(jnp.bfloat16)


def decoded(message):
    power = message.astype(jnp.float32)
    peak = power[0:1, message.shape[1] - 1 : message.shape[1]]
    size = jnp.maximum(jnp.abs(power), LEAST_POWER)
    fourth = lax.rsqrt(lax.rsqrt(size))
    root = fourth * lax.rsqrt(fourth)
    return jnp.where(power < 0, -root, root) * (peak * (1.0 / TOP_POWER))


def peak_of(value):
    largest = jnp.max(jnp.abs(value))
    largest = jnp.maximum(largest * (1.0 + 2.0**-6), LEAST_PEAK)
    return jnp.full((1, 1), largest, jnp.float32).astype(jnp.bfloat16).astype(jnp.float32)


class Plan:
    def __init__(self, images, channels, rows, width, bands, strips):
        self.images, self.channels, self.rows, self.width = images, channels, rows, width
        self.bands, self.strips = bands, strips
        self.sizes = (bands, strips)
        self.depth = channels // bands
        self.cols = channels // strips
        self.blocks = bands // 2
        self.half = channels // 2
        self.strip_bits = strips.bit_length() - 1
        self.band_bits = bands.bit_length() - 1
        assert bands == 1 << self.band_bits and strips == 1 << self.strip_bits
        assert self.band_bits >= 3 and self.strip_bits >= 1
        self.top_strip = 1 << (self.strip_bits - 1)
        self.rest_strip = [1 << k for k in reversed(range(self.strip_bits - 1))]
        self.rest_band = [1 << k for k in range(3, self.band_bits)]
        self.inner = self.blocks // 4
        self.half_used = len(TAP_STEPS) * self.half
        self.half_lanes = padded_lanes(self.half_used)
        self.used = len(TAP_STEPS) * self.cols
        self.lanes = padded_lanes(self.used)
        self.block_rows = len(TAP_STEPS) * self.depth
        self.part_rows = self.inner * self.block_rows
        self.cells = 2 * images * rows * width
        by_row, by_next, by_col = (2, 0), (4, 0), (0, self.top_strip)
        self.term_masks = ((by_col, by_row), (by_row, by_next), (by_next, by_col))
        self.gather_masks = ((by_next, by_col), (by_row, by_next), (by_col, by_row))

    def block_of(self, slot, by_next, by_row):
        bits = self.band_bits - 3
        turned = sum(((slot >> k) & 1) << (bits - 1 - k) for k in range(bits))
        return turned * 4 + by_next * 2 + by_row

    def chunks(self):
        return [(d, n, h) for d in range(2) for n in range(self.images) for h in range(self.rows)]


def place(plan):
    band, strip = lax.axis_index("band"), lax.axis_index("strip")
    return band % 2, (band // 2) % 2, (band // 4) % 2, strip // plan.top_strip


def mine(plan):
    core, by_row, by_next, by_col = place(plan)
    order = ((by_col, by_row, by_next), (by_row, by_next, by_col))
    return [jnp.where(core == 0, a, b) for a, b in zip(*order)]


def part_at(plan, bits):
    core = lax.axis_index("band") % 2
    first, second, third = bits
    order = ((second, third, first), (first, second, third))
    return [jnp.where(core == 0, a, b) for a, b in zip(*order)]


def grad_row(plan, grad_ref, top_ref, bottom_ref, image, row, start, strip):
    if row < 0:
        piece = top_ref[image, pl.ds(start, plan.half), :]
        return jnp.where(strip > 0, piece, jnp.zeros_like(piece))
    if row >= plan.rows:
        piece = bottom_ref[image, pl.ds(start, plan.half), :]
        return jnp.where(strip < plan.strips - 1, piece, jnp.zeros_like(piece))
    return grad_ref[image, row, pl.ds(start, plan.half), :]


def moved(value, step):
    width = value.shape[-1]
    if step == 0:
        return value
    lane = lax.broadcasted_iota(jnp.int32, value.shape, value.ndim - 1)
    turned = pltpu.roll(value, (-step) % width, value.ndim - 1)
    inside = lane < width - step if step > 0 else lane >= -step
    return jnp.where(inside, turned, 0.0)


def acts_kernel(plan, act0, act1, out):
    core = lax.axis_index("band") % 2
    depth, width = plan.depth, plan.width
    for at, (d, n, h) in enumerate(plan.chunks()):
        cells = (act0, act1)[d][n, h].astype(jnp.float32)
        shifted = []
        for m in range(plan.blocks):
            begin = 2 * m * depth
            even, odd = cells[begin : begin + depth], cells[begin + depth : begin + 2 * depth]
            block = jnp.where(core == 0, even, odd)
            shifted.append([moved(block, step) for step in TAP_STEPS])
        for y in range(2):
            for z in range(2):
                pieces = []
                for slot in range(plan.inner):
                    pieces += shifted[plan.block_of(slot, z, y)]
                out[y, z, :, at * width : (at + 1) * width] = jnp.concatenate(pieces, axis=0).astype(jnp.bfloat16)


def grads_kernel(plan, grad0, grad1, top0, top1, bottom0, bottom1, out):
    strip = lax.axis_index("strip")
    half, width = plan.half, plan.width
    sources = ((grad0, top0, bottom0), (grad1, top1, bottom1))
    for at, (d, n, h) in enumerate(plan.chunks()):
        cells = slice(at * width, (at + 1) * width)
        for x in range(2):
            for r, row_step in enumerate(TAP_STEPS):
                out[x, r * half : (r + 1) * half, cells] = grad_row(
                    plan, *sources[d], n, h - row_step, x * half, strip
                )
            out[x, plan.half_used :, cells] = jnp.zeros((plan.half_lanes - plan.half_used, width), jnp.bfloat16)


def part_terms(plan, acts, grads, bits):
    y, z, x = part_at(plan, bits)
    return lax.dot_general(acts[y, z], grads[x], (((1,), (1,)), ((), ())), preferred_element_type=jnp.float32)


def send_kernel(plan, same, acts, grads, out):
    first, second, third = mine(plan)
    for k in range(2):
        total = part_terms(plan, acts, grads, (1 - first, second if same else 1 - second, third if k else 1 - third))
        out[k] = encoded(peak_of(total), total, plan.half_used)


def keep_kernel(plan, same, acts, grads, out):
    first, second, third = mine(plan)
    for k in range(2):
        out[k] = part_terms(plan, acts, grads, (first, second if same else 1 - second, third if k else 1 - third))


def turn_kernel(plan, same, keep, message, out):
    for k in range(2):
        total = keep[k] + decoded(message[k])
        out[k] = total if same else encoded(peak_of(total), total, plan.half_used)


def part_kernel(plan, same, keep, message, out):
    k = 1 if same else 0
    total = keep[k] + decoded(message[k])
    out[...] = total if same else encoded(peak_of(total), total, plan.half_used)


def halve_kernel(plan, mask, used, same, keep, message, out):
    side = (lax.axis_index("band") // mask) % 2
    total = keep[...] + decoded(message[...])
    rows = total.shape[0] // 2
    lower, upper = total[:rows], total[rows:]
    if same:
        out[...] = jnp.where(side == 0, lower, upper)
    else:
        given = jnp.where(side == 0, upper, lower)
        out[...] = encoded(peak_of(given), given, used)


def last_kernel(plan, scale, keep, message, out):
    total = (keep[...] + decoded(message[...])) * scale
    depth, cols = plan.depth, plan.cols
    for r in range(len(TAP_STEPS)):
        for c in range(len(TAP_STEPS)):
            out[r * len(TAP_STEPS) + c] = total[c * depth : (c + 1) * depth, r * cols : (r + 1) * cols]


def pack_kernel(plan, kernel, out):
    rows = []
    for c in range(len(TAP_STEPS)):
        pieces = [kernel[r * len(TAP_STEPS) + c].astype(jnp.float32) for r in range(len(TAP_STEPS))]
        pieces.append(jnp.zeros((plan.depth, plan.lanes - plan.used), jnp.float32))
        rows.append(jnp.concatenate(pieces, axis=1))
    out[...] = jnp.concatenate(rows, axis=0).astype(jnp.bfloat16)


def cells_kernel(plan, own, other, grads, out0, out1, left):
    core, row_bit, next_bit, col_bit = place(plan)
    rest = lax.axis_index("band") // 8
    depth, width, half, lanes = plan.depth, plan.width, plan.half, plan.half_lanes
    steps = len(TAP_STEPS)
    for x in range(2):
        rows = [[] for _ in TAP_STEPS]
        for m in range(plan.blocks):
            row, behind, col = (m % 2) ^ row_bit, (m // 2 % 2) ^ next_bit, x ^ col_bit
            one = jnp.where(core == 0, behind, col)
            two = jnp.where(core == 0, row, behind)
            three = jnp.where(core == 0, col, row)
            slot = (two * 2 + one) * plan.inner + ((m // 4) ^ rest)
            block = jnp.where(three == 0, own[slot], other[slot]).astype(jnp.float32)
            for c in range(steps):
                rows[c].append(block[c * depth : (c + 1) * depth])
        for c in range(steps):
            left[c * half : (c + 1) * half, x * lanes : (x + 1) * lanes] = jnp.concatenate(
                rows[c], axis=0
            ).astype(jnp.bfloat16)
    group = 2
    chunks = plan.chunks()
    for begin in range(0, len(chunks), group):
        part = chunks[begin : begin + group]
        product = jnp.dot(
            left[...],
            grads[:, begin * width : (begin + len(part)) * width],
            preferred_element_type=jnp.float32,
        )
        for k, (d, n, h) in enumerate(part):
            total = None
            for c, col_step in enumerate(TAP_STEPS):
                term = moved(product[c * half : (c + 1) * half, k * width : (k + 1) * width], -col_step)
                total = term if total is None else total + term
            (out0, out1)[d][n, h] = total.astype(jnp.bfloat16)


def weave_kernel(plan, own, theirs, out):
    core = lax.axis_index("band") % 2
    depth = plan.depth
    for n in range(plan.images):
        for h in range(plan.rows):
            a, b = own[n, h].astype(jnp.float32), theirs[n, h].astype(jnp.float32)
            even, odd = jnp.where(core == 0, a, b), jnp.where(core == 0, b, a)
            pieces = []
            for m in range(plan.blocks):
                pieces += [even[m * depth : (m + 1) * depth], odd[m * depth : (m + 1) * depth]]
            out[n, h] = jnp.concatenate(pieces, axis=0).astype(jnp.bfloat16)


def after(value, *others):
    return lax.optimization_barrier((value, *others))[0]


def joined(packed, come, start):
    return after(jnp.concatenate([packed, after(come, start)], axis=0), start)


def first_kernel(plan, kernel):
    shape = jax.ShapeDtypeStruct((plan.block_rows, plan.lanes), jnp.bfloat16)
    packed = call("pack", functools.partial(pack_kernel, plan), shape, [kernel])[None]
    return [packed] + [swap(packed, plan.sizes, (mask, 0)) for mask in plan.rest_band[:1]]


def whole_kernel(plan, packed, starts):
    sizes = plan.sizes
    starts = list(starts)
    packed = joined(*packed, starts.pop(0)) if len(packed) > 1 else packed[0]
    for mask in plan.rest_band[1:]:
        packed = jnp.concatenate([packed, swap(packed, sizes, (mask, 0))], axis=0)
    if plan.rest_strip:
        packed = packed[None]
        for mask in reversed(plan.rest_strip):
            packed = jnp.concatenate([packed, swap(packed, sizes, (0, mask))], axis=0)
        count = packed.shape[0]
        order = jnp.arange(count) ^ (lax.axis_index("strip") % count)
        packed = jnp.take(packed, order, axis=0)[..., : plan.used]
        packed = packed.reshape(count, plan.inner, plan.block_rows, len(TAP_STEPS), plan.cols)
        packed = packed.transpose(1, 2, 3, 0, 4).reshape(plan.inner, plan.block_rows, plan.half_used)
        packed = jnp.pad(packed, ((0, 0), (0, 0), (0, plan.half_lanes - plan.half_used)))
    for masks in plan.gather_masks[:-1]:
        packed = joined(packed, swap(packed, sizes, *masks), starts.pop(0))
    return packed, swap(packed, sizes, *plan.gather_masks[-1])


def narrowed(plan, total):
    rows = total.shape[0]
    total = total[:, : plan.half_used].reshape(rows, len(TAP_STEPS), plan.half)
    for mask in plan.rest_strip:
        side = (lax.axis_index("strip") // mask) % 2
        parts = total.reshape(rows, len(TAP_STEPS), 2, total.shape[2] // 2)
        kept = jnp.where(side == 0, parts[:, :, 0], parts[:, :, 1])
        given = jnp.where(side == 0, parts[:, :, 1], parts[:, :, 0])
        total = kept + swap(given, plan.sizes, (0, mask))
    total = total.reshape(rows, plan.used)
    return jnp.pad(total, ((0, 0), (0, plan.lanes - plan.used)))


def kernel_terms(plan, acts, grads, scale):
    sizes, f32 = plan.sizes, jnp.float32
    rows, lanes = plan.part_rows, plan.half_lanes

    def run(name, kernel, shape, kind, operands):
        return call(name, kernel, jax.ShapeDtypeStruct(shape, kind), operands)

    part = functools.partial
    b16 = jnp.bfloat16
    shape = (2, rows, lanes)
    send0 = run("send0", part(send_kernel, plan, False), shape, b16, [acts, grads])
    come0 = swap(send0, sizes, *plan.term_masks[0])
    send1 = run("send1", part(send_kernel, plan, True), shape, b16, [after(acts, send0), grads])
    come1 = swap(send1, sizes, *plan.term_masks[0])
    keep0 = run("keep0", part(keep_kernel, plan, False), shape, f32, [after(acts, send1), grads])
    send = run("turn0", part(turn_kernel, plan, False), shape, b16, [keep0, come0])
    come = swap(send, sizes, *plan.term_masks[1])
    keep1 = run("keep1", part(keep_kernel, plan, True), shape, f32, [after(acts, send), grads])
    keep = run("turn1", part(turn_kernel, plan, True), shape, f32, [keep1, come1])
    steps = {"send1": send1, "keep0": keep0, "turn0": send, "keep1": keep1, "turn1": keep}
    shape = shape[1:]
    send = run("part0", part(part_kernel, plan, False), shape, b16, [keep, come])
    keep = run("part1", part(part_kernel, plan, True), shape, f32, [after(keep, send), come])
    steps.update(part0=send, part1=keep)
    come = swap(send, sizes, *plan.term_masks[2])
    if plan.rest_strip:
        keep = narrowed(plan, keep + decoded(come))
        come = jnp.zeros(keep.shape, b16)
    for mask in plan.rest_band:
        rows //= 2
        shape = (rows, plan.lanes)
        halve = part(halve_kernel, plan, mask, plan.used)
        send = run("halve0", part(halve, False), shape, b16, [keep, come])
        keep = run("halve1", part(halve, True), shape, f32, [after(keep, send), come])
        steps.update(halve0=send, halve1=keep)
        come = swap(send, sizes, (mask, 0))
    total = call(
        "last",
        part(last_kernel, plan, scale),
        jax.ShapeDtypeStruct((len(TAP_STEPS) ** 2, plan.depth, plan.cols), f32),
        [keep, come],
    )
    return total, steps


def edge_kernel(plan, grad, out):
    strip = lax.axis_index("strip")
    for n in range(plan.images):
        out[n] = jnp.where(strip == 0, grad[n, plan.rows - 1], grad[n, 0])


def borders(plan, grad):
    if plan.strips == 2:
        shape = jax.ShapeDtypeStruct((plan.images, plan.channels, plan.width), grad.dtype)
        edge = call("edge", functools.partial(edge_kernel, plan), shape, [grad])
        return [swap(edge, plan.sizes, (0, 1))]
    first, last = grad[:, 0], grad[:, plan.rows - 1]
    ends = plan.strips - 1
    return [
        lax.ppermute(last, "strip", [(i, i + 1) for i in range(ends)]),
        lax.ppermute(first, "strip", [(i + 1, i) for i in range(ends)]),
    ]


def body(activations, out_grad, kernel):
    images, channels, rows, width = activations.shape
    bands, strips = lax.axis_size("band"), lax.axis_size("strip")
    plan = Plan(images, channels, rows, width, bands, strips)
    scale = 1.0 / math.sqrt(images * bands * rows * strips * width)
    act = activations.transpose(0, 2, 1, 3)
    grad = out_grad.transpose(0, 2, 1, 3)
    edges = borders(plan, grad)
    act1 = swap(act, plan.sizes, (1, 0))
    grad1 = swap(grad, plan.sizes, (1, 0))
    packed = first_kernel(plan, kernel.transpose(1, 0, 2))
    shape = (2, 2, plan.part_rows, plan.cells)
    acts = call("acts", functools.partial(acts_kernel, plan), jax.ShapeDtypeStruct(shape, act.dtype), [act, act1])
    edges = [after(edge, acts) for edge in edges]
    edges1 = [swap(edge, plan.sizes, (1, 0)) for edge in edges]
    shape = (2, plan.half_lanes, plan.cells)
    grads = call(
        "grads",
        functools.partial(grads_kernel, plan),
        jax.ShapeDtypeStruct(shape, grad.dtype),
        [grad, grad1, edges[0], edges1[0], edges[-1], edges1[-1]],
    )
    kernel_grad, steps = kernel_terms(plan, acts, grads, scale)
    packed = whole_kernel(plan, packed, [steps[name] for name in GATHER_STEPS])
    shape = jax.ShapeDtypeStruct((images, rows, plan.half, width), jnp.bfloat16)
    own, given = call(
        "cells",
        functools.partial(cells_kernel, plan),
        (shape, shape),
        [after(packed[0], steps[CELLS_STEP]), packed[1], grads.reshape(2 * plan.half_lanes, plan.cells)],
        [pltpu.VMEM((len(TAP_STEPS) * plan.half, 2 * plan.half_lanes), jnp.bfloat16)],
    )
    theirs = swap(given, plan.sizes, (1, 0))
    input_grad = call(
        "weave",
        functools.partial(weave_kernel, plan),
        jax.ShapeDtypeStruct((images, rows, channels, width), jnp.bfloat16),
        [own, theirs],
    )
    return input_grad.transpose(0, 2, 1, 3), kernel_grad.transpose(1, 0, 2)


def solution(mesh):
    in_specs = (
        P("band", None, "strip", None),
        P("band", None, "strip", None),
        P("band", None, "strip"),
    )
    out_specs = (P("band", None, "strip", None), P("band", None, "strip"))
    return jax.shard_map(body, mesh=mesh, in_specs=in_specs, out_specs=out_specs, check_vma=False)
```

```python
import functools
import math

import jax
import jax.numpy as jnp
from jax import lax
from jax.experimental import pallas as pl
from jax.experimental.pallas import tpu as pltpu
from jax.sharding import PartitionSpec as P

AXES = ("band", "strip")
TAP_STEPS = (-1, 0, 1)
LANES = 128
TOP_POWER = 2.0**15.5
LEAST_POWER = 2.0**-126
LEAST_PEAK = 1e-30
VMEM_BYTES = 40 * 2**20
HINTS = {
    "edge": 8.0,
    "pack": 8.0,
    "acts": 0.6,
    "grads": 0.5,
    "send0": 1.4,
    "send1": 1.4,
    "keep0": 1.0,
    "keep1": 1.0,
    "turn0": 0.9,
    "turn1": 0.6,
    "part0": 0.5,
    "part1": 0.3,
    "halve0": 0.5,
    "halve1": 3.0,
    "last": 8.0,
    "given": 1.2,
    "own": 0.7,
    "weave": 0.9,
}
GATHER_STEPS = ("send0", "turn0", "part0")
CELLS_STEP = "halve1"
FLOPS_PER_US = 1.15e9


def padded_lanes(count):
    return (count // LANES + 1) * LANES


def swap(value, sizes, *masks):
    bands, strips = sizes
    pairs = []
    for b in range(bands):
        for s in range(strips):
            masks_here = masks[b % len(masks)]
            pairs.append((b * strips + s, (b ^ masks_here[0]) * strips + (s ^ masks_here[1])))
    return lax.ppermute(value, AXES, pairs)


def call(name, kernel, out_shape, operands, scratch=()):
    return pl.pallas_call(
        kernel,
        out_shape=out_shape,
        in_specs=[pl.BlockSpec(memory_space=pltpu.VMEM)] * len(operands),
        out_specs=jax.tree.map(lambda _: pl.BlockSpec(memory_space=pltpu.VMEM), out_shape),
        scratch_shapes=list(scratch),
        compiler_params=pltpu.CompilerParams(vmem_limit_bytes=VMEM_BYTES),
        cost_estimate=pl.CostEstimate(
            flops=int(HINTS[name] * FLOPS_PER_US), bytes_accessed=0, transcendentals=0
        ),
        name=name,
    )(*operands)


def encoded(peak, value, used):
    lane = lax.broadcasted_iota(jnp.int32, value.shape, value.ndim - 1)
    ratio = value * (TOP_POWER / peak)
    square = ratio * ratio
    power = ratio * jnp.abs(ratio) * square * (square * square)
    return jnp.where(lane < used, power, peak).astype(jnp.bfloat16)


def decoded(message):
    power = message.astype(jnp.float32)
    peak = power[0:1, message.shape[1] - 1 : message.shape[1]]
    size = jnp.maximum(jnp.abs(power), LEAST_POWER)
    fourth = lax.rsqrt(lax.rsqrt(size))
    root = fourth * lax.rsqrt(fourth)
    return jnp.where(power < 0, -root, root) * (peak * (1.0 / TOP_POWER))


def peak_of(value):
    largest = jnp.max(jnp.abs(value))
    largest = jnp.maximum(largest * (1.0 + 2.0**-6), LEAST_PEAK)
    return jnp.full((1, 1), largest, jnp.float32).astype(jnp.bfloat16).astype(jnp.float32)


class Plan:
    def __init__(self, images, channels, rows, width, bands, strips):
        self.images, self.channels, self.rows, self.width = images, channels, rows, width
        self.bands, self.strips = bands, strips
        self.sizes = (bands, strips)
        self.depth = channels // bands
        self.cols = channels // strips
        self.blocks = bands // 2
        self.half = channels // 2
        self.strip_bits = strips.bit_length() - 1
        self.band_bits = bands.bit_length() - 1
        assert bands == 1 << self.band_bits and strips == 1 << self.strip_bits
        assert self.band_bits >= 3 and self.strip_bits >= 1
        self.top_strip = 1 << (self.strip_bits - 1)
        self.rest_strip = [1 << k for k in reversed(range(self.strip_bits - 1))]
        self.rest_band = [1 << k for k in range(3, self.band_bits)]
        self.inner = self.blocks // 4
        self.half_used = len(TAP_STEPS) * self.half
        self.half_lanes = padded_lanes(self.half_used)
        self.used = len(TAP_STEPS) * self.cols
        self.lanes = padded_lanes(self.used)
        self.block_rows = len(TAP_STEPS) * self.depth
        self.part_rows = self.inner * self.block_rows
        self.cells = 2 * images * rows * width
        by_row, by_next, by_col = (2, 0), (4, 0), (0, self.top_strip)
        self.term_masks = ((by_col, by_next), (by_row, by_col), (by_next, by_row))
        self.gather_masks = ((by_next, by_col), (by_row, by_next), (by_col, by_row))

    def block_of(self, slot, by_next, by_row):
        bits = self.band_bits - 3
        turned = sum(((slot >> k) & 1) << (bits - 1 - k) for k in range(bits))
        return turned * 4 + by_next * 2 + by_row

    def chunks(self):
        return [(d, n, h) for d in range(2) for n in range(self.images) for h in range(self.rows)]


def place(plan):
    band, strip = lax.axis_index("band"), lax.axis_index("strip")
    return band % 2, (band // 2) % 2, (band // 4) % 2, strip // plan.top_strip


def mine(plan):
    core, by_row, by_next, by_col = place(plan)
    order = ((by_col, by_row, by_next), (by_next, by_col, by_row))
    return [jnp.where(core == 0, a, b) for a, b in zip(*order)]


def grad_row(plan, grad_ref, top_ref, bottom_ref, image, row, start, strip):
    if row < 0:
        piece = top_ref[image, pl.ds(start, plan.half), :]
        return jnp.where(strip > 0, piece, jnp.zeros_like(piece))
    if row >= plan.rows:
        piece = bottom_ref[image, pl.ds(start, plan.half), :]
        return jnp.where(strip < plan.strips - 1, piece, jnp.zeros_like(piece))
    return grad_ref[image, row, pl.ds(start, plan.half), :]


def moved(value, step):
    width = value.shape[-1]
    if step == 0:
        return value
    lane = lax.broadcasted_iota(jnp.int32, value.shape, value.ndim - 1)
    turned = pltpu.roll(value, (-step) % width, value.ndim - 1)
    inside = lane < width - step if step > 0 else lane >= -step
    return jnp.where(inside, turned, 0.0)


def acts_kernel(plan, act0, act1, out):
    core = lax.axis_index("band") % 2
    depth, width = plan.depth, plan.width
    for at, (d, n, h) in enumerate(plan.chunks()):
        cells = (act0, act1)[d][n, h].astype(jnp.float32)
        shifted = []
        for m in range(plan.blocks):
            begin = 2 * m * depth
            even, odd = cells[begin : begin + depth], cells[begin + depth : begin + 2 * depth]
            block = jnp.where(core == 0, even, odd)
            shifted.append([moved(block, step) for step in TAP_STEPS])
        for i in range(2):
            pieces = []
            for j in range(2):
                for slot in range(plan.inner):
                    here, there = shifted[plan.block_of(slot, j, i)], shifted[plan.block_of(slot, i, j)]
                    pieces += here if i == j else [jnp.where(core == 0, a, b) for a, b in zip(here, there)]
            out[i, :, at * width : (at + 1) * width] = jnp.concatenate(pieces, axis=0).astype(jnp.bfloat16)


def grads_kernel(plan, grad0, grad1, top0, top1, bottom0, bottom1, out):
    strip = lax.axis_index("strip")
    half, width = plan.half, plan.width
    sources = ((grad0, top0, bottom0), (grad1, top1, bottom1))
    for at, (d, n, h) in enumerate(plan.chunks()):
        cells = slice(at * width, (at + 1) * width)
        for x in range(2):
            for r, row_step in enumerate(TAP_STEPS):
                out[x, r * half : (r + 1) * half, cells] = grad_row(
                    plan, *sources[d], n, h - row_step, x * half, strip
                )
            out[x, plan.half_used :, cells] = jnp.zeros((plan.half_lanes - plan.half_used, width), jnp.bfloat16)


def pair_terms(plan, acts, grads, first, second):
    core = lax.axis_index("band") % 2
    i, x = jnp.where(core == 0, second, first), jnp.where(core == 0, first, second)
    return lax.dot_general(acts[i], grads[x], (((1,), (1,)), ((), ())), preferred_element_type=jnp.float32)


def send_kernel(plan, same, acts, grads, out):
    first, second, _ = mine(plan)
    total = pair_terms(plan, acts, grads, 1 - first, second if same else 1 - second)
    for k in range(2):
        half = total[k * plan.part_rows : (k + 1) * plan.part_rows]
        out[k] = encoded(peak_of(half), half, plan.half_used)


def keep_kernel(plan, same, acts, grads, out):
    first, second, _ = mine(plan)
    total = pair_terms(plan, acts, grads, first, second if same else 1 - second)
    for k in range(2):
        out[k] = total[k * plan.part_rows : (k + 1) * plan.part_rows]


def turn_kernel(plan, same, keep, message, out):
    for k in range(2):
        total = keep[k] + decoded(message[k])
        out[k] = total if same else encoded(peak_of(total), total, plan.half_used)


def part_kernel(plan, same, keep, message, out):
    third = mine(plan)[2]
    k = third if same else 1 - third
    total = keep[k] + decoded(message[k])
    out[...] = total if same else encoded(peak_of(total), total, plan.half_used)


def halve_kernel(plan, mask, used, same, keep, message, out):
    side = (lax.axis_index("band") // mask) % 2
    total = keep[...] + decoded(message[...])
    rows = total.shape[0] // 2
    lower, upper = total[:rows], total[rows:]
    if same:
        out[...] = jnp.where(side == 0, lower, upper)
    else:
        given = jnp.where(side == 0, upper, lower)
        out[...] = encoded(peak_of(given), given, used)


def last_kernel(plan, scale, keep, message, out):
    total = (keep[...] + decoded(message[...])) * scale
    depth, cols = plan.depth, plan.cols
    for r in range(len(TAP_STEPS)):
        for c in range(len(TAP_STEPS)):
            out[r * len(TAP_STEPS) + c] = total[c * depth : (c + 1) * depth, r * cols : (r + 1) * cols]


def pack_kernel(plan, kernel, out):
    rows = []
    for c in range(len(TAP_STEPS)):
        pieces = [kernel[r * len(TAP_STEPS) + c].astype(jnp.float32) for r in range(len(TAP_STEPS))]
        pieces.append(jnp.zeros((plan.depth, plan.lanes - plan.used), jnp.float32))
        rows.append(jnp.concatenate(pieces, axis=1))
    out[...] = jnp.concatenate(rows, axis=0).astype(jnp.bfloat16)


def cells_of(plan, d, left, grads, out):
    width, half = plan.width, plan.half
    rows = [(n, h) for n in range(plan.images) for h in range(plan.rows)]
    for begin in range(0, len(rows), 2):
        part = rows[begin : begin + 2]
        at = (d * len(rows) + begin) * width
        product = jnp.dot(
            left[...], grads[:, at : at + len(part) * width], preferred_element_type=jnp.float32
        )
        for k, (n, h) in enumerate(part):
            total = None
            for c, col_step in enumerate(TAP_STEPS):
                term = moved(product[c * half : (c + 1) * half, k * width : (k + 1) * width], -col_step)
                total = term if total is None else total + term
            out[n, h] = total.astype(jnp.bfloat16)


def given_kernel(plan, own, other, grads, out, left):
    core, row_bit, next_bit, col_bit = place(plan)
    rest = lax.axis_index("band") // 8
    depth, half, lanes = plan.depth, plan.half, plan.half_lanes
    for x in range(2):
        rows = [[] for _ in TAP_STEPS]
        for m in range(plan.blocks):
            row, behind, col = (m % 2) ^ row_bit, (m // 2 % 2) ^ next_bit, x ^ col_bit
            one = jnp.where(core == 0, behind, col)
            two = jnp.where(core == 0, row, behind)
            three = jnp.where(core == 0, col, row)
            slot = (two * 2 + one) * plan.inner + ((m // 4) ^ rest)
            block = jnp.where(three == 0, own[slot], other[slot]).astype(jnp.float32)
            for c in range(len(TAP_STEPS)):
                rows[c].append(block[c * depth : (c + 1) * depth])
        for c in range(len(TAP_STEPS)):
            left[c * half : (c + 1) * half, x * lanes : (x + 1) * lanes] = jnp.concatenate(
                rows[c], axis=0
            ).astype(jnp.bfloat16)
    cells_of(plan, 1, left, grads, out)


def own_kernel(plan, left, grads, out):
    cells_of(plan, 0, left, grads, out)


def weave_kernel(plan, own, theirs, out):
    core = lax.axis_index("band") % 2
    depth = plan.depth
    for n in range(plan.images):
        for h in range(plan.rows):
            a, b = own[n, h].astype(jnp.float32), theirs[n, h].astype(jnp.float32)
            even, odd = jnp.where(core == 0, a, b), jnp.where(core == 0, b, a)
            pieces = []
            for m in range(plan.blocks):
                pieces += [even[m * depth : (m + 1) * depth], odd[m * depth : (m + 1) * depth]]
            out[n, h] = jnp.concatenate(pieces, axis=0).astype(jnp.bfloat16)


def after(value, *others):
    return lax.optimization_barrier((value, *others))[0]


def joined(packed, come, start):
    return after(jnp.concatenate([packed, after(come, start)], axis=0), start)


def first_kernel(plan, kernel):
    shape = jax.ShapeDtypeStruct((plan.block_rows, plan.lanes), jnp.bfloat16)
    packed = call("pack", functools.partial(pack_kernel, plan), shape, [kernel])[None]
    return [packed] + [swap(packed, plan.sizes, (mask, 0)) for mask in plan.rest_band[:1]]


def whole_kernel(plan, packed, starts):
    sizes = plan.sizes
    starts = list(starts)
    packed = joined(*packed, starts.pop(0)) if len(packed) > 1 else packed[0]
    for mask in plan.rest_band[1:]:
        packed = jnp.concatenate([packed, swap(packed, sizes, (mask, 0))], axis=0)
    if plan.rest_strip:
        packed = packed[None]
        for mask in reversed(plan.rest_strip):
            packed = jnp.concatenate([packed, swap(packed, sizes, (0, mask))], axis=0)
        count = packed.shape[0]
        order = jnp.arange(count) ^ (lax.axis_index("strip") % count)
        packed = jnp.take(packed, order, axis=0)[..., : plan.used]
        packed = packed.reshape(count, plan.inner, plan.block_rows, len(TAP_STEPS), plan.cols)
        packed = packed.transpose(1, 2, 3, 0, 4).reshape(plan.inner, plan.block_rows, plan.half_used)
        packed = jnp.pad(packed, ((0, 0), (0, 0), (0, plan.half_lanes - plan.half_used)))
    for masks in plan.gather_masks[:-1]:
        packed = joined(packed, swap(packed, sizes, *masks), starts.pop(0))
    return packed, swap(packed, sizes, *plan.gather_masks[-1])


def narrowed(plan, total):
    rows = total.shape[0]
    total = total[:, : plan.half_used].reshape(rows, len(TAP_STEPS), plan.half)
    for mask in plan.rest_strip:
        side = (lax.axis_index("strip") // mask) % 2
        parts = total.reshape(rows, len(TAP_STEPS), 2, total.shape[2] // 2)
        kept = jnp.where(side == 0, parts[:, :, 0], parts[:, :, 1])
        given = jnp.where(side == 0, parts[:, :, 1], parts[:, :, 0])
        total = kept + swap(given, plan.sizes, (0, mask))
    total = total.reshape(rows, plan.used)
    return jnp.pad(total, ((0, 0), (0, plan.lanes - plan.used)))


def kernel_terms(plan, acts, grads, scale):
    sizes, f32 = plan.sizes, jnp.float32
    rows, lanes = plan.part_rows, plan.half_lanes

    def run(name, kernel, shape, kind, operands):
        return call(name, kernel, jax.ShapeDtypeStruct(shape, kind), operands)

    part = functools.partial
    b16 = jnp.bfloat16
    shape = (2, rows, lanes)
    send0 = run("send0", part(send_kernel, plan, False), shape, b16, [acts, grads])
    come0 = swap(send0, sizes, *plan.term_masks[0])
    send1 = run("send1", part(send_kernel, plan, True), shape, b16, [after(acts, send0), grads])
    come1 = swap(send1, sizes, *plan.term_masks[0])
    keep0 = run("keep0", part(keep_kernel, plan, False), shape, f32, [after(acts, send1), grads])
    send = run("turn0", part(turn_kernel, plan, False), shape, b16, [keep0, come0])
    come = swap(send, sizes, *plan.term_masks[1])
    keep1 = run("keep1", part(keep_kernel, plan, True), shape, f32, [after(acts, send), grads])
    keep = run("turn1", part(turn_kernel, plan, True), shape, f32, [keep1, come1])
    steps = {"send0": send0, "send1": send1, "keep0": keep0, "turn0": send, "keep1": keep1, "turn1": keep}
    shape = shape[1:]
    send = run("part0", part(part_kernel, plan, False), shape, b16, [keep, come])
    keep = run("part1", part(part_kernel, plan, True), shape, f32, [after(keep, send), come])
    steps.update(part0=send, part1=keep)
    come = swap(send, sizes, *plan.term_masks[2])
    if plan.rest_strip:
        keep = narrowed(plan, keep + decoded(come))
        come = jnp.zeros(keep.shape, b16)
    for mask in plan.rest_band:
        rows //= 2
        shape = (rows, plan.lanes)
        halve = part(halve_kernel, plan, mask, plan.used)
        send = run("halve0", part(halve, False), shape, b16, [keep, come])
        keep = run("halve1", part(halve, True), shape, f32, [after(keep, send), come])
        steps.update(halve0=send, halve1=keep)
        come = swap(send, sizes, (mask, 0))
    total = call(
        "last",
        part(last_kernel, plan, scale),
        jax.ShapeDtypeStruct((len(TAP_STEPS) ** 2, plan.depth, plan.cols), f32),
        [keep, come],
    )
    return total, steps


def edge_kernel(plan, grad, out, copy):
    strip = lax.axis_index("strip")
    for n in range(plan.images):
        out[n] = jnp.where(strip == 0, grad[n, plan.rows - 1], grad[n, 0])
    copy[...] = grad[...]


def borders(plan, grad):
    if plan.strips == 2:
        shape = jax.ShapeDtypeStruct((plan.images, plan.channels, plan.width), grad.dtype)
        copy = jax.ShapeDtypeStruct(grad.shape, grad.dtype)
        edge, grad = call("edge", functools.partial(edge_kernel, plan), (shape, copy), [grad])
        come = [swap(edge, plan.sizes, (core, 1)) for core in range(2)]
        return grad, come, come
    first, last = grad[:, 0], grad[:, plan.rows - 1]
    tops, bottoms = [], []
    for core in range(2):
        down = []
        for b in range(plan.bands):
            down += [(b * plan.strips + s, (b ^ core) * plan.strips + s + 1) for s in range(plan.strips - 1)]
        tops.append(lax.ppermute(last, AXES, down))
        bottoms.append(lax.ppermute(first, AXES, [(b, a) for a, b in down]))
    return grad, tops, bottoms


def body(activations, out_grad, kernel):
    images, channels, rows, width = activations.shape
    bands, strips = lax.axis_size("band"), lax.axis_size("strip")
    plan = Plan(images, channels, rows, width, bands, strips)
    scale = 1.0 / math.sqrt(images * bands * rows * strips * width)
    act = activations.transpose(0, 2, 1, 3)
    grad = out_grad.transpose(0, 2, 1, 3)
    grad0, tops, bottoms = borders(plan, grad)
    act1 = swap(act, plan.sizes, (1, 0))
    grad1 = swap(grad, plan.sizes, (1, 0))
    packed = first_kernel(plan, kernel.transpose(1, 0, 2))
    shape = (2, 2 * plan.part_rows, plan.cells)
    acts = call("acts", functools.partial(acts_kernel, plan), jax.ShapeDtypeStruct(shape, act.dtype), [act, act1])
    shape = (2, plan.half_lanes, plan.cells)
    grads = call(
        "grads",
        functools.partial(grads_kernel, plan),
        jax.ShapeDtypeStruct(shape, grad.dtype),
        [grad0, grad1, *tops, *bottoms],
    )
    kernel_grad, steps = kernel_terms(plan, acts, grads, scale)
    packed = whole_kernel(plan, packed, [steps[name] for name in GATHER_STEPS])
    shape = jax.ShapeDtypeStruct((images, rows, plan.half, width), jnp.bfloat16)
    left = jax.ShapeDtypeStruct((len(TAP_STEPS) * plan.half, 2 * plan.half_lanes), jnp.bfloat16)
    grads = grads.reshape(2 * plan.half_lanes, plan.cells)
    given, left = call(
        "given",
        functools.partial(given_kernel, plan),
        (shape, left),
        [after(packed[0], steps[CELLS_STEP]), packed[1], grads],
    )
    own = call("own", functools.partial(own_kernel, plan), shape, [after(left, given), grads])
    theirs = swap(given, plan.sizes, (1, 0))
    input_grad = call(
        "weave",
        functools.partial(weave_kernel, plan),
        jax.ShapeDtypeStruct((images, rows, channels, width), jnp.bfloat16),
        [own, theirs],
    )
    return input_grad.transpose(0, 2, 1, 3), kernel_grad.transpose(1, 0, 2)


def solution(mesh):
    in_specs = (
        P("band", None, "strip", None),
        P("band", None, "strip", None),
        P("band", None, "strip"),
    )
    out_specs = (P("band", None, "strip", None), P("band", None, "strip"))
    return jax.shard_map(body, mesh=mesh, in_specs=in_specs, out_specs=out_specs, check_vma=False)
```

```python
import functools
import math

import jax
import jax.numpy as jnp
from jax import lax
from jax.experimental import pallas as pl
from jax.experimental.pallas import tpu as pltpu
from jax.sharding import PartitionSpec as P

AXES = ("band", "strip")
TAP_STEPS = (-1, 0, 1)
LANES = 128
TOP_POWER = 2.0**15.5
LEAST_POWER = 2.0**-126
LEAST_PEAK = 1e-30
VMEM_BYTES = 40 * 2**20
HINTS = {
    "edge": 8.0,
    "pack": 8.0,
    "acts": 0.6,
    "grads": 0.5,
    "send0": 1.4,
    "send1": 1.4,
    "keep0": 1.0,
    "keep1": 1.0,
    "turn0": 0.9,
    "turn1": 0.6,
    "part0": 0.5,
    "part1": 0.3,
    "halve0": 0.5,
    "halve1": 3.0,
    "last": 8.0,
    "given": 1.2,
    "own": 0.7,
    "weave": 0.9,
}
GATHER_STEP = "part0"
CELLS_STEP = "halve1"
FLOPS_PER_US = 1.15e9


def padded_lanes(count):
    return (count // LANES + 1) * LANES


def swap(value, sizes, *masks):
    bands, strips = sizes
    pairs = []
    for b in range(bands):
        for s in range(strips):
            masks_here = masks[b % len(masks)]
            pairs.append((b * strips + s, (b ^ masks_here[0]) * strips + (s ^ masks_here[1])))
    return lax.ppermute(value, AXES, pairs)


def call(name, kernel, out_shape, operands, scratch=()):
    return pl.pallas_call(
        kernel,
        out_shape=out_shape,
        in_specs=[pl.BlockSpec(memory_space=pltpu.VMEM)] * len(operands),
        out_specs=jax.tree.map(lambda _: pl.BlockSpec(memory_space=pltpu.VMEM), out_shape),
        scratch_shapes=list(scratch),
        compiler_params=pltpu.CompilerParams(vmem_limit_bytes=VMEM_BYTES),
        cost_estimate=pl.CostEstimate(
            flops=int(HINTS[name] * FLOPS_PER_US), bytes_accessed=0, transcendentals=0
        ),
        name=name,
    )(*operands)


def encoded(peak, value, used):
    lane = lax.broadcasted_iota(jnp.int32, value.shape, value.ndim - 1)
    ratio = value * (TOP_POWER / peak)
    square = ratio * ratio
    power = ratio * jnp.abs(ratio) * square * (square * square)
    return jnp.where(lane < used, power, peak).astype(jnp.bfloat16)


def decoded(message):
    power = message.astype(jnp.float32)
    peak = power[0:1, message.shape[1] - 1 : message.shape[1]]
    size = jnp.maximum(jnp.abs(power), LEAST_POWER)
    fourth = lax.rsqrt(lax.rsqrt(size))
    root = fourth * lax.rsqrt(fourth)
    return jnp.where(power < 0, -root, root) * (peak * (1.0 / TOP_POWER))


def peak_of(value):
    largest = jnp.max(jnp.abs(value))
    largest = jnp.maximum(largest * (1.0 + 2.0**-6), LEAST_PEAK)
    return jnp.full((1, 1), largest, jnp.float32).astype(jnp.bfloat16).astype(jnp.float32)


class Plan:
    def __init__(self, images, channels, rows, width, bands, strips):
        self.images, self.channels, self.rows, self.width = images, channels, rows, width
        self.bands, self.strips = bands, strips
        self.sizes = (bands, strips)
        self.depth = channels // bands
        self.cols = channels // strips
        self.blocks = bands // 2
        self.half = channels // 2
        self.strip_bits = strips.bit_length() - 1
        self.band_bits = bands.bit_length() - 1
        assert bands == 1 << self.band_bits and strips == 1 << self.strip_bits
        assert self.band_bits >= 3 and self.strip_bits >= 1
        self.top_strip = 1 << (self.strip_bits - 1)
        self.rest_strip = [1 << k for k in reversed(range(self.strip_bits - 1))]
        self.rest_band = [1 << k for k in range(3, self.band_bits)]
        self.inner = self.blocks // 4
        self.half_used = len(TAP_STEPS) * self.half
        self.half_lanes = padded_lanes(self.half_used)
        self.used = len(TAP_STEPS) * self.cols
        self.lanes = padded_lanes(self.used)
        self.block_rows = len(TAP_STEPS) * self.depth
        self.part_rows = self.inner * self.block_rows
        self.cells = 2 * images * rows * width
        by_row, by_next, by_col = (2, 0), (4, 0), (0, self.top_strip)
        self.term_masks = ((by_col, by_row), (by_next, by_col), (by_row, by_next))
        self.gather_masks = ((by_col, by_row), (by_row, by_next), (by_next, by_col))

    def block_of(self, slot, by_next, by_row):
        bits = self.band_bits - 3
        turned = sum(((slot >> k) & 1) << (bits - 1 - k) for k in range(bits))
        return turned * 4 + by_next * 2 + by_row

    def chunks(self):
        return [(d, n, h) for d in range(2) for n in range(self.images) for h in range(self.rows)]


def place(plan):
    band, strip = lax.axis_index("band"), lax.axis_index("strip")
    return band % 2, (band // 2) % 2, (band // 4) % 2, strip // plan.top_strip


def mine(plan):
    core, by_row, by_next, by_col = place(plan)
    order = ((by_col, by_next, by_row), (by_row, by_col, by_next))
    return [jnp.where(core == 0, a, b) for a, b in zip(*order)]


def grad_row(plan, grad_ref, top_ref, bottom_ref, image, row, start, strip):
    if row < 0:
        piece = top_ref[image, pl.ds(start, plan.half), :]
        return jnp.where(strip > 0, piece, jnp.zeros_like(piece))
    if row >= plan.rows:
        piece = bottom_ref[image, pl.ds(start, plan.half), :]
        return jnp.where(strip < plan.strips - 1, piece, jnp.zeros_like(piece))
    return grad_ref[image, row, pl.ds(start, plan.half), :]


def moved(value, step):
    width = value.shape[-1]
    if step == 0:
        return value
    lane = lax.broadcasted_iota(jnp.int32, value.shape, value.ndim - 1)
    turned = pltpu.roll(value, (-step) % width, value.ndim - 1)
    inside = lane < width - step if step > 0 else lane >= -step
    return jnp.where(inside, turned, 0.0)


def acts_kernel(plan, act0, act1, out):
    core = lax.axis_index("band") % 2
    depth, width = plan.depth, plan.width
    for at, (d, n, h) in enumerate(plan.chunks()):
        cells = (act0, act1)[d][n, h].astype(jnp.float32)
        shifted = []
        for m in range(plan.blocks):
            begin = 2 * m * depth
            even, odd = cells[begin : begin + depth], cells[begin + depth : begin + 2 * depth]
            block = jnp.where(core == 0, even, odd)
            shifted.append([moved(block, step) for step in TAP_STEPS])
        for i in range(2):
            pieces = []
            for j in range(2):
                for slot in range(plan.inner):
                    here, there = shifted[plan.block_of(slot, i, j)], shifted[plan.block_of(slot, j, i)]
                    pieces += here if i == j else [jnp.where(core == 0, a, b) for a, b in zip(here, there)]
            out[i, :, at * width : (at + 1) * width] = jnp.concatenate(pieces, axis=0).astype(jnp.bfloat16)


def grads_kernel(plan, grad0, grad1, top0, top1, bottom0, bottom1, out):
    strip = lax.axis_index("strip")
    half, width = plan.half, plan.width
    sources = ((grad0, top0, bottom0), (grad1, top1, bottom1))
    for at, (d, n, h) in enumerate(plan.chunks()):
        cells = slice(at * width, (at + 1) * width)
        for x in range(2):
            for r, row_step in enumerate(TAP_STEPS):
                out[x, r * half : (r + 1) * half, cells] = grad_row(
                    plan, *sources[d], n, h - row_step, x * half, strip
                )
            out[x, plan.half_used :, cells] = jnp.zeros((plan.half_lanes - plan.half_used, width), jnp.bfloat16)


def pair_terms(plan, acts, grads, first, second):
    core = lax.axis_index("band") % 2
    i, x = jnp.where(core == 0, second, first), jnp.where(core == 0, first, second)
    return lax.dot_general(acts[i], grads[x], (((1,), (1,)), ((), ())), preferred_element_type=jnp.float32)


def send_kernel(plan, same, acts, grads, *rest):
    packed, out = rest if same else (None, rest[0])
    first, second, _ = mine(plan)
    rows = plan.part_rows
    total = pair_terms(plan, acts, grads, 1 - first, second if same else 1 - second)
    for k in range(2):
        half = total[k * rows : (k + 1) * rows]
        out[k * rows : (k + 1) * rows] = encoded(peak_of(half), half, plan.half_used)
    if same:
        blocks = [packed[k].astype(jnp.float32) for k in range(plan.inner)]
        out[2 * rows :] = jnp.concatenate(blocks, axis=0).astype(jnp.bfloat16)


def keep_kernel(plan, same, acts, grads, out):
    first, second, _ = mine(plan)
    total = pair_terms(plan, acts, grads, first, second if same else 1 - second)
    for k in range(2):
        out[k] = total[k * plan.part_rows : (k + 1) * plan.part_rows]


def turn_kernel(plan, same, keep, message, *rest):
    rows = plan.part_rows
    for k in range(2):
        total = keep[k] + decoded(message[k * rows : (k + 1) * rows])
        rest[1 if same else 0][k] = total if same else encoded(peak_of(total), total, plan.half_used)
    if same:
        sent, _, gathered = rest
        gathered[0] = sent[2 * rows :]
        gathered[1] = message[2 * rows :]


def part_kernel(plan, same, keep, message, out):
    third = mine(plan)[2]
    k = third if same else 1 - third
    total = keep[k] + decoded(message[k])
    out[...] = total if same else encoded(peak_of(total), total, plan.half_used)


def halve_kernel(plan, mask, used, same, keep, message, out):
    side = (lax.axis_index("band") // mask) % 2
    total = keep[...] + decoded(message[...])
    rows = total.shape[0] // 2
    lower, upper = total[:rows], total[rows:]
    if same:
        out[...] = jnp.where(side == 0, lower, upper)
    else:
        given = jnp.where(side == 0, upper, lower)
        out[...] = encoded(peak_of(given), given, used)


def last_kernel(plan, scale, keep, message, out):
    total = (keep[...] + decoded(message[...])) * scale
    depth, cols = plan.depth, plan.cols
    for r in range(len(TAP_STEPS)):
        for c in range(len(TAP_STEPS)):
            out[r * len(TAP_STEPS) + c] = total[c * depth : (c + 1) * depth, r * cols : (r + 1) * cols]


def pack_kernel(plan, kernel, out):
    rows = []
    for c in range(len(TAP_STEPS)):
        pieces = [kernel[r * len(TAP_STEPS) + c].astype(jnp.float32) for r in range(len(TAP_STEPS))]
        pieces.append(jnp.zeros((plan.depth, plan.lanes - plan.used), jnp.float32))
        rows.append(jnp.concatenate(pieces, axis=1))
    out[...] = jnp.concatenate(rows, axis=0).astype(jnp.bfloat16)


def cells_of(plan, d, left, grads, out):
    width, half = plan.width, plan.half
    rows = [(n, h) for n in range(plan.images) for h in range(plan.rows)]
    for begin in range(0, len(rows), 2):
        part = rows[begin : begin + 2]
        at = (d * len(rows) + begin) * width
        product = jnp.dot(
            left[...], grads[:, at : at + len(part) * width], preferred_element_type=jnp.float32
        )
        for k, (n, h) in enumerate(part):
            total = None
            for c, col_step in enumerate(TAP_STEPS):
                term = moved(product[c * half : (c + 1) * half, k * width : (k + 1) * width], -col_step)
                total = term if total is None else total + term
            out[n, h] = total.astype(jnp.bfloat16)


def given_kernel(plan, own, other, grads, out, left):
    core, row_bit, next_bit, col_bit = place(plan)
    rest = lax.axis_index("band") // 8
    depth, half, lanes = plan.depth, plan.half, plan.half_lanes
    for x in range(2):
        rows = [[] for _ in TAP_STEPS]
        for m in range(plan.blocks):
            row, behind, col = (m % 2) ^ row_bit, (m // 2 % 2) ^ next_bit, x ^ col_bit
            one = jnp.where(core == 0, col, row)
            two = jnp.where(core == 0, row, behind)
            three = jnp.where(core == 0, behind, col)
            slot = two * 2 + one
            pair = jnp.where(three == 0, own[slot], other[slot]).astype(jnp.float32)
            block = pair[: plan.block_rows]
            for k in range(1, plan.inner):
                at = pair[k * plan.block_rows : (k + 1) * plan.block_rows]
                block = jnp.where(((m // 4) ^ rest) == k, at, block)
            for c in range(len(TAP_STEPS)):
                rows[c].append(block[c * depth : (c + 1) * depth])
        for c in range(len(TAP_STEPS)):
            left[c * half : (c + 1) * half, x * lanes : (x + 1) * lanes] = jnp.concatenate(
                rows[c], axis=0
            ).astype(jnp.bfloat16)
    cells_of(plan, 1, left, grads, out)


def own_kernel(plan, left, grads, out):
    cells_of(plan, 0, left, grads, out)


def weave_kernel(plan, own, theirs, out):
    core = lax.axis_index("band") % 2
    depth = plan.depth
    for n in range(plan.images):
        for h in range(plan.rows):
            a, b = own[n, h].astype(jnp.float32), theirs[n, h].astype(jnp.float32)
            even, odd = jnp.where(core == 0, a, b), jnp.where(core == 0, b, a)
            pieces = []
            for m in range(plan.blocks):
                pieces += [even[m * depth : (m + 1) * depth], odd[m * depth : (m + 1) * depth]]
            out[n, h] = jnp.concatenate(pieces, axis=0).astype(jnp.bfloat16)


def after(value, *others):
    return lax.optimization_barrier((value, *others))[0]


def first_kernel(plan, kernel, step):
    sizes = plan.sizes
    shape = jax.ShapeDtypeStruct((plan.block_rows, plan.lanes), jnp.bfloat16)
    packed = call("pack", functools.partial(pack_kernel, plan), shape, [kernel])[None]
    for mask in reversed(plan.rest_band):
        packed = jnp.concatenate([packed, after(swap(packed, sizes, (mask, 0)), step)], axis=0)
    if plan.rest_strip:
        packed = packed[None]
        for mask in reversed(plan.rest_strip):
            packed = jnp.concatenate([packed, swap(packed, sizes, (0, mask))], axis=0)
        count = packed.shape[0]
        order = jnp.arange(count) ^ (lax.axis_index("strip") % count)
        packed = jnp.take(packed, order, axis=0)[..., : plan.used]
        packed = packed.reshape(count, plan.inner, plan.block_rows, len(TAP_STEPS), plan.cols)
        packed = packed.transpose(1, 2, 3, 0, 4).reshape(plan.inner, plan.block_rows, plan.half_used)
        packed = jnp.pad(packed, ((0, 0), (0, 0), (0, plan.half_lanes - plan.half_used)))
    return packed


def whole_kernel(plan, packed, step):
    packed = jnp.concatenate([packed, swap(packed, plan.sizes, *plan.gather_masks[1])], axis=0)
    packed = after(packed, step)
    return packed, swap(packed, plan.sizes, *plan.gather_masks[2])


def narrowed(plan, total):
    rows = total.shape[0]
    total = total[:, : plan.half_used].reshape(rows, len(TAP_STEPS), plan.half)
    for mask in plan.rest_strip:
        side = (lax.axis_index("strip") // mask) % 2
        parts = total.reshape(rows, len(TAP_STEPS), 2, total.shape[2] // 2)
        kept = jnp.where(side == 0, parts[:, :, 0], parts[:, :, 1])
        given = jnp.where(side == 0, parts[:, :, 1], parts[:, :, 0])
        total = kept + swap(given, plan.sizes, (0, mask))
    total = total.reshape(rows, plan.used)
    return jnp.pad(total, ((0, 0), (0, plan.lanes - plan.used)))


def kernel_terms(plan, acts, grads, kernel, scale):
    sizes, f32 = plan.sizes, jnp.float32
    rows, lanes = plan.part_rows, plan.half_lanes

    def run(name, kernel, shape, kind, operands):
        return call(name, kernel, jax.ShapeDtypeStruct(shape, kind), operands)

    part = functools.partial
    b16 = jnp.bfloat16
    shape = (2, rows, lanes)
    send0 = run("send0", part(send_kernel, plan, False), (2 * rows, lanes), b16, [acts, grads])
    come0 = swap(send0, sizes, *plan.term_masks[0])
    keep0 = run("keep0", part(keep_kernel, plan, False), shape, f32, [after(acts, send0), grads])
    packed = first_kernel(plan, kernel, keep0)
    send1 = run("send1", part(send_kernel, plan, True), (3 * rows, lanes), b16, [after(acts, keep0), grads, packed])
    come1 = swap(send1, sizes, *plan.term_masks[0])
    send = run("turn0", part(turn_kernel, plan, False), shape, b16, [keep0, come0])
    come = swap(send, sizes, *plan.term_masks[1])
    keep1 = run("keep1", part(keep_kernel, plan, True), shape, f32, [after(acts, send), grads])
    shapes = (jax.ShapeDtypeStruct(shape, f32), jax.ShapeDtypeStruct(shape, b16))
    keep, packed = call("turn1", part(turn_kernel, plan, True), shapes, [keep1, come1, send1])
    steps = {"send0": send0, "send1": send1, "keep0": keep0, "turn0": send, "keep1": keep1, "turn1": keep}
    shape = shape[1:]
    send = run("part0", part(part_kernel, plan, False), shape, b16, [keep, come])
    keep = run("part1", part(part_kernel, plan, True), shape, f32, [after(keep, send), come])
    steps.update(part0=send, part1=keep)
    come = swap(send, sizes, *plan.term_masks[2])
    if plan.rest_strip:
        keep = narrowed(plan, keep + decoded(come))
        come = jnp.zeros(keep.shape, b16)
    for mask in plan.rest_band:
        rows //= 2
        shape = (rows, plan.lanes)
        halve = part(halve_kernel, plan, mask, plan.used)
        send = run("halve0", part(halve, False), shape, b16, [keep, come])
        keep = run("halve1", part(halve, True), shape, f32, [after(keep, send), come])
        steps.update(halve0=send, halve1=keep)
        come = swap(send, sizes, (mask, 0))
    total = call(
        "last",
        part(last_kernel, plan, scale),
        jax.ShapeDtypeStruct((len(TAP_STEPS) ** 2, plan.depth, plan.cols), f32),
        [keep, come],
    )
    return total, packed, steps


def edge_kernel(plan, grad, out, copy):
    strip = lax.axis_index("strip")
    for n in range(plan.images):
        out[n] = jnp.where(strip == 0, grad[n, plan.rows - 1], grad[n, 0])
    copy[...] = grad[...]


def borders(plan, grad):
    if plan.strips == 2:
        shape = jax.ShapeDtypeStruct((plan.images, plan.channels, plan.width), grad.dtype)
        copy = jax.ShapeDtypeStruct(grad.shape, grad.dtype)
        edge, grad = call("edge", functools.partial(edge_kernel, plan), (shape, copy), [grad])
        come = [swap(edge, plan.sizes, (core, 1)) for core in range(2)]
        return grad, come, come
    first, last = grad[:, 0], grad[:, plan.rows - 1]
    tops, bottoms = [], []
    for core in range(2):
        down = []
        for b in range(plan.bands):
            down += [(b * plan.strips + s, (b ^ core) * plan.strips + s + 1) for s in range(plan.strips - 1)]
        tops.append(lax.ppermute(last, AXES, down))
        bottoms.append(lax.ppermute(first, AXES, [(b, a) for a, b in down]))
    return grad, tops, bottoms


def body(activations, out_grad, kernel):
    images, channels, rows, width = activations.shape
    bands, strips = lax.axis_size("band"), lax.axis_size("strip")
    plan = Plan(images, channels, rows, width, bands, strips)
    scale = 1.0 / math.sqrt(images * bands * rows * strips * width)
    act = activations.transpose(0, 2, 1, 3)
    grad = out_grad.transpose(0, 2, 1, 3)
    grad0, tops, bottoms = borders(plan, grad)
    act1 = swap(act, plan.sizes, (1, 0))
    grad1 = swap(grad, plan.sizes, (1, 0))
    shape = (2, 2 * plan.part_rows, plan.cells)
    acts = call("acts", functools.partial(acts_kernel, plan), jax.ShapeDtypeStruct(shape, act.dtype), [act, act1])
    shape = (2, plan.half_lanes, plan.cells)
    grads = call(
        "grads",
        functools.partial(grads_kernel, plan),
        jax.ShapeDtypeStruct(shape, grad.dtype),
        [grad0, grad1, *tops, *bottoms],
    )
    kernel_grad, packed, steps = kernel_terms(plan, acts, grads, kernel.transpose(1, 0, 2), scale)
    packed = whole_kernel(plan, packed, steps[GATHER_STEP])
    shape = jax.ShapeDtypeStruct((images, rows, plan.half, width), jnp.bfloat16)
    left = jax.ShapeDtypeStruct((len(TAP_STEPS) * plan.half, 2 * plan.half_lanes), jnp.bfloat16)
    grads = grads.reshape(2 * plan.half_lanes, plan.cells)
    given, left = call(
        "given",
        functools.partial(given_kernel, plan),
        (shape, left),
        [after(packed[0], steps[CELLS_STEP]), packed[1], grads],
    )
    own = call("own", functools.partial(own_kernel, plan), shape, [after(left, given), grads])
    theirs = swap(given, plan.sizes, (1, 0))
    input_grad = call(
        "weave",
        functools.partial(weave_kernel, plan),
        jax.ShapeDtypeStruct((images, rows, channels, width), jnp.bfloat16),
        [own, theirs],
    )
    return input_grad.transpose(0, 2, 1, 3), kernel_grad.transpose(1, 0, 2)


def solution(mesh):
    in_specs = (
        P("band", None, "strip", None),
        P("band", None, "strip", None),
        P("band", None, "strip"),
    )
    out_specs = (P("band", None, "strip", None), P("band", None, "strip"))
    return jax.shard_map(body, mesh=mesh, in_specs=in_specs, out_specs=out_specs, check_vma=False)
```

```python
import functools
import math

import jax
import jax.numpy as jnp
from jax import lax
from jax.experimental import pallas as pl
from jax.experimental.pallas import tpu as pltpu
from jax.sharding import PartitionSpec as P

AXES = ("band", "strip")
TAP_STEPS = (-1, 0, 1)
LANES = 128
TOP_POWER = 2.0**15.5
LEAST_POWER = 2.0**-126
LEAST_PEAK = 1e-30
VMEM_BYTES = 40 * 2**20
HINTS = {
    "edge": 8.0,
    "pair": 0.2,
    "pack": 8.0,
    "acts": 0.6,
    "grads": 0.5,
    "send0": 1.4,
    "send1": 1.4,
    "keep0": 1.0,
    "keep1": 1.0,
    "turn0": 0.9,
    "turn1": 0.6,
    "part0": 0.5,
    "part1": 0.3,
    "halve0": 0.5,
    "halve1": 3.0,
    "last": 8.0,
    "given": 1.2,
    "own": 0.7,
    "weave": 0.9,
}
GATHER_STEPS = ("keep0", "turn0", "part0")
CELLS_STEP = "halve1"
FLOPS_PER_US = 1.15e9


def padded_lanes(count):
    return (count // LANES + 1) * LANES


def swap(value, sizes, *masks):
    bands, strips = sizes
    pairs = []
    for b in range(bands):
        for s in range(strips):
            masks_here = masks[b % len(masks)]
            pairs.append((b * strips + s, (b ^ masks_here[0]) * strips + (s ^ masks_here[1])))
    return lax.ppermute(value, AXES, pairs)


def call(name, kernel, out_shape, operands, scratch=()):
    return pl.pallas_call(
        kernel,
        out_shape=out_shape,
        in_specs=[pl.BlockSpec(memory_space=pltpu.VMEM)] * len(operands),
        out_specs=jax.tree.map(lambda _: pl.BlockSpec(memory_space=pltpu.VMEM), out_shape),
        scratch_shapes=list(scratch),
        compiler_params=pltpu.CompilerParams(vmem_limit_bytes=VMEM_BYTES),
        cost_estimate=pl.CostEstimate(
            flops=int(HINTS[name] * FLOPS_PER_US), bytes_accessed=0, transcendentals=0
        ),
        name=name,
    )(*operands)


def encoded(peak, value, used):
    lane = lax.broadcasted_iota(jnp.int32, value.shape, value.ndim - 1)
    ratio = value * (TOP_POWER / peak)
    square = ratio * ratio
    power = ratio * jnp.abs(ratio) * square * (square * square)
    return jnp.where(lane < used, power, peak).astype(jnp.bfloat16)


def decoded(message):
    power = message.astype(jnp.float32)
    peak = power[0:1, message.shape[1] - 1 : message.shape[1]]
    size = jnp.maximum(jnp.abs(power), LEAST_POWER)
    fourth = lax.rsqrt(lax.rsqrt(size))
    root = fourth * lax.rsqrt(fourth)
    return jnp.where(power < 0, -root, root) * (peak * (1.0 / TOP_POWER))


def peak_of(value):
    largest = jnp.max(jnp.abs(value))
    largest = jnp.maximum(largest * (1.0 + 2.0**-6), LEAST_PEAK)
    return jnp.full((1, 1), largest, jnp.float32).astype(jnp.bfloat16).astype(jnp.float32)


class Plan:
    def __init__(self, images, channels, rows, width, bands, strips):
        self.images, self.channels, self.rows, self.width = images, channels, rows, width
        self.bands, self.strips = bands, strips
        self.sizes = (bands, strips)
        self.depth = channels // bands
        self.cols = channels // strips
        self.blocks = bands // 2
        self.half = channels // 2
        self.strip_bits = strips.bit_length() - 1
        self.band_bits = bands.bit_length() - 1
        assert bands == 1 << self.band_bits and strips == 1 << self.strip_bits
        assert self.band_bits >= 3 and self.strip_bits >= 1
        self.top_strip = 1 << (self.strip_bits - 1)
        self.rest_strip = [1 << k for k in reversed(range(self.strip_bits - 1))]
        self.rest_band = [1 << k for k in range(3, self.band_bits)]
        self.inner = self.blocks // 4
        self.half_used = len(TAP_STEPS) * self.half
        self.half_lanes = padded_lanes(self.half_used)
        self.used = len(TAP_STEPS) * self.cols
        self.lanes = padded_lanes(self.used)
        self.block_rows = len(TAP_STEPS) * self.depth
        self.part_rows = self.inner * self.block_rows
        self.cells = 2 * images * rows * width
        by_row, by_next, by_col = (2, 0), (4, 0), (0, self.top_strip)
        self.term_masks = ((by_col, by_next), (by_row, by_col), (by_next, by_row))
        self.gather_masks = ((by_row, by_col), (by_next, by_next), (by_col, by_row))

    def block_of(self, slot, by_next, by_row):
        bits = self.band_bits - 3
        turned = sum(((slot >> k) & 1) << (bits - 1 - k) for k in range(bits))
        return turned * 4 + by_next * 2 + by_row

    def chunks(self):
        return [(d, n, h) for d in range(2) for n in range(self.images) for h in range(self.rows)]


def place(plan):
    band, strip = lax.axis_index("band"), lax.axis_index("strip")
    return band % 2, (band // 2) % 2, (band // 4) % 2, strip // plan.top_strip


def mine(plan):
    core, by_row, by_next, by_col = place(plan)
    order = ((by_col, by_row, by_next), (by_next, by_col, by_row))
    return [jnp.where(core == 0, a, b) for a, b in zip(*order)]


def grad_row(plan, grad_ref, top_ref, bottom_ref, image, row, start, strip):
    if row < 0:
        piece = top_ref[image, pl.ds(start, plan.half), :]
        return jnp.where(strip > 0, piece, jnp.zeros_like(piece))
    if row >= plan.rows:
        piece = bottom_ref[image, pl.ds(start, plan.half), :]
        return jnp.where(strip < plan.strips - 1, piece, jnp.zeros_like(piece))
    return grad_ref[image, row, pl.ds(start, plan.half), :]


def moved(value, step):
    width = value.shape[-1]
    if step == 0:
        return value
    lane = lax.broadcasted_iota(jnp.int32, value.shape, value.ndim - 1)
    turned = pltpu.roll(value, (-step) % width, value.ndim - 1)
    inside = lane < width - step if step > 0 else lane >= -step
    return jnp.where(inside, turned, 0.0)


def acts_kernel(plan, act0, act1, out):
    core = lax.axis_index("band") % 2
    depth, width = plan.depth, plan.width
    for at, (d, n, h) in enumerate(plan.chunks()):
        cells = (act0, act1)[d][n, h].astype(jnp.float32)
        shifted = []
        for m in range(plan.blocks):
            begin = 2 * m * depth
            even, odd = cells[begin : begin + depth], cells[begin + depth : begin + 2 * depth]
            block = jnp.where(core == 0, even, odd)
            shifted.append([moved(block, step) for step in TAP_STEPS])
        for i in range(2):
            pieces = []
            for j in range(2):
                for slot in range(plan.inner):
                    here, there = shifted[plan.block_of(slot, j, i)], shifted[plan.block_of(slot, i, j)]
                    pieces += here if i == j else [jnp.where(core == 0, a, b) for a, b in zip(here, there)]
            out[i, :, at * width : (at + 1) * width] = jnp.concatenate(pieces, axis=0).astype(jnp.bfloat16)


def grads_kernel(plan, grad0, grad1, top0, top1, bottom0, bottom1, out):
    strip = lax.axis_index("strip")
    half, width = plan.half, plan.width
    sources = ((grad0, top0, bottom0), (grad1, top1, bottom1))
    for at, (d, n, h) in enumerate(plan.chunks()):
        cells = slice(at * width, (at + 1) * width)
        for x in range(2):
            for r, row_step in enumerate(TAP_STEPS):
                out[x, r * half : (r + 1) * half, cells] = grad_row(
                    plan, *sources[d], n, h - row_step, x * half, strip
                )
            out[x, plan.half_used :, cells] = jnp.zeros((plan.half_lanes - plan.half_used, width), jnp.bfloat16)


def pair_terms(plan, acts, grads, first, second):
    core = lax.axis_index("band") % 2
    i, x = jnp.where(core == 0, second, first), jnp.where(core == 0, first, second)
    return lax.dot_general(acts[i], grads[x], (((1,), (1,)), ((), ())), preferred_element_type=jnp.float32)


def send_kernel(plan, same, acts, grads, out):
    first, second, _ = mine(plan)
    total = pair_terms(plan, acts, grads, 1 - first, second if same else 1 - second)
    for k in range(2):
        half = total[k * plan.part_rows : (k + 1) * plan.part_rows]
        out[k] = encoded(peak_of(half), half, plan.half_used)


def keep_kernel(plan, same, acts, grads, out):
    first, second, _ = mine(plan)
    total = pair_terms(plan, acts, grads, first, second if same else 1 - second)
    for k in range(2):
        out[k] = total[k * plan.part_rows : (k + 1) * plan.part_rows]


def turn_kernel(plan, same, keep, message, out):
    for k in range(2):
        total = keep[k] + decoded(message[k])
        out[k] = total if same else encoded(peak_of(total), total, plan.half_used)


def part_kernel(plan, same, keep, message, out):
    third = mine(plan)[2]
    k = third if same else 1 - third
    total = keep[k] + decoded(message[k])
    out[...] = total if same else encoded(peak_of(total), total, plan.half_used)


def halve_kernel(plan, mask, used, same, keep, message, out):
    side = (lax.axis_index("band") // mask) % 2
    total = keep[...] + decoded(message[...])
    rows = total.shape[0] // 2
    lower, upper = total[:rows], total[rows:]
    if same:
        out[...] = jnp.where(side == 0, lower, upper)
    else:
        given = jnp.where(side == 0, upper, lower)
        out[...] = encoded(peak_of(given), given, used)


def last_kernel(plan, scale, keep, message, out):
    total = (keep[...] + decoded(message[...])) * scale
    depth, cols = plan.depth, plan.cols
    for r in range(len(TAP_STEPS)):
        for c in range(len(TAP_STEPS)):
            out[r * len(TAP_STEPS) + c] = total[c * depth : (c + 1) * depth, r * cols : (r + 1) * cols]


def pack_kernel(plan, kernel, out):
    rows = []
    for c in range(len(TAP_STEPS)):
        pieces = [kernel[r * len(TAP_STEPS) + c].astype(jnp.float32) for r in range(len(TAP_STEPS))]
        pieces.append(jnp.zeros((plan.depth, plan.lanes - plan.used), jnp.float32))
        rows.append(jnp.concatenate(pieces, axis=1))
    out[...] = jnp.concatenate(rows, axis=0).astype(jnp.bfloat16)


def cells_of(plan, d, left, grads, out):
    width, half = plan.width, plan.half
    rows = [(n, h) for n in range(plan.images) for h in range(plan.rows)]
    for begin in range(0, len(rows), 2):
        part = rows[begin : begin + 2]
        at = (d * len(rows) + begin) * width
        product = jnp.dot(
            left[...], grads[:, at : at + len(part) * width], preferred_element_type=jnp.float32
        )
        for k, (n, h) in enumerate(part):
            total = None
            for c, col_step in enumerate(TAP_STEPS):
                term = moved(product[c * half : (c + 1) * half, k * width : (k + 1) * width], -col_step)
                total = term if total is None else total + term
            out[n, h] = total.astype(jnp.bfloat16)


def given_kernel(plan, own, other, grads, out, left):
    core, row_bit, next_bit, col_bit = place(plan)
    rest = lax.axis_index("band") // 8
    depth, half, lanes = plan.depth, plan.half, plan.half_lanes
    for x in range(2):
        rows = [[] for _ in TAP_STEPS]
        for m in range(plan.blocks):
            row, behind, col = (m % 2) ^ row_bit, (m // 2 % 2) ^ next_bit, x ^ col_bit
            one = jnp.where(core == 0, row, col)
            three = jnp.where(core == 0, col, row)
            slot = behind * 2 + one
            pair = jnp.where(three == 0, own[slot], other[slot]).astype(jnp.float32)
            block = pair[: plan.block_rows]
            for k in range(1, plan.inner):
                at = pair[k * plan.block_rows : (k + 1) * plan.block_rows]
                block = jnp.where(((m // 4) ^ rest) == k, at, block)
            for c in range(len(TAP_STEPS)):
                rows[c].append(block[c * depth : (c + 1) * depth])
        for c in range(len(TAP_STEPS)):
            left[c * half : (c + 1) * half, x * lanes : (x + 1) * lanes] = jnp.concatenate(
                rows[c], axis=0
            ).astype(jnp.bfloat16)
    cells_of(plan, 1, left, grads, out)


def own_kernel(plan, left, grads, out):
    cells_of(plan, 0, left, grads, out)


def weave_kernel(plan, own, theirs, out):
    core = lax.axis_index("band") % 2
    depth = plan.depth
    for n in range(plan.images):
        for h in range(plan.rows):
            a, b = own[n, h].astype(jnp.float32), theirs[n, h].astype(jnp.float32)
            even, odd = jnp.where(core == 0, a, b), jnp.where(core == 0, b, a)
            pieces = []
            for m in range(plan.blocks):
                pieces += [even[m * depth : (m + 1) * depth], odd[m * depth : (m + 1) * depth]]
            out[n, h] = jnp.concatenate(pieces, axis=0).astype(jnp.bfloat16)


def after(value, *others):
    return lax.optimization_barrier((value, *others))[0]


def pair_kernel(plan, *refs):
    blocks = [ref[k].astype(jnp.float32) for ref in refs[:-1] for k in range(ref.shape[0])]
    refs[-1][0] = jnp.concatenate(blocks, axis=0).astype(jnp.bfloat16)


def first_kernel(plan, kernel):
    shape = jax.ShapeDtypeStruct((plan.block_rows, plan.lanes), jnp.bfloat16)
    packed = call("pack", functools.partial(pack_kernel, plan), shape, [kernel])[None]
    for mask in plan.rest_band[:0:-1]:
        packed = jnp.concatenate([packed, swap(packed, plan.sizes, (mask, 0))], axis=0)
    return [packed] + [swap(packed, plan.sizes, (mask, 0)) for mask in plan.rest_band[:1]]


def whole_kernel(plan, packed, starts):
    sizes = plan.sizes
    starts = list(starts)
    packed = [*packed[:-1], after(packed[-1], starts[0])]
    if plan.rest_strip:
        packed = jnp.concatenate(packed, axis=0)[None]
        for mask in reversed(plan.rest_strip):
            packed = jnp.concatenate([packed, swap(packed, sizes, (0, mask))], axis=0)
        count = packed.shape[0]
        order = jnp.arange(count) ^ (lax.axis_index("strip") % count)
        packed = jnp.take(packed, order, axis=0)[..., : plan.used]
        packed = packed.reshape(count, plan.inner, plan.block_rows, len(TAP_STEPS), plan.cols)
        packed = packed.transpose(1, 2, 3, 0, 4).reshape(plan.inner, plan.block_rows, plan.half_used)
        packed = [jnp.pad(packed, ((0, 0), (0, 0), (0, plan.half_lanes - plan.half_used)))]
    shape = jax.ShapeDtypeStruct((1, plan.part_rows, plan.half_lanes), jnp.bfloat16)
    packed = call("pair", functools.partial(pair_kernel, plan), shape, packed)
    packed = after(packed, starts.pop(0))
    for masks in plan.gather_masks[:-1]:
        come = after(swap(packed, sizes, *masks), starts[0])
        packed = after(jnp.concatenate([packed, come], axis=0), starts.pop(0))
    return packed, swap(packed, sizes, *plan.gather_masks[-1])


def narrowed(plan, total):
    rows = total.shape[0]
    total = total[:, : plan.half_used].reshape(rows, len(TAP_STEPS), plan.half)
    for mask in plan.rest_strip:
        side = (lax.axis_index("strip") // mask) % 2
        parts = total.reshape(rows, len(TAP_STEPS), 2, total.shape[2] // 2)
        kept = jnp.where(side == 0, parts[:, :, 0], parts[:, :, 1])
        given = jnp.where(side == 0, parts[:, :, 1], parts[:, :, 0])
        total = kept + swap(given, plan.sizes, (0, mask))
    total = total.reshape(rows, plan.used)
    return jnp.pad(total, ((0, 0), (0, plan.lanes - plan.used)))


def kernel_terms(plan, acts, grads, scale):
    sizes, f32 = plan.sizes, jnp.float32
    rows, lanes = plan.part_rows, plan.half_lanes

    def run(name, kernel, shape, kind, operands):
        return call(name, kernel, jax.ShapeDtypeStruct(shape, kind), operands)

    part = functools.partial
    b16 = jnp.bfloat16
    shape = (2, rows, lanes)
    send0 = run("send0", part(send_kernel, plan, False), shape, b16, [acts, grads])
    come0 = swap(send0, sizes, *plan.term_masks[0])
    keep0 = run("keep0", part(keep_kernel, plan, False), shape, f32, [after(acts, send0), grads])
    send1 = run("send1", part(send_kernel, plan, True), shape, b16, [after(acts, keep0), grads])
    come1 = swap(send1, sizes, *plan.term_masks[0])
    send = run("turn0", part(turn_kernel, plan, False), shape, b16, [keep0, come0])
    come = swap(send, sizes, *plan.term_masks[1])
    keep1 = run("keep1", part(keep_kernel, plan, True), shape, f32, [after(acts, send), grads])
    keep = run("turn1", part(turn_kernel, plan, True), shape, f32, [keep1, come1])
    steps = {"send0": send0, "send1": send1, "keep0": keep0, "turn0": send, "keep1": keep1, "turn1": keep}
    shape = shape[1:]
    send = run("part0", part(part_kernel, plan, False), shape, b16, [keep, come])
    keep = run("part1", part(part_kernel, plan, True), shape, f32, [after(keep, send), come])
    steps.update(part0=send, part1=keep)
    come = swap(send, sizes, *plan.term_masks[2])
    if plan.rest_strip:
        keep = narrowed(plan, keep + decoded(come))
        come = jnp.zeros(keep.shape, b16)
    for mask in plan.rest_band:
        rows //= 2
        shape = (rows, plan.lanes)
        halve = part(halve_kernel, plan, mask, plan.used)
        send = run("halve0", part(halve, False), shape, b16, [keep, come])
        keep = run("halve1", part(halve, True), shape, f32, [after(keep, send), come])
        steps.update(halve0=send, halve1=keep)
        come = swap(send, sizes, (mask, 0))
    total = call(
        "last",
        part(last_kernel, plan, scale),
        jax.ShapeDtypeStruct((len(TAP_STEPS) ** 2, plan.depth, plan.cols), f32),
        [keep, come],
    )
    return total, steps


def edge_kernel(plan, grad, out, copy):
    strip = lax.axis_index("strip")
    for n in range(plan.images):
        out[n] = jnp.where(strip == 0, grad[n, plan.rows - 1], grad[n, 0])
    copy[...] = grad[...]


def borders(plan, grad):
    if plan.strips == 2:
        shape = jax.ShapeDtypeStruct((plan.images, plan.channels, plan.width), grad.dtype)
        copy = jax.ShapeDtypeStruct(grad.shape, grad.dtype)
        edge, grad = call("edge", functools.partial(edge_kernel, plan), (shape, copy), [grad])
        come = [swap(edge, plan.sizes, (core, 1)) for core in range(2)]
        return grad, come, come
    first, last = grad[:, 0], grad[:, plan.rows - 1]
    tops, bottoms = [], []
    for core in range(2):
        down = []
        for b in range(plan.bands):
            down += [(b * plan.strips + s, (b ^ core) * plan.strips + s + 1) for s in range(plan.strips - 1)]
        tops.append(lax.ppermute(last, AXES, down))
        bottoms.append(lax.ppermute(first, AXES, [(b, a) for a, b in down]))
    return grad, tops, bottoms


def body(activations, out_grad, kernel):
    images, channels, rows, width = activations.shape
    bands, strips = lax.axis_size("band"), lax.axis_size("strip")
    plan = Plan(images, channels, rows, width, bands, strips)
    scale = 1.0 / math.sqrt(images * bands * rows * strips * width)
    act = activations.transpose(0, 2, 1, 3)
    grad = out_grad.transpose(0, 2, 1, 3)
    grad0, tops, bottoms = borders(plan, grad)
    act1 = swap(act, plan.sizes, (1, 0))
    grad1 = swap(grad, plan.sizes, (1, 0))
    packed = first_kernel(plan, kernel.transpose(1, 0, 2))
    shape = (2, 2 * plan.part_rows, plan.cells)
    acts = call("acts", functools.partial(acts_kernel, plan), jax.ShapeDtypeStruct(shape, act.dtype), [act, act1])
    shape = (2, plan.half_lanes, plan.cells)
    grads = call(
        "grads",
        functools.partial(grads_kernel, plan),
        jax.ShapeDtypeStruct(shape, grad.dtype),
        [grad0, grad1, *tops, *bottoms],
    )
    kernel_grad, steps = kernel_terms(plan, acts, grads, scale)
    packed = whole_kernel(plan, packed, [steps[name] for name in GATHER_STEPS])
    shape = jax.ShapeDtypeStruct((images, rows, plan.half, width), jnp.bfloat16)
    left = jax.ShapeDtypeStruct((len(TAP_STEPS) * plan.half, 2 * plan.half_lanes), jnp.bfloat16)
    grads = grads.reshape(2 * plan.half_lanes, plan.cells)
    given, left = call(
        "given",
        functools.partial(given_kernel, plan),
        (shape, left),
        [after(packed[0], steps[CELLS_STEP]), packed[1], grads],
    )
    own = call("own", functools.partial(own_kernel, plan), shape, [after(left, given), grads])
    theirs = swap(given, plan.sizes, (1, 0))
    input_grad = call(
        "weave",
        functools.partial(weave_kernel, plan),
        jax.ShapeDtypeStruct((images, rows, channels, width), jnp.bfloat16),
        [own, theirs],
    )
    return input_grad.transpose(0, 2, 1, 3), kernel_grad.transpose(1, 0, 2)


def solution(mesh):
    in_specs = (
        P("band", None, "strip", None),
        P("band", None, "strip", None),
        P("band", None, "strip"),
    )
    out_specs = (P("band", None, "strip", None), P("band", None, "strip"))
    return jax.shard_map(body, mesh=mesh, in_specs=in_specs, out_specs=out_specs, check_vma=False)
```

```python
import functools
import math

import jax
import jax.numpy as jnp
from jax import lax
from jax.experimental import pallas as pl
from jax.experimental.pallas import tpu as pltpu
from jax.sharding import PartitionSpec as P

AXES = ("band", "strip")
TAP_STEPS = (-1, 0, 1)
LANES = 128
TOP_POWER = 2.0**15.5
LEAST_POWER = 2.0**-126
LEAST_PEAK = 1e-30
VMEM_BYTES = 40 * 2**20
HINTS = {
    "edge": 8.0,
    "pair": 0.2,
    "pack": 8.0,
    "acts": 0.6,
    "grads": 0.5,
    "send0": 1.4,
    "send1": 1.4,
    "keep0": 1.0,
    "keep1": 1.0,
    "turn0": 0.9,
    "turn1": 0.6,
    "part0": 0.5,
    "part1": 0.3,
    "halve0": 0.5,
    "halve1": 3.0,
    "last": 8.0,
    "given": 1.2,
    "own": 0.7,
    "weave": 0.9,
}
GATHER_STEPS = ("keep0", "turn0", "part0")
CELLS_STEP = "halve1"
FLOPS_PER_US = 1.15e9


def padded_lanes(count):
    return (count // LANES + 1) * LANES


def swap(value, sizes, *masks):
    bands, strips = sizes
    pairs = []
    for b in range(bands):
        for s in range(strips):
            masks_here = masks[b % len(masks)]
            pairs.append((b * strips + s, (b ^ masks_here[0]) * strips + (s ^ masks_here[1])))
    return lax.ppermute(value, AXES, pairs)


def call(name, kernel, out_shape, operands, scratch=()):
    return pl.pallas_call(
        kernel,
        out_shape=out_shape,
        in_specs=[pl.BlockSpec(memory_space=pltpu.VMEM)] * len(operands),
        out_specs=jax.tree.map(lambda _: pl.BlockSpec(memory_space=pltpu.VMEM), out_shape),
        scratch_shapes=list(scratch),
        compiler_params=pltpu.CompilerParams(vmem_limit_bytes=VMEM_BYTES),
        cost_estimate=pl.CostEstimate(
            flops=int(HINTS[name] * FLOPS_PER_US), bytes_accessed=0, transcendentals=0
        ),
        name=name,
    )(*operands)


def encoded(peak, value, used):
    lane = lax.broadcasted_iota(jnp.int32, value.shape, value.ndim - 1)
    ratio = value * (TOP_POWER / peak)
    square = ratio * ratio
    power = ratio * jnp.abs(ratio) * square * (square * square)
    return jnp.where(lane < used, power, peak).astype(jnp.bfloat16)


def decoded(message):
    power = message.astype(jnp.float32)
    peak = power[0:1, message.shape[1] - 1 : message.shape[1]]
    size = jnp.maximum(jnp.abs(power), LEAST_POWER)
    fourth = lax.rsqrt(lax.rsqrt(size))
    root = fourth * lax.rsqrt(fourth)
    return jnp.where(power < 0, -root, root) * (peak * (1.0 / TOP_POWER))


def peak_of(value):
    largest = jnp.max(jnp.abs(value))
    largest = jnp.maximum(largest * (1.0 + 2.0**-6), LEAST_PEAK)
    return jnp.full((1, 1), largest, jnp.float32).astype(jnp.bfloat16).astype(jnp.float32)


class Plan:
    def __init__(self, images, channels, rows, width, bands, strips):
        self.images, self.channels, self.rows, self.width = images, channels, rows, width
        self.bands, self.strips = bands, strips
        self.sizes = (bands, strips)
        self.depth = channels // bands
        self.cols = channels // strips
        self.blocks = bands // 2
        self.half = channels // 2
        self.strip_bits = strips.bit_length() - 1
        self.band_bits = bands.bit_length() - 1
        assert bands == 1 << self.band_bits and strips == 1 << self.strip_bits
        assert self.band_bits >= 3 and self.strip_bits >= 1
        self.top_strip = 1 << (self.strip_bits - 1)
        self.rest_strip = [1 << k for k in reversed(range(self.strip_bits - 1))]
        self.rest_band = [1 << k for k in range(3, self.band_bits)]
        self.inner = self.blocks // 4
        self.half_used = len(TAP_STEPS) * self.half
        self.half_lanes = padded_lanes(self.half_used)
        self.used = len(TAP_STEPS) * self.cols
        self.lanes = padded_lanes(self.used)
        self.block_rows = len(TAP_STEPS) * self.depth
        self.part_rows = self.inner * self.block_rows
        self.cells = 2 * images * rows * width
        by_row, by_next, by_col = (2, 0), (4, 0), (0, self.top_strip)
        self.term_masks = ((by_col, by_next), (by_row, by_col), (by_next, by_row))
        self.gather_masks = ((by_row, by_row), (by_col, by_next), (by_next, by_col))

    def block_of(self, slot, by_next, by_row):
        bits = self.band_bits - 3
        turned = sum(((slot >> k) & 1) << (bits - 1 - k) for k in range(bits))
        return turned * 4 + by_next * 2 + by_row

    def chunks(self):
        return [(d, n, h) for d in range(2) for n in range(self.images) for h in range(self.rows)]


def place(plan):
    band, strip = lax.axis_index("band"), lax.axis_index("strip")
    return band % 2, (band // 2) % 2, (band // 4) % 2, strip // plan.top_strip


def mine(plan):
    core, by_row, by_next, by_col = place(plan)
    order = ((by_col, by_row, by_next), (by_next, by_col, by_row))
    return [jnp.where(core == 0, a, b) for a, b in zip(*order)]


def grad_row(plan, grad_ref, top_ref, bottom_ref, image, row, start, strip):
    if row < 0:
        piece = top_ref[image, pl.ds(start, plan.half), :]
        return jnp.where(strip > 0, piece, jnp.zeros_like(piece))
    if row >= plan.rows:
        piece = bottom_ref[image, pl.ds(start, plan.half), :]
        return jnp.where(strip < plan.strips - 1, piece, jnp.zeros_like(piece))
    return grad_ref[image, row, pl.ds(start, plan.half), :]


def moved(value, step):
    width = value.shape[-1]
    if step == 0:
        return value
    lane = lax.broadcasted_iota(jnp.int32, value.shape, value.ndim - 1)
    turned = pltpu.roll(value, (-step) % width, value.ndim - 1)
    inside = lane < width - step if step > 0 else lane >= -step
    return jnp.where(inside, turned, 0.0)


def acts_kernel(plan, act0, act1, out):
    core = lax.axis_index("band") % 2
    depth, width = plan.depth, plan.width
    for at, (d, n, h) in enumerate(plan.chunks()):
        cells = (act0, act1)[d][n, h].astype(jnp.float32)
        shifted = []
        for m in range(plan.blocks):
            begin = 2 * m * depth
            even, odd = cells[begin : begin + depth], cells[begin + depth : begin + 2 * depth]
            block = jnp.where(core == 0, even, odd)
            shifted.append([moved(block, step) for step in TAP_STEPS])
        for i in range(2):
            pieces = []
            for j in range(2):
                for slot in range(plan.inner):
                    here, there = shifted[plan.block_of(slot, j, i)], shifted[plan.block_of(slot, i, j)]
                    pieces += here if i == j else [jnp.where(core == 0, a, b) for a, b in zip(here, there)]
            out[i, :, at * width : (at + 1) * width] = jnp.concatenate(pieces, axis=0).astype(jnp.bfloat16)


def grads_kernel(plan, grad0, grad1, top0, top1, bottom0, bottom1, out):
    strip = lax.axis_index("strip")
    half, width = plan.half, plan.width
    sources = ((grad0, top0, bottom0), (grad1, top1, bottom1))
    for at, (d, n, h) in enumerate(plan.chunks()):
        cells = slice(at * width, (at + 1) * width)
        for x in range(2):
            for r, row_step in enumerate(TAP_STEPS):
                out[x, r * half : (r + 1) * half, cells] = grad_row(
                    plan, *sources[d], n, h - row_step, x * half, strip
                )
            out[x, plan.half_used :, cells] = jnp.zeros((plan.half_lanes - plan.half_used, width), jnp.bfloat16)


def pair_terms(plan, acts, grads, first, second):
    core = lax.axis_index("band") % 2
    i, x = jnp.where(core == 0, second, first), jnp.where(core == 0, first, second)
    return lax.dot_general(acts[i], grads[x], (((1,), (1,)), ((), ())), preferred_element_type=jnp.float32)


def send_kernel(plan, same, acts, grads, out):
    first, second, _ = mine(plan)
    total = pair_terms(plan, acts, grads, 1 - first, second if same else 1 - second)
    for k in range(2):
        half = total[k * plan.part_rows : (k + 1) * plan.part_rows]
        out[k] = encoded(peak_of(half), half, plan.half_used)


def keep_kernel(plan, same, acts, grads, out):
    first, second, _ = mine(plan)
    total = pair_terms(plan, acts, grads, first, second if same else 1 - second)
    for k in range(2):
        out[k] = total[k * plan.part_rows : (k + 1) * plan.part_rows]


def turn_kernel(plan, same, keep, message, out):
    for k in range(2):
        total = keep[k] + decoded(message[k])
        out[k] = total if same else encoded(peak_of(total), total, plan.half_used)


def part_kernel(plan, same, keep, message, out):
    third = mine(plan)[2]
    k = third if same else 1 - third
    total = keep[k] + decoded(message[k])
    out[...] = total if same else encoded(peak_of(total), total, plan.half_used)


def halve_kernel(plan, mask, used, same, keep, message, out):
    side = (lax.axis_index("band") // mask) % 2
    total = keep[...] + decoded(message[...])
    rows = total.shape[0] // 2
    lower, upper = total[:rows], total[rows:]
    if same:
        out[...] = jnp.where(side == 0, lower, upper)
    else:
        given = jnp.where(side == 0, upper, lower)
        out[...] = encoded(peak_of(given), given, used)


def last_kernel(plan, scale, keep, message, out):
    total = (keep[...] + decoded(message[...])) * scale
    depth, cols = plan.depth, plan.cols
    for r in range(len(TAP_STEPS)):
        for c in range(len(TAP_STEPS)):
            out[r * len(TAP_STEPS) + c] = total[c * depth : (c + 1) * depth, r * cols : (r + 1) * cols]


def pack_kernel(plan, kernel, out):
    rows = []
    for c in range(len(TAP_STEPS)):
        pieces = [kernel[r * len(TAP_STEPS) + c].astype(jnp.float32) for r in range(len(TAP_STEPS))]
        pieces.append(jnp.zeros((plan.depth, plan.lanes - plan.used), jnp.float32))
        rows.append(jnp.concatenate(pieces, axis=1))
    out[...] = jnp.concatenate(rows, axis=0).astype(jnp.bfloat16)


def cells_of(plan, d, left, grads, out):
    width, half = plan.width, plan.half
    rows = [(n, h) for n in range(plan.images) for h in range(plan.rows)]
    for begin in range(0, len(rows), 2):
        part = rows[begin : begin + 2]
        at = (d * len(rows) + begin) * width
        product = jnp.dot(
            left[...], grads[:, at : at + len(part) * width], preferred_element_type=jnp.float32
        )
        for k, (n, h) in enumerate(part):
            total = None
            for c, col_step in enumerate(TAP_STEPS):
                term = moved(product[c * half : (c + 1) * half, k * width : (k + 1) * width], -col_step)
                total = term if total is None else total + term
            out[n, h] = total.astype(jnp.bfloat16)


def given_kernel(plan, own, other, grads, out, left):
    core, row_bit, next_bit, col_bit = place(plan)
    rest = lax.axis_index("band") // 8
    depth, half, lanes = plan.depth, plan.half, plan.half_lanes
    for x in range(2):
        rows = [[] for _ in TAP_STEPS]
        for m in range(plan.blocks):
            row, behind, col = (m % 2) ^ row_bit, (m // 2 % 2) ^ next_bit, x ^ col_bit
            two = jnp.where(core == 0, col, behind)
            three = jnp.where(core == 0, behind, col)
            slot = two * 2 + row
            pair = jnp.where(three == 0, own[slot], other[slot]).astype(jnp.float32)
            block = pair[: plan.block_rows]
            for k in range(1, plan.inner):
                at = pair[k * plan.block_rows : (k + 1) * plan.block_rows]
                block = jnp.where(((m // 4) ^ rest) == k, at, block)
            for c in range(len(TAP_STEPS)):
                rows[c].append(block[c * depth : (c + 1) * depth])
        for c in range(len(TAP_STEPS)):
            left[c * half : (c + 1) * half, x * lanes : (x + 1) * lanes] = jnp.concatenate(
                rows[c], axis=0
            ).astype(jnp.bfloat16)
    cells_of(plan, 1, left, grads, out)


def own_kernel(plan, left, grads, out):
    cells_of(plan, 0, left, grads, out)


def weave_kernel(plan, own, theirs, out):
    core = lax.axis_index("band") % 2
    depth = plan.depth
    for n in range(plan.images):
        for h in range(plan.rows):
            a, b = own[n, h].astype(jnp.float32), theirs[n, h].astype(jnp.float32)
            even, odd = jnp.where(core == 0, a, b), jnp.where(core == 0, b, a)
            pieces = []
            for m in range(plan.blocks):
                pieces += [even[m * depth : (m + 1) * depth], odd[m * depth : (m + 1) * depth]]
            out[n, h] = jnp.concatenate(pieces, axis=0).astype(jnp.bfloat16)


def after(value, *others):
    return lax.optimization_barrier((value, *others))[0]


def pair_kernel(plan, *refs):
    blocks = [ref[k].astype(jnp.float32) for ref in refs[:-1] for k in range(ref.shape[0])]
    refs[-1][0] = jnp.concatenate(blocks, axis=0).astype(jnp.bfloat16)


def first_kernel(plan, kernel):
    shape = jax.ShapeDtypeStruct((plan.block_rows, plan.lanes), jnp.bfloat16)
    packed = call("pack", functools.partial(pack_kernel, plan), shape, [kernel])[None]
    for mask in plan.rest_band[:0:-1]:
        packed = jnp.concatenate([packed, swap(packed, plan.sizes, (mask, 0))], axis=0)
    return [packed] + [swap(packed, plan.sizes, (mask, 0)) for mask in plan.rest_band[:1]]


def whole_kernel(plan, packed, starts):
    sizes = plan.sizes
    starts = list(starts)
    packed = [*packed[:-1], after(packed[-1], starts[0])]
    if plan.rest_strip:
        packed = jnp.concatenate(packed, axis=0)[None]
        for mask in reversed(plan.rest_strip):
            packed = jnp.concatenate([packed, swap(packed, sizes, (0, mask))], axis=0)
        count = packed.shape[0]
        order = jnp.arange(count) ^ (lax.axis_index("strip") % count)
        packed = jnp.take(packed, order, axis=0)[..., : plan.used]
        packed = packed.reshape(count, plan.inner, plan.block_rows, len(TAP_STEPS), plan.cols)
        packed = packed.transpose(1, 2, 3, 0, 4).reshape(plan.inner, plan.block_rows, plan.half_used)
        packed = [jnp.pad(packed, ((0, 0), (0, 0), (0, plan.half_lanes - plan.half_used)))]
    shape = jax.ShapeDtypeStruct((1, plan.part_rows, plan.half_lanes), jnp.bfloat16)
    packed = call("pair", functools.partial(pair_kernel, plan), shape, packed)
    packed = after(packed, starts.pop(0))
    for masks in plan.gather_masks[:-1]:
        come = after(swap(packed, sizes, *masks), starts[0])
        packed = after(jnp.concatenate([packed, come], axis=0), starts.pop(0))
    return packed, swap(packed, sizes, *plan.gather_masks[-1])


def narrowed(plan, total):
    rows = total.shape[0]
    total = total[:, : plan.half_used].reshape(rows, len(TAP_STEPS), plan.half)
    for mask in plan.rest_strip:
        side = (lax.axis_index("strip") // mask) % 2
        parts = total.reshape(rows, len(TAP_STEPS), 2, total.shape[2] // 2)
        kept = jnp.where(side == 0, parts[:, :, 0], parts[:, :, 1])
        given = jnp.where(side == 0, parts[:, :, 1], parts[:, :, 0])
        total = kept + swap(given, plan.sizes, (0, mask))
    total = total.reshape(rows, plan.used)
    return jnp.pad(total, ((0, 0), (0, plan.lanes - plan.used)))


def kernel_terms(plan, acts, grads, scale):
    sizes, f32 = plan.sizes, jnp.float32
    rows, lanes = plan.part_rows, plan.half_lanes

    def run(name, kernel, shape, kind, operands):
        return call(name, kernel, jax.ShapeDtypeStruct(shape, kind), operands)

    part = functools.partial
    b16 = jnp.bfloat16
    shape = (2, rows, lanes)
    send0 = run("send0", part(send_kernel, plan, False), shape, b16, [acts, grads])
    come0 = swap(send0, sizes, *plan.term_masks[0])
    keep0 = run("keep0", part(keep_kernel, plan, False), shape, f32, [after(acts, send0), grads])
    send1 = run("send1", part(send_kernel, plan, True), shape, b16, [after(acts, keep0), grads])
    come1 = swap(send1, sizes, *plan.term_masks[0])
    send = run("turn0", part(turn_kernel, plan, False), shape, b16, [keep0, come0])
    come = swap(send, sizes, *plan.term_masks[1])
    keep1 = run("keep1", part(keep_kernel, plan, True), shape, f32, [after(acts, send), grads])
    keep = run("turn1", part(turn_kernel, plan, True), shape, f32, [keep1, come1])
    steps = {"send0": send0, "send1": send1, "keep0": keep0, "turn0": send, "keep1": keep1, "turn1": keep}
    shape = shape[1:]
    send = run("part0", part(part_kernel, plan, False), shape, b16, [keep, come])
    keep = run("part1", part(part_kernel, plan, True), shape, f32, [after(keep, send), come])
    steps.update(part0=send, part1=keep)
    come = swap(send, sizes, *plan.term_masks[2])
    if plan.rest_strip:
        keep = narrowed(plan, keep + decoded(come))
        come = jnp.zeros(keep.shape, b16)
    for mask in plan.rest_band:
        rows //= 2
        shape = (rows, plan.lanes)
        halve = part(halve_kernel, plan, mask, plan.used)
        send = run("halve0", part(halve, False), shape, b16, [keep, come])
        keep = run("halve1", part(halve, True), shape, f32, [after(keep, send), come])
        steps.update(halve0=send, halve1=keep)
        come = swap(send, sizes, (mask, 0))
    total = call(
        "last",
        part(last_kernel, plan, scale),
        jax.ShapeDtypeStruct((len(TAP_STEPS) ** 2, plan.depth, plan.cols), f32),
        [keep, come],
    )
    return total, steps


def edge_kernel(plan, grad, out, copy):
    strip = lax.axis_index("strip")
    for n in range(plan.images):
        out[n] = jnp.where(strip == 0, grad[n, plan.rows - 1], grad[n, 0])
    copy[...] = grad[...]


def borders(plan, grad):
    if plan.strips == 2:
        shape = jax.ShapeDtypeStruct((plan.images, plan.channels, plan.width), grad.dtype)
        copy = jax.ShapeDtypeStruct(grad.shape, grad.dtype)
        edge, grad = call("edge", functools.partial(edge_kernel, plan), (shape, copy), [grad])
        come = [swap(edge, plan.sizes, (core, 1)) for core in range(2)]
        return grad, come, come
    first, last = grad[:, 0], grad[:, plan.rows - 1]
    tops, bottoms = [], []
    for core in range(2):
        down = []
        for b in range(plan.bands):
            down += [(b * plan.strips + s, (b ^ core) * plan.strips + s + 1) for s in range(plan.strips - 1)]
        tops.append(lax.ppermute(last, AXES, down))
        bottoms.append(lax.ppermute(first, AXES, [(b, a) for a, b in down]))
    return grad, tops, bottoms


def body(activations, out_grad, kernel):
    images, channels, rows, width = activations.shape
    bands, strips = lax.axis_size("band"), lax.axis_size("strip")
    plan = Plan(images, channels, rows, width, bands, strips)
    scale = 1.0 / math.sqrt(images * bands * rows * strips * width)
    act = activations.transpose(0, 2, 1, 3)
    grad = out_grad.transpose(0, 2, 1, 3)
    grad0, tops, bottoms = borders(plan, grad)
    act1 = swap(act, plan.sizes, (1, 0))
    grad1 = swap(grad, plan.sizes, (1, 0))
    packed = first_kernel(plan, kernel.transpose(1, 0, 2))
    shape = (2, 2 * plan.part_rows, plan.cells)
    acts = call("acts", functools.partial(acts_kernel, plan), jax.ShapeDtypeStruct(shape, act.dtype), [act, act1])
    shape = (2, plan.half_lanes, plan.cells)
    grads = call(
        "grads",
        functools.partial(grads_kernel, plan),
        jax.ShapeDtypeStruct(shape, grad.dtype),
        [grad0, grad1, *tops, *bottoms],
    )
    kernel_grad, steps = kernel_terms(plan, acts, grads, scale)
    packed = whole_kernel(plan, packed, [steps[name] for name in GATHER_STEPS])
    shape = jax.ShapeDtypeStruct((images, rows, plan.half, width), jnp.bfloat16)
    left = jax.ShapeDtypeStruct((len(TAP_STEPS) * plan.half, 2 * plan.half_lanes), jnp.bfloat16)
    grads = grads.reshape(2 * plan.half_lanes, plan.cells)
    given, left = call(
        "given",
        functools.partial(given_kernel, plan),
        (shape, left),
        [after(packed[0], steps[CELLS_STEP]), packed[1], grads],
    )
    own = call("own", functools.partial(own_kernel, plan), shape, [after(left, given), grads])
    theirs = swap(given, plan.sizes, (1, 0))
    input_grad = call(
        "weave",
        functools.partial(weave_kernel, plan),
        jax.ShapeDtypeStruct((images, rows, channels, width), jnp.bfloat16),
        [own, theirs],
    )
    return input_grad.transpose(0, 2, 1, 3), kernel_grad.transpose(1, 0, 2)


def solution(mesh):
    in_specs = (
        P("band", None, "strip", None),
        P("band", None, "strip", None),
        P("band", None, "strip"),
    )
    out_specs = (P("band", None, "strip", None), P("band", None, "strip"))
    return jax.shard_map(body, mesh=mesh, in_specs=in_specs, out_specs=out_specs, check_vma=False)
```

```python
import functools
import math

import jax
import jax.numpy as jnp
from jax import lax
from jax.experimental import pallas as pl
from jax.experimental.pallas import tpu as pltpu
from jax.sharding import PartitionSpec as P

AXES = ("band", "strip")
TAP_STEPS = (-1, 0, 1)
LANES = 128
TOP_POWER = 2.0**15.5
LEAST_POWER = 2.0**-126
LEAST_PEAK = 1e-30
VMEM_BYTES = 40 * 2**20
HINTS = {
    "edge": 8.0,
    "pair": 0.2,
    "pack": 8.0,
    "acts": 0.6,
    "grads": 0.5,
    "send0": 1.4,
    "send1": 1.4,
    "keep0": 1.0,
    "keep1": 1.0,
    "turn0": 0.9,
    "turn1": 0.6,
    "part0": 0.5,
    "part1": 0.3,
    "halve0": 0.5,
    "halve1": 3.0,
    "last": 8.0,
    "given": 1.2,
    "own": 0.7,
    "weave": 0.9,
}
GATHER_STEPS = ("keep0", "turn0", "part0")
CELLS_STEP = "halve1"
FLOPS_PER_US = 1.15e9


def padded_lanes(count):
    return (count // LANES + 1) * LANES


def swap(value, sizes, *masks):
    bands, strips = sizes
    pairs = []
    for b in range(bands):
        for s in range(strips):
            masks_here = masks[b % len(masks)]
            pairs.append((b * strips + s, (b ^ masks_here[0]) * strips + (s ^ masks_here[1])))
    return lax.ppermute(value, AXES, pairs)


def call(name, kernel, out_shape, operands, scratch=()):
    return pl.pallas_call(
        kernel,
        out_shape=out_shape,
        in_specs=[pl.BlockSpec(memory_space=pltpu.VMEM)] * len(operands),
        out_specs=jax.tree.map(lambda _: pl.BlockSpec(memory_space=pltpu.VMEM), out_shape),
        scratch_shapes=list(scratch),
        compiler_params=pltpu.CompilerParams(vmem_limit_bytes=VMEM_BYTES),
        cost_estimate=pl.CostEstimate(
            flops=int(HINTS[name] * FLOPS_PER_US), bytes_accessed=0, transcendentals=0
        ),
        name=name,
    )(*operands)


def encoded(peak, value, used):
    lane = lax.broadcasted_iota(jnp.int32, value.shape, value.ndim - 1)
    ratio = value * (TOP_POWER / peak)
    square = ratio * ratio
    power = ratio * jnp.abs(ratio) * square * (square * square)
    return jnp.where(lane < used, power, peak).astype(jnp.bfloat16)


def decoded(message):
    power = message.astype(jnp.float32)
    peak = power[0:1, message.shape[1] - 1 : message.shape[1]]
    size = jnp.maximum(jnp.abs(power), LEAST_POWER)
    fourth = lax.rsqrt(lax.rsqrt(size))
    root = fourth * lax.rsqrt(fourth)
    return jnp.where(power < 0, -root, root) * (peak * (1.0 / TOP_POWER))


def peak_of(value):
    largest = jnp.max(jnp.abs(value))
    largest = jnp.maximum(largest * (1.0 + 2.0**-6), LEAST_PEAK)
    return jnp.full((1, 1), largest, jnp.float32).astype(jnp.bfloat16).astype(jnp.float32)


class Plan:
    def __init__(self, images, channels, rows, width, bands, strips):
        self.images, self.channels, self.rows, self.width = images, channels, rows, width
        self.bands, self.strips = bands, strips
        self.sizes = (bands, strips)
        self.depth = channels // bands
        self.cols = channels // strips
        self.blocks = bands // 2
        self.half = channels // 2
        self.strip_bits = strips.bit_length() - 1
        self.band_bits = bands.bit_length() - 1
        assert bands == 1 << self.band_bits and strips == 1 << self.strip_bits
        assert self.band_bits >= 3 and self.strip_bits >= 1
        self.top_strip = 1 << (self.strip_bits - 1)
        self.rest_strip = [1 << k for k in reversed(range(self.strip_bits - 1))]
        self.rest_band = [1 << k for k in range(3, self.band_bits)]
        self.inner = self.blocks // 4
        self.half_used = len(TAP_STEPS) * self.half
        self.half_lanes = padded_lanes(self.half_used)
        self.used = len(TAP_STEPS) * self.cols
        self.lanes = padded_lanes(self.used)
        self.block_rows = len(TAP_STEPS) * self.depth
        self.part_rows = self.inner * self.block_rows
        self.cells = 2 * images * rows * width
        by_row, by_next, by_col = (2, 0), (4, 0), (0, self.top_strip)
        self.term_masks = ((by_col, by_next), (by_row, by_col), (by_next, by_row))
        self.gather_masks = ((by_row, by_next), (by_next, by_col), (by_col, by_row))

    def block_of(self, slot, by_next, by_row):
        bits = self.band_bits - 3
        turned = sum(((slot >> k) & 1) << (bits - 1 - k) for k in range(bits))
        return turned * 4 + by_next * 2 + by_row

    def chunks(self):
        return [(d, n, h) for d in range(2) for n in range(self.images) for h in range(self.rows)]


def place(plan):
    band, strip = lax.axis_index("band"), lax.axis_index("strip")
    return band % 2, (band // 2) % 2, (band // 4) % 2, strip // plan.top_strip


def mine(plan):
    core, by_row, by_next, by_col = place(plan)
    order = ((by_col, by_row, by_next), (by_next, by_col, by_row))
    return [jnp.where(core == 0, a, b) for a, b in zip(*order)]


def grad_row(plan, grad_ref, top_ref, bottom_ref, image, row, start, strip):
    if row < 0:
        piece = top_ref[image, pl.ds(start, plan.half), :]
        return jnp.where(strip > 0, piece, jnp.zeros_like(piece))
    if row >= plan.rows:
        piece = bottom_ref[image, pl.ds(start, plan.half), :]
        return jnp.where(strip < plan.strips - 1, piece, jnp.zeros_like(piece))
    return grad_ref[image, row, pl.ds(start, plan.half), :]


def moved(value, step):
    width = value.shape[-1]
    if step == 0:
        return value
    lane = lax.broadcasted_iota(jnp.int32, value.shape, value.ndim - 1)
    turned = pltpu.roll(value, (-step) % width, value.ndim - 1)
    inside = lane < width - step if step > 0 else lane >= -step
    return jnp.where(inside, turned, 0.0)


def acts_kernel(plan, act0, act1, out):
    core = lax.axis_index("band") % 2
    depth, width = plan.depth, plan.width
    for at, (d, n, h) in enumerate(plan.chunks()):
        cells = (act0, act1)[d][n, h].astype(jnp.float32)
        shifted = []
        for m in range(plan.blocks):
            begin = 2 * m * depth
            even, odd = cells[begin : begin + depth], cells[begin + depth : begin + 2 * depth]
            block = jnp.where(core == 0, even, odd)
            shifted.append([moved(block, step) for step in TAP_STEPS])
        for i in range(2):
            pieces = []
            for j in range(2):
                for slot in range(plan.inner):
                    here, there = shifted[plan.block_of(slot, j, i)], shifted[plan.block_of(slot, i, j)]
                    pieces += here if i == j else [jnp.where(core == 0, a, b) for a, b in zip(here, there)]
            out[i, :, at * width : (at + 1) * width] = jnp.concatenate(pieces, axis=0).astype(jnp.bfloat16)


def grads_kernel(plan, grad0, grad1, top0, top1, bottom0, bottom1, out):
    strip = lax.axis_index("strip")
    half, width = plan.half, plan.width
    sources = ((grad0, top0, bottom0), (grad1, top1, bottom1))
    for at, (d, n, h) in enumerate(plan.chunks()):
        cells = slice(at * width, (at + 1) * width)
        for x in range(2):
            for r, row_step in enumerate(TAP_STEPS):
                out[x, r * half : (r + 1) * half, cells] = grad_row(
                    plan, *sources[d], n, h - row_step, x * half, strip
                )
            out[x, plan.half_used :, cells] = jnp.zeros((plan.half_lanes - plan.half_used, width), jnp.bfloat16)


def pair_terms(plan, acts, grads, first, second):
    core = lax.axis_index("band") % 2
    i, x = jnp.where(core == 0, second, first), jnp.where(core == 0, first, second)
    return lax.dot_general(acts[i], grads[x], (((1,), (1,)), ((), ())), preferred_element_type=jnp.float32)


def send_kernel(plan, same, acts, grads, out):
    first, second, _ = mine(plan)
    total = pair_terms(plan, acts, grads, 1 - first, second if same else 1 - second)
    for k in range(2):
        half = total[k * plan.part_rows : (k + 1) * plan.part_rows]
        out[k] = encoded(peak_of(half), half, plan.half_used)


def keep_kernel(plan, same, acts, grads, out):
    first, second, _ = mine(plan)
    total = pair_terms(plan, acts, grads, first, second if same else 1 - second)
    for k in range(2):
        out[k] = total[k * plan.part_rows : (k + 1) * plan.part_rows]


def turn_kernel(plan, same, keep, message, out):
    for k in range(2):
        total = keep[k] + decoded(message[k])
        out[k] = total if same else encoded(peak_of(total), total, plan.half_used)


def part_kernel(plan, same, keep, message, out):
    third = mine(plan)[2]
    k = third if same else 1 - third
    total = keep[k] + decoded(message[k])
    out[...] = total if same else encoded(peak_of(total), total, plan.half_used)


def halve_kernel(plan, mask, used, same, keep, message, out):
    side = (lax.axis_index("band") // mask) % 2
    total = keep[...] + decoded(message[...])
    rows = total.shape[0] // 2
    lower, upper = total[:rows], total[rows:]
    if same:
        out[...] = jnp.where(side == 0, lower, upper)
    else:
        given = jnp.where(side == 0, upper, lower)
        out[...] = encoded(peak_of(given), given, used)


def last_kernel(plan, scale, keep, message, out):
    total = (keep[...] + decoded(message[...])) * scale
    depth, cols = plan.depth, plan.cols
    for r in range(len(TAP_STEPS)):
        for c in range(len(TAP_STEPS)):
            out[r * len(TAP_STEPS) + c] = total[c * depth : (c + 1) * depth, r * cols : (r + 1) * cols]


def pack_kernel(plan, kernel, out):
    rows = []
    for c in range(len(TAP_STEPS)):
        pieces = [kernel[r * len(TAP_STEPS) + c].astype(jnp.float32) for r in range(len(TAP_STEPS))]
        pieces.append(jnp.zeros((plan.depth, plan.lanes - plan.used), jnp.float32))
        rows.append(jnp.concatenate(pieces, axis=1))
    out[...] = jnp.concatenate(rows, axis=0).astype(jnp.bfloat16)


def cells_of(plan, d, left, grads, out):
    width, half = plan.width, plan.half
    rows = [(n, h) for n in range(plan.images) for h in range(plan.rows)]
    for begin in range(0, len(rows), 2):
        part = rows[begin : begin + 2]
        at = (d * len(rows) + begin) * width
        product = jnp.dot(
            left[...], grads[:, at : at + len(part) * width], preferred_element_type=jnp.float32
        )
        for k, (n, h) in enumerate(part):
            total = None
            for c, col_step in enumerate(TAP_STEPS):
                term = moved(product[c * half : (c + 1) * half, k * width : (k + 1) * width], -col_step)
                total = term if total is None else total + term
            out[n, h] = total.astype(jnp.bfloat16)


def given_kernel(plan, own, other, grads, out, left):
    core, row_bit, next_bit, col_bit = place(plan)
    rest = lax.axis_index("band") // 8
    depth, half, lanes = plan.depth, plan.half, plan.half_lanes
    for x in range(2):
        rows = [[] for _ in TAP_STEPS]
        for m in range(plan.blocks):
            row, behind, col = (m % 2) ^ row_bit, (m // 2 % 2) ^ next_bit, x ^ col_bit
            one = jnp.where(core == 0, row, behind)
            two = jnp.where(core == 0, behind, col)
            three = jnp.where(core == 0, col, row)
            slot = two * 2 + one
            pair = jnp.where(three == 0, own[slot], other[slot]).astype(jnp.float32)
            block = pair[: plan.block_rows]
            for k in range(1, plan.inner):
                at = pair[k * plan.block_rows : (k + 1) * plan.block_rows]
                block = jnp.where(((m // 4) ^ rest) == k, at, block)
            for c in range(len(TAP_STEPS)):
                rows[c].append(block[c * depth : (c + 1) * depth])
        for c in range(len(TAP_STEPS)):
            left[c * half : (c + 1) * half, x * lanes : (x + 1) * lanes] = jnp.concatenate(
                rows[c], axis=0
            ).astype(jnp.bfloat16)
    cells_of(plan, 1, left, grads, out)


def own_kernel(plan, left, grads, out):
    cells_of(plan, 0, left, grads, out)


def weave_kernel(plan, own, theirs, out):
    core = lax.axis_index("band") % 2
    depth = plan.depth
    for n in range(plan.images):
        for h in range(plan.rows):
            a, b = own[n, h].astype(jnp.float32), theirs[n, h].astype(jnp.float32)
            even, odd = jnp.where(core == 0, a, b), jnp.where(core == 0, b, a)
            pieces = []
            for m in range(plan.blocks):
                pieces += [even[m * depth : (m + 1) * depth], odd[m * depth : (m + 1) * depth]]
            out[n, h] = jnp.concatenate(pieces, axis=0).astype(jnp.bfloat16)


def after(value, *others):
    return lax.optimization_barrier((value, *others))[0]


def pair_kernel(plan, *refs):
    blocks = [ref[k].astype(jnp.float32) for ref in refs[:-1] for k in range(ref.shape[0])]
    refs[-1][0] = jnp.concatenate(blocks, axis=0).astype(jnp.bfloat16)


def first_kernel(plan, kernel):
    shape = jax.ShapeDtypeStruct((plan.block_rows, plan.lanes), jnp.bfloat16)
    packed = call("pack", functools.partial(pack_kernel, plan), shape, [kernel])[None]
    for mask in plan.rest_band[:0:-1]:
        packed = jnp.concatenate([packed, swap(packed, plan.sizes, (mask, 0))], axis=0)
    return [packed] + [swap(packed, plan.sizes, (mask, 0)) for mask in plan.rest_band[:1]]


def whole_kernel(plan, packed, starts):
    sizes = plan.sizes
    starts = list(starts)
    packed = [*packed[:-1], after(packed[-1], starts[0])]
    if plan.rest_strip:
        packed = jnp.concatenate(packed, axis=0)[None]
        for mask in reversed(plan.rest_strip):
            packed = jnp.concatenate([packed, swap(packed, sizes, (0, mask))], axis=0)
        count = packed.shape[0]
        order = jnp.arange(count) ^ (lax.axis_index("strip") % count)
        packed = jnp.take(packed, order, axis=0)[..., : plan.used]
        packed = packed.reshape(count, plan.inner, plan.block_rows, len(TAP_STEPS), plan.cols)
        packed = packed.transpose(1, 2, 3, 0, 4).reshape(plan.inner, plan.block_rows, plan.half_used)
        packed = [jnp.pad(packed, ((0, 0), (0, 0), (0, plan.half_lanes - plan.half_used)))]
    shape = jax.ShapeDtypeStruct((1, plan.part_rows, plan.half_lanes), jnp.bfloat16)
    packed = call("pair", functools.partial(pair_kernel, plan), shape, packed)
    packed = after(packed, starts.pop(0))
    for masks in plan.gather_masks[:-1]:
        come = after(swap(packed, sizes, *masks), starts[0])
        packed = after(jnp.concatenate([packed, come], axis=0), starts.pop(0))
    return packed, swap(packed, sizes, *plan.gather_masks[-1])


def narrowed(plan, total):
    rows = total.shape[0]
    total = total[:, : plan.half_used].reshape(rows, len(TAP_STEPS), plan.half)
    for mask in plan.rest_strip:
        side = (lax.axis_index("strip") // mask) % 2
        parts = total.reshape(rows, len(TAP_STEPS), 2, total.shape[2] // 2)
        kept = jnp.where(side == 0, parts[:, :, 0], parts[:, :, 1])
        given = jnp.where(side == 0, parts[:, :, 1], parts[:, :, 0])
        total = kept + swap(given, plan.sizes, (0, mask))
    total = total.reshape(rows, plan.used)
    return jnp.pad(total, ((0, 0), (0, plan.lanes - plan.used)))


def kernel_terms(plan, acts, grads, scale):
    sizes, f32 = plan.sizes, jnp.float32
    rows, lanes = plan.part_rows, plan.half_lanes

    def run(name, kernel, shape, kind, operands):
        return call(name, kernel, jax.ShapeDtypeStruct(shape, kind), operands)

    part = functools.partial
    b16 = jnp.bfloat16
    shape = (2, rows, lanes)
    send0 = run("send0", part(send_kernel, plan, False), shape, b16, [acts, grads])
    come0 = swap(send0, sizes, *plan.term_masks[0])
    send1 = run("send1", part(send_kernel, plan, True), shape, b16, [after(acts, send0), grads])
    come1 = swap(send1, sizes, *plan.term_masks[0])
    keep0 = run("keep0", part(keep_kernel, plan, False), shape, f32, [after(acts, send1), grads])
    send = run("turn0", part(turn_kernel, plan, False), shape, b16, [keep0, come0])
    come = swap(send, sizes, *plan.term_masks[1])
    keep1 = run("keep1", part(keep_kernel, plan, True), shape, f32, [after(acts, send), grads])
    keep = run("turn1", part(turn_kernel, plan, True), shape, f32, [keep1, come1])
    steps = {"send0": send0, "send1": send1, "keep0": keep0, "turn0": send, "keep1": keep1, "turn1": keep}
    shape = shape[1:]
    send = run("part0", part(part_kernel, plan, False), shape, b16, [keep, come])
    keep = run("part1", part(part_kernel, plan, True), shape, f32, [after(keep, send), come])
    steps.update(part0=send, part1=keep)
    come = swap(send, sizes, *plan.term_masks[2])
    if plan.rest_strip:
        keep = narrowed(plan, keep + decoded(come))
        come = jnp.zeros(keep.shape, b16)
    for mask in plan.rest_band:
        rows //= 2
        shape = (rows, plan.lanes)
        halve = part(halve_kernel, plan, mask, plan.used)
        send = run("halve0", part(halve, False), shape, b16, [keep, come])
        keep = run("halve1", part(halve, True), shape, f32, [after(keep, send), come])
        steps.update(halve0=send, halve1=keep)
        come = swap(send, sizes, (mask, 0))
    total = call(
        "last",
        part(last_kernel, plan, scale),
        jax.ShapeDtypeStruct((len(TAP_STEPS) ** 2, plan.depth, plan.cols), f32),
        [keep, come],
    )
    return total, steps


def edge_kernel(plan, grad, out, copy):
    strip = lax.axis_index("strip")
    for n in range(plan.images):
        out[n] = jnp.where(strip == 0, grad[n, plan.rows - 1], grad[n, 0])
    copy[...] = grad[...]


def borders(plan, grad):
    if plan.strips == 2:
        shape = jax.ShapeDtypeStruct((plan.images, plan.channels, plan.width), grad.dtype)
        copy = jax.ShapeDtypeStruct(grad.shape, grad.dtype)
        edge, grad = call("edge", functools.partial(edge_kernel, plan), (shape, copy), [grad])
        come = [swap(edge, plan.sizes, (core, 1)) for core in range(2)]
        return grad, come, come
    first, last = grad[:, 0], grad[:, plan.rows - 1]
    tops, bottoms = [], []
    for core in range(2):
        down = []
        for b in range(plan.bands):
            down += [(b * plan.strips + s, (b ^ core) * plan.strips + s + 1) for s in range(plan.strips - 1)]
        tops.append(lax.ppermute(last, AXES, down))
        bottoms.append(lax.ppermute(first, AXES, [(b, a) for a, b in down]))
    return grad, tops, bottoms


def body(activations, out_grad, kernel):
    images, channels, rows, width = activations.shape
    bands, strips = lax.axis_size("band"), lax.axis_size("strip")
    plan = Plan(images, channels, rows, width, bands, strips)
    scale = 1.0 / math.sqrt(images * bands * rows * strips * width)
    act = activations.transpose(0, 2, 1, 3)
    grad = out_grad.transpose(0, 2, 1, 3)
    grad0, tops, bottoms = borders(plan, grad)
    act1 = swap(act, plan.sizes, (1, 0))
    grad1 = swap(grad, plan.sizes, (1, 0))
    packed = first_kernel(plan, kernel.transpose(1, 0, 2))
    shape = (2, 2 * plan.part_rows, plan.cells)
    acts = call("acts", functools.partial(acts_kernel, plan), jax.ShapeDtypeStruct(shape, act.dtype), [act, act1])
    shape = (2, plan.half_lanes, plan.cells)
    grads = call(
        "grads",
        functools.partial(grads_kernel, plan),
        jax.ShapeDtypeStruct(shape, grad.dtype),
        [grad0, grad1, *tops, *bottoms],
    )
    kernel_grad, steps = kernel_terms(plan, acts, grads, scale)
    packed = whole_kernel(plan, packed, [steps[name] for name in GATHER_STEPS])
    shape = jax.ShapeDtypeStruct((images, rows, plan.half, width), jnp.bfloat16)
    left = jax.ShapeDtypeStruct((len(TAP_STEPS) * plan.half, 2 * plan.half_lanes), jnp.bfloat16)
    grads = grads.reshape(2 * plan.half_lanes, plan.cells)
    given, left = call(
        "given",
        functools.partial(given_kernel, plan),
        (shape, left),
        [after(packed[0], steps[CELLS_STEP]), packed[1], grads],
    )
    own = call("own", functools.partial(own_kernel, plan), shape, [after(left, given), grads])
    theirs = swap(given, plan.sizes, (1, 0))
    input_grad = call(
        "weave",
        functools.partial(weave_kernel, plan),
        jax.ShapeDtypeStruct((images, rows, channels, width), jnp.bfloat16),
        [own, theirs],
    )
    return input_grad.transpose(0, 2, 1, 3), kernel_grad.transpose(1, 0, 2)


def solution(mesh):
    in_specs = (
        P("band", None, "strip", None),
        P("band", None, "strip", None),
        P("band", None, "strip"),
    )
    out_specs = (P("band", None, "strip", None), P("band", None, "strip"))
    return jax.shard_map(body, mesh=mesh, in_specs=in_specs, out_specs=out_specs, check_vma=False)
```

```python
import functools
import math

import jax
import jax.numpy as jnp
from jax import lax
from jax.experimental import pallas as pl
from jax.experimental.pallas import tpu as pltpu
from jax.sharding import PartitionSpec as P

AXES = ("band", "strip")
TAP_STEPS = (-1, 0, 1)
LANES = 128
TOP_POWER = 2.0**15.5
LEAST_POWER = 2.0**-126
LEAST_PEAK = 1e-30
VMEM_BYTES = 40 * 2**20
HINTS = {
    "edge": 8.0,
    "pair": 0.2,
    "pack": 8.0,
    "acts": 0.6,
    "grads": 0.5,
    "send0": 1.4,
    "send1": 1.4,
    "keep0": 1.0,
    "keep1": 1.0,
    "turn0": 0.9,
    "turn1": 0.6,
    "part0": 0.5,
    "part1": 0.3,
    "halve0": 0.5,
    "halve1": 3.0,
    "given": 1.2,
    "own": 8.0,
    "weave": 0.9,
}
GATHER_STEPS = ("keep0", "turn0", "part0")
CELLS_STEP = "halve1"
FLOPS_PER_US = 1.15e9


def padded_lanes(count):
    return (count // LANES + 1) * LANES


def swap(value, sizes, *masks):
    bands, strips = sizes
    pairs = []
    for b in range(bands):
        for s in range(strips):
            masks_here = masks[b % len(masks)]
            pairs.append((b * strips + s, (b ^ masks_here[0]) * strips + (s ^ masks_here[1])))
    return lax.ppermute(value, AXES, pairs)


def call(name, kernel, out_shape, operands, scratch=(), far=0):
    outs = jax.tree.map(lambda _: pl.BlockSpec(memory_space=pltpu.VMEM), out_shape)
    if far:
        outs = outs[:-far] + (pl.BlockSpec(memory_space=pl.ANY),) * far
    return pl.pallas_call(
        kernel,
        out_shape=out_shape,
        in_specs=[pl.BlockSpec(memory_space=pltpu.VMEM)] * len(operands),
        out_specs=outs,
        scratch_shapes=list(scratch),
        compiler_params=pltpu.CompilerParams(vmem_limit_bytes=VMEM_BYTES),
        cost_estimate=pl.CostEstimate(
            flops=int(HINTS[name] * FLOPS_PER_US), bytes_accessed=0, transcendentals=0
        ),
        name=name,
    )(*operands)


def encoded(peak, value, used):
    lane = lax.broadcasted_iota(jnp.int32, value.shape, value.ndim - 1)
    ratio = value * (TOP_POWER / peak)
    square = ratio * ratio
    power = ratio * jnp.abs(ratio) * square * (square * square)
    return jnp.where(lane < used, power, peak).astype(jnp.bfloat16)


def decoded(message):
    power = message.astype(jnp.float32)
    peak = power[0:1, message.shape[1] - 1 : message.shape[1]]
    size = jnp.maximum(jnp.abs(power), LEAST_POWER)
    fourth = lax.rsqrt(lax.rsqrt(size))
    root = fourth * lax.rsqrt(fourth)
    return jnp.where(power < 0, -root, root) * (peak * (1.0 / TOP_POWER)), peak


def rounded_up(peak):
    return jnp.maximum(peak * (1.0 + 2.0**-6), LEAST_PEAK).astype(jnp.bfloat16).astype(jnp.float32)


def largest(value):
    return jnp.full((1, 1), jnp.max(jnp.abs(value)), jnp.float32)


def noted(peak, value, used):
    lane = lax.broadcasted_iota(jnp.int32, value.shape, value.ndim - 1)
    return jnp.where(lane < used, value, peak)


def added(keep, message):
    value, peak = decoded(message)
    return keep + value, peak + keep[0:1, keep.shape[1] - 1 : keep.shape[1]]


class Plan:
    def __init__(self, images, channels, rows, width, bands, strips):
        self.images, self.channels, self.rows, self.width = images, channels, rows, width
        self.bands, self.strips = bands, strips
        self.sizes = (bands, strips)
        self.depth = channels // bands
        self.cols = channels // strips
        self.blocks = bands // 2
        self.half = channels // 2
        self.strip_bits = strips.bit_length() - 1
        self.band_bits = bands.bit_length() - 1
        assert bands == 1 << self.band_bits and strips == 1 << self.strip_bits
        assert self.band_bits >= 3 and self.strip_bits >= 1
        self.top_strip = 1 << (self.strip_bits - 1)
        self.rest_strip = [1 << k for k in reversed(range(self.strip_bits - 1))]
        self.rest_band = [1 << k for k in range(3, self.band_bits)]
        self.inner = self.blocks // 4
        self.half_used = len(TAP_STEPS) * self.half
        self.half_lanes = padded_lanes(self.half_used)
        self.used = len(TAP_STEPS) * self.cols
        self.lanes = padded_lanes(self.used)
        self.block_rows = len(TAP_STEPS) * self.depth
        self.part_rows = self.inner * self.block_rows
        self.cells = 2 * images * rows * width
        by_row, by_next, by_col = (2, 0), (4, 0), (0, self.top_strip)
        self.term_masks = ((by_col, by_next), (by_row, by_col), (by_next, by_row))
        self.gather_masks = ((by_row, by_next), (by_next, by_col), (by_col, by_row))

    def block_of(self, slot, by_next, by_row):
        bits = self.band_bits - 3
        turned = sum(((slot >> k) & 1) << (bits - 1 - k) for k in range(bits))
        return turned * 4 + by_next * 2 + by_row

    def chunks(self):
        return [(d, n, h) for d in range(2) for n in range(self.images) for h in range(self.rows)]


def place(plan):
    band, strip = lax.axis_index("band"), lax.axis_index("strip")
    return band % 2, (band // 2) % 2, (band // 4) % 2, strip // plan.top_strip


def mine(plan):
    core, by_row, by_next, by_col = place(plan)
    order = ((by_col, by_row, by_next), (by_next, by_col, by_row))
    return [jnp.where(core == 0, a, b) for a, b in zip(*order)]


def grad_row(plan, grad_ref, top_ref, bottom_ref, image, row, start, strip):
    if row < 0:
        piece = top_ref[image, pl.ds(start, plan.half), :]
        return jnp.where(strip > 0, piece, jnp.zeros_like(piece))
    if row >= plan.rows:
        piece = bottom_ref[image, pl.ds(start, plan.half), :]
        return jnp.where(strip < plan.strips - 1, piece, jnp.zeros_like(piece))
    return grad_ref[image, row, pl.ds(start, plan.half), :]


def moved(value, step):
    width = value.shape[-1]
    if step == 0:
        return value
    lane = lax.broadcasted_iota(jnp.int32, value.shape, value.ndim - 1)
    turned = pltpu.roll(value, (-step) % width, value.ndim - 1)
    inside = lane < width - step if step > 0 else lane >= -step
    return jnp.where(inside, turned, 0.0)


def acts_kernel(plan, act0, act1, out):
    core = lax.axis_index("band") % 2
    depth, width = plan.depth, plan.width
    for at, (d, n, h) in enumerate(plan.chunks()):
        cells = (act0, act1)[d][n, h].astype(jnp.float32)
        shifted = []
        for m in range(plan.blocks):
            begin = 2 * m * depth
            even, odd = cells[begin : begin + depth], cells[begin + depth : begin + 2 * depth]
            block = jnp.where(core == 0, even, odd)
            shifted.append([moved(block, step) for step in TAP_STEPS])
        for i in range(2):
            pieces = []
            for j in range(2):
                for slot in range(plan.inner):
                    here, there = shifted[plan.block_of(slot, j, i)], shifted[plan.block_of(slot, i, j)]
                    pieces += here if i == j else [jnp.where(core == 0, a, b) for a, b in zip(here, there)]
            out[i, :, at * width : (at + 1) * width] = jnp.concatenate(pieces, axis=0).astype(jnp.bfloat16)


def grads_kernel(plan, grad0, grad1, top0, top1, bottom0, bottom1, out):
    strip = lax.axis_index("strip")
    half, width = plan.half, plan.width
    sources = ((grad0, top0, bottom0), (grad1, top1, bottom1))
    for at, (d, n, h) in enumerate(plan.chunks()):
        cells = slice(at * width, (at + 1) * width)
        for x in range(2):
            for r, row_step in enumerate(TAP_STEPS):
                out[x, r * half : (r + 1) * half, cells] = grad_row(
                    plan, *sources[d], n, h - row_step, x * half, strip
                )
            out[x, plan.half_used :, cells] = jnp.zeros((plan.half_lanes - plan.half_used, width), jnp.bfloat16)


def pair_terms(plan, acts, grads, first, second):
    core = lax.axis_index("band") % 2
    i, x = jnp.where(core == 0, second, first), jnp.where(core == 0, first, second)
    return lax.dot_general(acts[i], grads[x], (((1,), (1,)), ((), ())), preferred_element_type=jnp.float32)


def send_kernel(plan, same, acts, grads, out):
    first, second, _ = mine(plan)
    total = pair_terms(plan, acts, grads, 1 - first, second if same else 1 - second)
    for k in range(2):
        half = total[k * plan.part_rows : (k + 1) * plan.part_rows]
        out[k] = encoded(rounded_up(largest(half)), half, plan.half_used)


def keep_kernel(plan, same, acts, grads, out):
    first, second, _ = mine(plan)
    total = pair_terms(plan, acts, grads, first, second if same else 1 - second)
    for k in range(2):
        half = total[k * plan.part_rows : (k + 1) * plan.part_rows]
        out[k] = noted(largest(half), half, plan.half_used)


def turn_kernel(plan, same, keep, message, out):
    for k in range(2):
        total, peak = added(keep[k], message[k])
        out[k] = noted(peak, total, plan.half_used) if same else encoded(rounded_up(peak), total, plan.half_used)


def part_kernel(plan, same, keep, message, out):
    third = mine(plan)[2]
    k = third if same else 1 - third
    total, peak = added(keep[k], message[k])
    out[...] = noted(peak, total, plan.half_used) if same else encoded(rounded_up(peak), total, plan.half_used)


def halve_kernel(plan, mask, used, same, keep, message, out):
    side = (lax.axis_index("band") // mask) % 2
    total, peak = added(keep[...], message[...])
    rows = total.shape[0] // 2
    lower, upper = total[:rows], total[rows:]
    if same:
        out[...] = noted(peak, jnp.where(side == 0, lower, upper), used)
    else:
        out[...] = encoded(rounded_up(peak), jnp.where(side == 0, upper, lower), used)


def pack_kernel(plan, kernel, out):
    rows = []
    for c in range(len(TAP_STEPS)):
        pieces = [kernel[r * len(TAP_STEPS) + c].astype(jnp.float32) for r in range(len(TAP_STEPS))]
        pieces.append(jnp.zeros((plan.depth, plan.lanes - plan.used), jnp.float32))
        rows.append(jnp.concatenate(pieces, axis=1))
    out[...] = jnp.concatenate(rows, axis=0).astype(jnp.bfloat16)


def cells_of(plan, d, left, grads, out):
    width, half = plan.width, plan.half
    rows = [(n, h) for n in range(plan.images) for h in range(plan.rows)]
    for begin in range(0, len(rows), 2):
        part = rows[begin : begin + 2]
        at = (d * len(rows) + begin) * width
        product = jnp.dot(
            left[...], grads[:, at : at + len(part) * width], preferred_element_type=jnp.float32
        )
        for k, (n, h) in enumerate(part):
            total = None
            for c, col_step in enumerate(TAP_STEPS):
                term = moved(product[c * half : (c + 1) * half, k * width : (k + 1) * width], -col_step)
                total = term if total is None else total + term
            out[n, h] = total.astype(jnp.bfloat16)


def given_kernel(plan, own, other, grads, out, left):
    core, row_bit, next_bit, col_bit = place(plan)
    rest = lax.axis_index("band") // 8
    depth, half, lanes = plan.depth, plan.half, plan.half_lanes
    for x in range(2):
        rows = [[] for _ in TAP_STEPS]
        for m in range(plan.blocks):
            row, behind, col = (m % 2) ^ row_bit, (m // 2 % 2) ^ next_bit, x ^ col_bit
            one = jnp.where(core == 0, row, behind)
            two = jnp.where(core == 0, behind, col)
            three = jnp.where(core == 0, col, row)
            slot = two * 2 + one
            pair = jnp.where(three == 0, own[slot], other[slot]).astype(jnp.float32)
            block = pair[: plan.block_rows]
            for k in range(1, plan.inner):
                at = pair[k * plan.block_rows : (k + 1) * plan.block_rows]
                block = jnp.where(((m // 4) ^ rest) == k, at, block)
            for c in range(len(TAP_STEPS)):
                rows[c].append(block[c * depth : (c + 1) * depth])
        for c in range(len(TAP_STEPS)):
            left[c * half : (c + 1) * half, x * lanes : (x + 1) * lanes] = jnp.concatenate(
                rows[c], axis=0
            ).astype(jnp.bfloat16)
    cells_of(plan, 1, left, grads, out)


def own_kernel(plan, scale, left, grads, keep, message, out, far, terms, sem):
    total = added(keep[...], message[...])[0] * scale
    depth, cols = plan.depth, plan.cols
    for r in range(len(TAP_STEPS)):
        for c in range(len(TAP_STEPS)):
            terms[r * len(TAP_STEPS) + c] = total[c * depth : (c + 1) * depth, r * cols : (r + 1) * cols]
    copy = pltpu.make_async_copy(terms, far, sem)
    copy.start()
    cells_of(plan, 0, left, grads, out)
    copy.wait()


def weave_kernel(plan, own, theirs, far, out, sems):
    core = lax.axis_index("band") % 2
    depth = plan.depth
    copies = []
    for n in range(plan.images):
        for h in range(plan.rows):
            a, b = own[n, h].astype(jnp.float32), theirs[n, h].astype(jnp.float32)
            even, odd = jnp.where(core == 0, a, b), jnp.where(core == 0, b, a)
            pieces = []
            for m in range(plan.blocks):
                pieces += [even[m * depth : (m + 1) * depth], odd[m * depth : (m + 1) * depth]]
            out[n, h] = jnp.concatenate(pieces, axis=0).astype(jnp.bfloat16)
            copies.append(pltpu.make_async_copy(out.at[n, h], far.at[n, h], sems.at[n, h]))
            copies[-1].start()
    for copy in copies:
        copy.wait()


def after(value, *others):
    return lax.optimization_barrier((value, *others))[0]


def pair_kernel(plan, *refs):
    blocks = [ref[k].astype(jnp.float32) for ref in refs[:-1] for k in range(ref.shape[0])]
    refs[-1][0] = jnp.concatenate(blocks, axis=0).astype(jnp.bfloat16)


def first_kernel(plan, kernel):
    shape = jax.ShapeDtypeStruct((plan.block_rows, plan.lanes), jnp.bfloat16)
    packed = call("pack", functools.partial(pack_kernel, plan), shape, [kernel])[None]
    for mask in plan.rest_band[:0:-1]:
        packed = jnp.concatenate([packed, swap(packed, plan.sizes, (mask, 0))], axis=0)
    return [packed] + [swap(packed, plan.sizes, (mask, 0)) for mask in plan.rest_band[:1]]


def whole_kernel(plan, packed, starts):
    sizes = plan.sizes
    starts = list(starts)
    packed = [*packed[:-1], after(packed[-1], starts[0])]
    if plan.rest_strip:
        packed = jnp.concatenate(packed, axis=0)[None]
        for mask in reversed(plan.rest_strip):
            packed = jnp.concatenate([packed, swap(packed, sizes, (0, mask))], axis=0)
        count = packed.shape[0]
        order = jnp.arange(count) ^ (lax.axis_index("strip") % count)
        packed = jnp.take(packed, order, axis=0)[..., : plan.used]
        packed = packed.reshape(count, plan.inner, plan.block_rows, len(TAP_STEPS), plan.cols)
        packed = packed.transpose(1, 2, 3, 0, 4).reshape(plan.inner, plan.block_rows, plan.half_used)
        packed = [jnp.pad(packed, ((0, 0), (0, 0), (0, plan.half_lanes - plan.half_used)))]
    shape = jax.ShapeDtypeStruct((1, plan.part_rows, plan.half_lanes), jnp.bfloat16)
    packed = call("pair", functools.partial(pair_kernel, plan), shape, packed)
    packed = after(packed, starts.pop(0))
    for masks in plan.gather_masks[:-1]:
        come = after(swap(packed, sizes, *masks), starts[0])
        packed = after(jnp.concatenate([packed, come], axis=0), starts.pop(0))
    return packed, swap(packed, sizes, *plan.gather_masks[-1])


def narrowed(plan, total):
    rows = total.shape[0]
    total = total[:, : plan.half_used].reshape(rows, len(TAP_STEPS), plan.half)
    for mask in plan.rest_strip:
        side = (lax.axis_index("strip") // mask) % 2
        parts = total.reshape(rows, len(TAP_STEPS), 2, total.shape[2] // 2)
        kept = jnp.where(side == 0, parts[:, :, 0], parts[:, :, 1])
        given = jnp.where(side == 0, parts[:, :, 1], parts[:, :, 0])
        total = kept + swap(given, plan.sizes, (0, mask))
    total = total.reshape(rows, plan.used)
    return noted(largest(total), jnp.pad(total, ((0, 0), (0, plan.lanes - plan.used))), plan.used)


def kernel_terms(plan, acts, grads):
    sizes, f32 = plan.sizes, jnp.float32
    rows, lanes = plan.part_rows, plan.half_lanes

    def run(name, kernel, shape, kind, operands):
        return call(name, kernel, jax.ShapeDtypeStruct(shape, kind), operands)

    part = functools.partial
    b16 = jnp.bfloat16
    shape = (2, rows, lanes)
    send0 = run("send0", part(send_kernel, plan, False), shape, b16, [acts, grads])
    come0 = swap(send0, sizes, *plan.term_masks[0])
    send1 = run("send1", part(send_kernel, plan, True), shape, b16, [after(acts, send0), grads])
    come1 = swap(send1, sizes, *plan.term_masks[0])
    keep0 = run("keep0", part(keep_kernel, plan, False), shape, f32, [after(acts, send1), grads])
    send = run("turn0", part(turn_kernel, plan, False), shape, b16, [keep0, come0])
    come = swap(send, sizes, *plan.term_masks[1])
    keep1 = run("keep1", part(keep_kernel, plan, True), shape, f32, [after(acts, send), grads])
    keep = run("turn1", part(turn_kernel, plan, True), shape, f32, [keep1, come1])
    steps = {"send0": send0, "send1": send1, "keep0": keep0, "turn0": send, "keep1": keep1, "turn1": keep}
    shape = shape[1:]
    send = run("part0", part(part_kernel, plan, False), shape, b16, [keep, come])
    keep = run("part1", part(part_kernel, plan, True), shape, f32, [after(keep, send), come])
    steps.update(part0=send, part1=keep)
    come = swap(send, sizes, *plan.term_masks[2])
    if plan.rest_strip:
        keep = narrowed(plan, added(keep, come)[0])
        come = jnp.zeros(keep.shape, b16)
    for mask in plan.rest_band:
        rows //= 2
        shape = (rows, plan.lanes)
        halve = part(halve_kernel, plan, mask, plan.used)
        send = run("halve0", part(halve, False), shape, b16, [keep, come])
        keep = run("halve1", part(halve, True), shape, f32, [after(keep, send), come])
        steps.update(halve0=send, halve1=keep)
        come = swap(send, sizes, (mask, 0))
    return keep, come, steps


def edge_kernel(plan, grad, out, copy):
    strip = lax.axis_index("strip")
    for n in range(plan.images):
        out[n] = jnp.where(strip == 0, grad[n, plan.rows - 1], grad[n, 0])
    copy[...] = grad[...]


def borders(plan, grad):
    if plan.strips == 2:
        shape = jax.ShapeDtypeStruct((plan.images, plan.channels, plan.width), grad.dtype)
        copy = jax.ShapeDtypeStruct(grad.shape, grad.dtype)
        edge, grad = call("edge", functools.partial(edge_kernel, plan), (shape, copy), [grad])
        come = [swap(edge, plan.sizes, (core, 1)) for core in range(2)]
        return grad, come, come
    first, last = grad[:, 0], grad[:, plan.rows - 1]
    tops, bottoms = [], []
    for core in range(2):
        down = []
        for b in range(plan.bands):
            down += [(b * plan.strips + s, (b ^ core) * plan.strips + s + 1) for s in range(plan.strips - 1)]
        tops.append(lax.ppermute(last, AXES, down))
        bottoms.append(lax.ppermute(first, AXES, [(b, a) for a, b in down]))
    return grad, tops, bottoms


def body(activations, out_grad, kernel):
    images, channels, rows, width = activations.shape
    bands, strips = lax.axis_size("band"), lax.axis_size("strip")
    plan = Plan(images, channels, rows, width, bands, strips)
    scale = 1.0 / math.sqrt(images * bands * rows * strips * width)
    act = activations.transpose(0, 2, 1, 3)
    grad = out_grad.transpose(0, 2, 1, 3)
    grad0, tops, bottoms = borders(plan, grad)
    act1 = swap(act, plan.sizes, (1, 0))
    grad1 = swap(grad, plan.sizes, (1, 0))
    packed = first_kernel(plan, kernel.transpose(1, 0, 2))
    shape = (2, 2 * plan.part_rows, plan.cells)
    acts = call("acts", functools.partial(acts_kernel, plan), jax.ShapeDtypeStruct(shape, act.dtype), [act, act1])
    shape = (2, plan.half_lanes, plan.cells)
    grads = call(
        "grads",
        functools.partial(grads_kernel, plan),
        jax.ShapeDtypeStruct(shape, grad.dtype),
        [grad0, grad1, *tops, *bottoms],
    )
    keep, come, steps = kernel_terms(plan, acts, grads)
    packed = whole_kernel(plan, packed, [steps[name] for name in GATHER_STEPS])
    shape = jax.ShapeDtypeStruct((images, rows, plan.half, width), jnp.bfloat16)
    left = jax.ShapeDtypeStruct((len(TAP_STEPS) * plan.half, 2 * plan.half_lanes), jnp.bfloat16)
    grads = grads.reshape(2 * plan.half_lanes, plan.cells)
    given, left = call(
        "given",
        functools.partial(given_kernel, plan),
        (shape, left),
        [after(packed[0], steps[CELLS_STEP]), packed[1], grads],
    )
    terms = (len(TAP_STEPS) ** 2, plan.depth, plan.cols)
    own, kernel_grad = call(
        "own",
        functools.partial(own_kernel, plan, scale),
        (shape, jax.ShapeDtypeStruct(terms, jnp.float32)),
        [after(left, given), grads, keep, come],
        [pltpu.VMEM(terms, jnp.float32), pltpu.SemaphoreType.DMA(())],
        far=1,
    )
    theirs = swap(given, plan.sizes, (1, 0))
    shape = (images, rows, channels, width)
    input_grad = call(
        "weave",
        functools.partial(weave_kernel, plan),
        (jax.ShapeDtypeStruct(shape, jnp.bfloat16),),
        [own, theirs],
        [pltpu.VMEM(shape, jnp.bfloat16), pltpu.SemaphoreType.DMA((images, rows))],
        far=1,
    )[0]
    return input_grad.transpose(0, 2, 1, 3), kernel_grad.transpose(1, 0, 2)


def solution(mesh):
    in_specs = (
        P("band", None, "strip", None),
        P("band", None, "strip", None),
        P("band", None, "strip"),
    )
    out_specs = (P("band", None, "strip", None), P("band", None, "strip"))
    return jax.shard_map(body, mesh=mesh, in_specs=in_specs, out_specs=out_specs, check_vma=False)
```

```python
import functools
import math

import jax
import jax.numpy as jnp
from jax import lax
from jax.experimental import pallas as pl
from jax.experimental.pallas import tpu as pltpu
from jax.sharding import PartitionSpec as P

AXES = ("band", "strip")
TAP_STEPS = (-1, 0, 1)
LANES = 128
TOP_POWER = 2.0**15.5
LEAST_POWER = 2.0**-126
LEAST_PEAK = 1e-30
VMEM_BYTES = 40 * 2**20
HINTS = {
    "edge": 8.0,
    "pair": 0.2,
    "pack": 8.0,
    "acts": 0.6,
    "grads": 0.5,
    "send0": 1.4,
    "send1": 1.4,
    "keep0": 1.0,
    "keep1": 1.0,
    "turn0": 0.9,
    "turn1": 0.6,
    "part0": 0.5,
    "part1": 0.3,
    "halve0": 0.5,
    "halve1": 3.0,
    "given": 1.2,
    "own": 1.0,
    "last": 8.0,
    "weave": 0.9,
}
FLOPS_PER_US = 1.15e9


def padded_lanes(count):
    return (count // LANES + 1) * LANES


def swap(value, sizes, *masks):
    bands, strips = sizes
    pairs = []
    for b in range(bands):
        for s in range(strips):
            masks_here = masks[b % len(masks)]
            pairs.append((b * strips + s, (b ^ masks_here[0]) * strips + (s ^ masks_here[1])))
    return lax.ppermute(value, AXES, pairs)


def call(name, kernel, out_shape, operands, scratch=(), far=0):
    outs = jax.tree.map(lambda _: pl.BlockSpec(memory_space=pltpu.VMEM), out_shape)
    if far:
        outs = outs[:-far] + (pl.BlockSpec(memory_space=pl.ANY),) * far
    return pl.pallas_call(
        kernel,
        out_shape=out_shape,
        in_specs=[pl.BlockSpec(memory_space=pltpu.VMEM)] * len(operands),
        out_specs=outs,
        scratch_shapes=list(scratch),
        compiler_params=pltpu.CompilerParams(vmem_limit_bytes=VMEM_BYTES),
        cost_estimate=pl.CostEstimate(
            flops=int(HINTS[name] * FLOPS_PER_US), bytes_accessed=0, transcendentals=0
        ),
        name=name,
    )(*operands)


def encoded(peak, value, used):
    lane = lax.broadcasted_iota(jnp.int32, value.shape, value.ndim - 1)
    ratio = value * (TOP_POWER / peak)
    square = ratio * ratio
    power = ratio * jnp.abs(ratio) * square * (square * square)
    return jnp.where(lane < used, power, peak).astype(jnp.bfloat16)


def decoded(message):
    power = message.astype(jnp.float32)
    peak = power[0:1, message.shape[1] - 1 : message.shape[1]]
    size = jnp.maximum(jnp.abs(power), LEAST_POWER)
    fourth = lax.rsqrt(lax.rsqrt(size))
    root = fourth * lax.rsqrt(fourth)
    return jnp.where(power < 0, -root, root) * (peak * (1.0 / TOP_POWER)), peak


def rounded_up(peak):
    return jnp.maximum(peak * (1.0 + 2.0**-6), LEAST_PEAK).astype(jnp.bfloat16).astype(jnp.float32)


def largest(value):
    return jnp.full((1, 1), jnp.max(jnp.abs(value)), jnp.float32)


def noted(peak, value, used):
    lane = lax.broadcasted_iota(jnp.int32, value.shape, value.ndim - 1)
    return jnp.where(lane < used, value, peak)


def added(keep, message):
    value, peak = decoded(message)
    return keep + value, peak + keep[0:1, keep.shape[1] - 1 : keep.shape[1]]


class Plan:
    def __init__(self, images, channels, rows, width, bands, strips):
        self.images, self.channels, self.rows, self.width = images, channels, rows, width
        self.bands, self.strips = bands, strips
        self.sizes = (bands, strips)
        self.depth = channels // bands
        self.cols = channels // strips
        self.blocks = bands // 2
        self.half = channels // 2
        self.strip_bits = strips.bit_length() - 1
        self.band_bits = bands.bit_length() - 1
        assert bands == 1 << self.band_bits and strips == 1 << self.strip_bits
        assert self.band_bits >= 3 and self.strip_bits >= 1
        self.top_strip = 1 << (self.strip_bits - 1)
        self.rest_strip = [1 << k for k in reversed(range(self.strip_bits - 1))]
        self.rest_band = [1 << k for k in range(3, self.band_bits)]
        self.inner = self.blocks // 4
        self.half_used = len(TAP_STEPS) * self.half
        self.half_lanes = padded_lanes(self.half_used)
        self.used = len(TAP_STEPS) * self.cols
        self.lanes = padded_lanes(self.used)
        self.block_rows = len(TAP_STEPS) * self.depth
        self.part_rows = self.inner * self.block_rows
        self.cells = 2 * images * rows * width
        by_row, by_next, by_col = (2, 0), (4, 0), (0, self.top_strip)
        self.term_masks = ((by_col, by_next), (by_row, by_col), (by_next, by_row))
        self.gather_masks = ((by_next, by_row), (by_col, by_next), (by_row, by_col))

    def block_of(self, slot, by_next, by_row):
        bits = self.band_bits - 3
        turned = sum(((slot >> k) & 1) << (bits - 1 - k) for k in range(bits))
        return turned * 4 + by_next * 2 + by_row

    def chunks(self):
        return [(d, n, h) for d in range(2) for n in range(self.images) for h in range(self.rows)]


def place(plan):
    band, strip = lax.axis_index("band"), lax.axis_index("strip")
    return band % 2, (band // 2) % 2, (band // 4) % 2, strip // plan.top_strip


def mine(plan):
    core, by_row, by_next, by_col = place(plan)
    order = ((by_col, by_row, by_next), (by_next, by_col, by_row))
    return [jnp.where(core == 0, a, b) for a, b in zip(*order)]


def grad_row(plan, grad_ref, top_ref, bottom_ref, image, row, start, strip):
    if row < 0:
        piece = top_ref[image, pl.ds(start, plan.half), :]
        return jnp.where(strip > 0, piece, jnp.zeros_like(piece))
    if row >= plan.rows:
        piece = bottom_ref[image, pl.ds(start, plan.half), :]
        return jnp.where(strip < plan.strips - 1, piece, jnp.zeros_like(piece))
    return grad_ref[image, row, pl.ds(start, plan.half), :]


def moved(value, step):
    width = value.shape[-1]
    if step == 0:
        return value
    lane = lax.broadcasted_iota(jnp.int32, value.shape, value.ndim - 1)
    turned = pltpu.roll(value, (-step) % width, value.ndim - 1)
    inside = lane < width - step if step > 0 else lane >= -step
    return jnp.where(inside, turned, 0.0)


def acts_kernel(plan, act0, act1, out):
    core = lax.axis_index("band") % 2
    depth, width = plan.depth, plan.width
    for at, (d, n, h) in enumerate(plan.chunks()):
        cells = (act0, act1)[d][n, h].astype(jnp.float32)
        shifted = []
        for m in range(plan.blocks):
            begin = 2 * m * depth
            even, odd = cells[begin : begin + depth], cells[begin + depth : begin + 2 * depth]
            block = jnp.where(core == 0, even, odd)
            shifted.append([moved(block, step) for step in TAP_STEPS])
        for i in range(2):
            pieces = []
            for j in range(2):
                for slot in range(plan.inner):
                    here, there = shifted[plan.block_of(slot, j, i)], shifted[plan.block_of(slot, i, j)]
                    pieces += here if i == j else [jnp.where(core == 0, a, b) for a, b in zip(here, there)]
            out[i, :, at * width : (at + 1) * width] = jnp.concatenate(pieces, axis=0).astype(jnp.bfloat16)


def grads_kernel(plan, grad0, grad1, top0, top1, bottom0, bottom1, out):
    strip = lax.axis_index("strip")
    half, width = plan.half, plan.width
    sources = ((grad0, top0, bottom0), (grad1, top1, bottom1))
    for at, (d, n, h) in enumerate(plan.chunks()):
        cells = slice(at * width, (at + 1) * width)
        for x in range(2):
            for r, row_step in enumerate(TAP_STEPS):
                out[x, r * half : (r + 1) * half, cells] = grad_row(
                    plan, *sources[d], n, h - row_step, x * half, strip
                )
            out[x, plan.half_used :, cells] = jnp.zeros((plan.half_lanes - plan.half_used, width), jnp.bfloat16)


def pair_terms(plan, acts, grads, first, second):
    core = lax.axis_index("band") % 2
    i, x = jnp.where(core == 0, second, first), jnp.where(core == 0, first, second)
    return lax.dot_general(acts[i], grads[x], (((1,), (1,)), ((), ())), preferred_element_type=jnp.float32)


def send_kernel(plan, same, acts, grads, out):
    first, second, _ = mine(plan)
    total = pair_terms(plan, acts, grads, 1 - first, second if same else 1 - second)
    for k in range(2):
        half = total[k * plan.part_rows : (k + 1) * plan.part_rows]
        out[k] = encoded(rounded_up(largest(half)), half, plan.half_used)


def keep_kernel(plan, same, acts, grads, out):
    first, second, _ = mine(plan)
    total = pair_terms(plan, acts, grads, first, second if same else 1 - second)
    for k in range(2):
        half = total[k * plan.part_rows : (k + 1) * plan.part_rows]
        out[k] = noted(largest(half), half, plan.half_used)


def turn_kernel(plan, same, keep, message, out):
    for k in range(2):
        total, peak = added(keep[k], message[k])
        out[k] = noted(peak, total, plan.half_used) if same else encoded(rounded_up(peak), total, plan.half_used)


def part_kernel(plan, same, keep, message, out):
    third = mine(plan)[2]
    k = third if same else 1 - third
    total, peak = added(keep[k], message[k])
    out[...] = noted(peak, total, plan.half_used) if same else encoded(rounded_up(peak), total, plan.half_used)


def halve_kernel(plan, mask, used, same, keep, message, out):
    side = (lax.axis_index("band") // mask) % 2
    total, peak = added(keep[...], message[...])
    rows = total.shape[0] // 2
    lower, upper = total[:rows], total[rows:]
    if same:
        out[...] = noted(peak, jnp.where(side == 0, lower, upper), used)
    else:
        out[...] = encoded(rounded_up(peak), jnp.where(side == 0, upper, lower), used)


def pack_kernel(plan, kernel, out):
    rows = []
    for c in range(len(TAP_STEPS)):
        pieces = [kernel[r * len(TAP_STEPS) + c].astype(jnp.float32) for r in range(len(TAP_STEPS))]
        pieces.append(jnp.zeros((plan.depth, plan.lanes - plan.used), jnp.float32))
        rows.append(jnp.concatenate(pieces, axis=1))
    out[...] = jnp.concatenate(rows, axis=0).astype(jnp.bfloat16)


def cells_of(plan, d, left, grads, out):
    width, half = plan.width, plan.half
    rows = [(n, h) for n in range(plan.images) for h in range(plan.rows)]
    for begin in range(0, len(rows), 2):
        part = rows[begin : begin + 2]
        at = (d * len(rows) + begin) * width
        product = jnp.dot(
            left[...], grads[:, at : at + len(part) * width], preferred_element_type=jnp.float32
        )
        for k, (n, h) in enumerate(part):
            total = None
            for c, col_step in enumerate(TAP_STEPS):
                term = moved(product[c * half : (c + 1) * half, k * width : (k + 1) * width], -col_step)
                total = term if total is None else total + term
            out[n, h] = total.astype(jnp.bfloat16)


def given_kernel(plan, own, third, last0, last1, grads, out, left):
    core, row_bit, next_bit, col_bit = place(plan)
    rest = lax.axis_index("band") // 8
    depth, half, lanes = plan.depth, plan.half, plan.half_lanes
    for x in range(2):
        rows = [[] for _ in TAP_STEPS]
        for m in range(plan.blocks):
            row, behind, col = (m % 2) ^ row_bit, (m // 2 % 2) ^ next_bit, x ^ col_bit
            one = jnp.where(core == 0, behind, row)
            two = jnp.where(core == 0, col, behind)
            three = jnp.where(core == 0, row, col)
            before = jnp.where(two == 0, own[one], third[one])
            pair = jnp.where(three == 0, before, jnp.where(two == 0, last0[one], last1[one])).astype(jnp.float32)
            block = pair[: plan.block_rows]
            for k in range(1, plan.inner):
                at = pair[k * plan.block_rows : (k + 1) * plan.block_rows]
                block = jnp.where(((m // 4) ^ rest) == k, at, block)
            for c in range(len(TAP_STEPS)):
                rows[c].append(block[c * depth : (c + 1) * depth])
        for c in range(len(TAP_STEPS)):
            left[c * half : (c + 1) * half, x * lanes : (x + 1) * lanes] = jnp.concatenate(
                rows[c], axis=0
            ).astype(jnp.bfloat16)
    cells_of(plan, 1, left, grads, out)


def own_kernel(plan, left, grads, out):
    cells_of(plan, 0, left, grads, out)


def last_kernel(plan, scale, keep, message, out):
    total = added(keep[...], message[...])[0] * scale
    depth, cols = plan.depth, plan.cols
    for r in range(len(TAP_STEPS)):
        for c in range(len(TAP_STEPS)):
            out[r * len(TAP_STEPS) + c] = total[c * depth : (c + 1) * depth, r * cols : (r + 1) * cols]


def weave_kernel(plan, own, theirs, far, out, sems):
    core = lax.axis_index("band") % 2
    depth = plan.depth
    copies = []
    for n in range(plan.images):
        for h in range(plan.rows):
            a, b = own[n, h].astype(jnp.float32), theirs[n, h].astype(jnp.float32)
            even, odd = jnp.where(core == 0, a, b), jnp.where(core == 0, b, a)
            pieces = []
            for m in range(plan.blocks):
                pieces += [even[m * depth : (m + 1) * depth], odd[m * depth : (m + 1) * depth]]
            out[n, h] = jnp.concatenate(pieces, axis=0).astype(jnp.bfloat16)
            copies.append(pltpu.make_async_copy(out.at[n, h], far.at[n, h], sems.at[n, h]))
            copies[-1].start()
    for copy in copies:
        copy.wait()


def after(value, *others):
    return lax.optimization_barrier((value, *others))[0]


def pair_kernel(plan, *refs):
    blocks = [ref[k].astype(jnp.float32) for ref in refs[:-1] for k in range(ref.shape[0])]
    refs[-1][0] = jnp.concatenate(blocks, axis=0).astype(jnp.bfloat16)


def first_kernel(plan, kernel):
    shape = jax.ShapeDtypeStruct((plan.block_rows, plan.lanes), jnp.bfloat16)
    packed = call("pack", functools.partial(pack_kernel, plan), shape, [kernel])[None]
    for mask in plan.rest_band[:0:-1]:
        packed = jnp.concatenate([packed, swap(packed, plan.sizes, (mask, 0))], axis=0)
    return [packed] + [swap(packed, plan.sizes, (mask, 0)) for mask in plan.rest_band[:1]]


def more_kernel(plan, packed, start, end, last):
    sizes = plan.sizes
    packed = [*packed[:-1], after(packed[-1], start)]
    if plan.rest_strip:
        packed = jnp.concatenate(packed, axis=0)[None]
        for mask in reversed(plan.rest_strip):
            packed = jnp.concatenate([packed, swap(packed, sizes, (0, mask))], axis=0)
        count = packed.shape[0]
        order = jnp.arange(count) ^ (lax.axis_index("strip") % count)
        packed = jnp.take(packed, order, axis=0)[..., : plan.used]
        packed = packed.reshape(count, plan.inner, plan.block_rows, len(TAP_STEPS), plan.cols)
        packed = packed.transpose(1, 2, 3, 0, 4).reshape(plan.inner, plan.block_rows, plan.half_used)
        packed = [jnp.pad(packed, ((0, 0), (0, 0), (0, plan.half_lanes - plan.half_used)))]
    shape = jax.ShapeDtypeStruct((1, plan.part_rows, plan.half_lanes), jnp.bfloat16)
    packed = after(call("pair", functools.partial(pair_kernel, plan), shape, packed), start)
    come = after(swap(packed, sizes, *plan.gather_masks[0]), end)
    packed = after(jnp.concatenate([packed, come], axis=0), end)
    third = swap(packed, sizes, *plan.gather_masks[1])
    return packed, third, swap(after(packed, last), sizes, *plan.gather_masks[2])


def narrowed(plan, total):
    rows = total.shape[0]
    total = total[:, : plan.half_used].reshape(rows, len(TAP_STEPS), plan.half)
    for mask in plan.rest_strip:
        side = (lax.axis_index("strip") // mask) % 2
        parts = total.reshape(rows, len(TAP_STEPS), 2, total.shape[2] // 2)
        kept = jnp.where(side == 0, parts[:, :, 0], parts[:, :, 1])
        given = jnp.where(side == 0, parts[:, :, 1], parts[:, :, 0])
        total = kept + swap(given, plan.sizes, (0, mask))
    total = total.reshape(rows, plan.used)
    return noted(largest(total), jnp.pad(total, ((0, 0), (0, plan.lanes - plan.used))), plan.used)


def kernel_terms(plan, acts, grads, packed):
    sizes, f32 = plan.sizes, jnp.float32
    rows, lanes = plan.part_rows, plan.half_lanes

    def run(name, kernel, shape, kind, operands):
        return call(name, kernel, jax.ShapeDtypeStruct(shape, kind), operands)

    part = functools.partial
    b16 = jnp.bfloat16
    shape = (2, rows, lanes)
    send0 = run("send0", part(send_kernel, plan, False), shape, b16, [acts, grads])
    come0 = swap(send0, sizes, *plan.term_masks[0])
    send1 = run("send1", part(send_kernel, plan, True), shape, b16, [after(acts, send0), grads])
    come1 = swap(send1, sizes, *plan.term_masks[0])
    keep0 = run("keep0", part(keep_kernel, plan, False), shape, f32, [after(acts, send1), grads])
    send = run("turn0", part(turn_kernel, plan, False), shape, b16, [keep0, come0])
    come = swap(send, sizes, *plan.term_masks[1])
    keep1 = run("keep1", part(keep_kernel, plan, True), shape, f32, [after(acts, send), grads])
    keep = run("turn1", part(turn_kernel, plan, True), shape, f32, [keep1, come1])
    packed, third, last0 = more_kernel(plan, packed, keep0, send, keep1)
    shape = shape[1:]
    send = run("part0", part(part_kernel, plan, False), shape, b16, [keep, come])
    last1 = swap(after(third, send), sizes, *plan.gather_masks[2])
    keep = run("part1", part(part_kernel, plan, True), shape, f32, [after(keep, send), come])
    come = swap(send, sizes, *plan.term_masks[2])
    if plan.rest_strip:
        keep = narrowed(plan, added(keep, come)[0])
        come = jnp.zeros(keep.shape, b16)
    for mask in plan.rest_band:
        rows //= 2
        shape = (rows, plan.lanes)
        halve = part(halve_kernel, plan, mask, plan.used)
        send = run("halve0", part(halve, False), shape, b16, [keep, come])
        keep = run("halve1", part(halve, True), shape, f32, [after(keep, send, last0), come])
        come = swap(send, sizes, (mask, 0))
    return keep, come, (packed, third, last0, after(last1, keep))


def edge_kernel(plan, grad, out, copy):
    strip = lax.axis_index("strip")
    for n in range(plan.images):
        out[n] = jnp.where(strip == 0, grad[n, plan.rows - 1], grad[n, 0])
    copy[...] = grad[...]


def borders(plan, grad):
    if plan.strips == 2:
        shape = jax.ShapeDtypeStruct((plan.images, plan.channels, plan.width), grad.dtype)
        copy = jax.ShapeDtypeStruct(grad.shape, grad.dtype)
        edge, grad = call("edge", functools.partial(edge_kernel, plan), (shape, copy), [grad])
        come = [swap(edge, plan.sizes, (core, 1)) for core in range(2)]
        return grad, come, come
    first, last = grad[:, 0], grad[:, plan.rows - 1]
    tops, bottoms = [], []
    for core in range(2):
        down = []
        for b in range(plan.bands):
            down += [(b * plan.strips + s, (b ^ core) * plan.strips + s + 1) for s in range(plan.strips - 1)]
        tops.append(lax.ppermute(last, AXES, down))
        bottoms.append(lax.ppermute(first, AXES, [(b, a) for a, b in down]))
    return grad, tops, bottoms


def body(activations, out_grad, kernel):
    images, channels, rows, width = activations.shape
    bands, strips = lax.axis_size("band"), lax.axis_size("strip")
    plan = Plan(images, channels, rows, width, bands, strips)
    scale = 1.0 / math.sqrt(images * bands * rows * strips * width)
    act = activations.transpose(0, 2, 1, 3)
    grad = out_grad.transpose(0, 2, 1, 3)
    grad0, tops, bottoms = borders(plan, grad)
    act1 = swap(act, plan.sizes, (1, 0))
    grad1 = swap(grad, plan.sizes, (1, 0))
    packed = first_kernel(plan, kernel.transpose(1, 0, 2))
    shape = (2, 2 * plan.part_rows, plan.cells)
    acts = call("acts", functools.partial(acts_kernel, plan), jax.ShapeDtypeStruct(shape, act.dtype), [act, act1])
    shape = (2, plan.half_lanes, plan.cells)
    grads = call(
        "grads",
        functools.partial(grads_kernel, plan),
        jax.ShapeDtypeStruct(shape, grad.dtype),
        [grad0, grad1, *tops, *bottoms],
    )
    keep, come, packed = kernel_terms(plan, acts, grads, packed)
    shape = jax.ShapeDtypeStruct((images, rows, plan.half, width), jnp.bfloat16)
    left = jax.ShapeDtypeStruct((len(TAP_STEPS) * plan.half, 2 * plan.half_lanes), jnp.bfloat16)
    grads = grads.reshape(2 * plan.half_lanes, plan.cells)
    given, left = call(
        "given",
        functools.partial(given_kernel, plan),
        (shape, left),
        [*packed, grads],
    )
    own = call("own", functools.partial(own_kernel, plan), shape, [after(left, given), grads])
    theirs = swap(given, plan.sizes, (1, 0))
    shape = (images, rows, channels, width)
    input_grad = call(
        "weave",
        functools.partial(weave_kernel, plan),
        (jax.ShapeDtypeStruct(shape, jnp.bfloat16),),
        [own, theirs],
        [pltpu.VMEM(shape, jnp.bfloat16), pltpu.SemaphoreType.DMA((images, rows))],
        far=1,
    )[0]
    shape = jax.ShapeDtypeStruct((len(TAP_STEPS) ** 2, plan.depth, plan.cols), jnp.float32)
    kernel_grad = call("last", functools.partial(last_kernel, plan, scale), shape, [keep, come])
    return input_grad.transpose(0, 2, 1, 3), kernel_grad.transpose(1, 0, 2)


def solution(mesh):
    in_specs = (
        P("band", None, "strip", None),
        P("band", None, "strip", None),
        P("band", None, "strip"),
    )
    out_specs = (P("band", None, "strip", None), P("band", None, "strip"))
    return jax.shard_map(body, mesh=mesh, in_specs=in_specs, out_specs=out_specs, check_vma=False)
```

```python
import functools
import math

import jax
import jax.numpy as jnp
from jax import lax
from jax.experimental import pallas as pl
from jax.experimental.pallas import tpu as pltpu
from jax.sharding import PartitionSpec as P

AXES = ("band", "strip")
TAP_STEPS = (-1, 0, 1)
LANES = 128
TOP_POWER = 2.0**15.5
LEAST_POWER = 2.0**-126
LEAST_PEAK = 1e-30
ROW_FIRST = False
VMEM_BYTES = 40 * 2**20
HINTS = {
    "edge": 8.0,
    "pair": 0.2,
    "pack": 8.0,
    "acts": 0.6,
    "grads": 0.5,
    "send0": 1.4,
    "send1": 1.4,
    "keep0": 1.0,
    "keep1": 1.0,
    "turn0": 0.9,
    "turn1": 0.6,
    "part0": 0.5,
    "part1": 0.3,
    "halve0": 0.5,
    "halve1": 3.0,
    "early": 1.7,
    "given": 0.5,
    "own": 0.5,
    "last": 8.0,
    "weave": 0.9,
}
FLOPS_PER_US = 1.15e9


def padded_lanes(count):
    return (count // LANES + 1) * LANES


def swap(value, sizes, *masks):
    bands, strips = sizes
    pairs = []
    for b in range(bands):
        for s in range(strips):
            masks_here = masks[b % len(masks)]
            pairs.append((b * strips + s, (b ^ masks_here[0]) * strips + (s ^ masks_here[1])))
    return lax.ppermute(value, AXES, pairs)


def call(name, kernel, out_shape, operands, scratch=(), far=0):
    outs = jax.tree.map(lambda _: pl.BlockSpec(memory_space=pltpu.VMEM), out_shape)
    if far:
        outs = outs[:-far] + (pl.BlockSpec(memory_space=pl.ANY),) * far
    return pl.pallas_call(
        kernel,
        out_shape=out_shape,
        in_specs=[pl.BlockSpec(memory_space=pltpu.VMEM)] * len(operands),
        out_specs=outs,
        scratch_shapes=list(scratch),
        compiler_params=pltpu.CompilerParams(vmem_limit_bytes=VMEM_BYTES),
        cost_estimate=pl.CostEstimate(
            flops=int(HINTS[name] * FLOPS_PER_US), bytes_accessed=0, transcendentals=0
        ),
        name=name,
    )(*operands)


def encoded(peak, value, used):
    lane = lax.broadcasted_iota(jnp.int32, value.shape, value.ndim - 1)
    ratio = value * (TOP_POWER / peak)
    square = ratio * ratio
    power = ratio * jnp.abs(ratio) * square * (square * square)
    return jnp.where(lane < used, power, peak).astype(jnp.bfloat16)


def decoded(message):
    power = message.astype(jnp.float32)
    peak = power[0:1, message.shape[1] - 1 : message.shape[1]]
    size = jnp.maximum(jnp.abs(power), LEAST_POWER)
    fourth = lax.rsqrt(lax.rsqrt(size))
    root = fourth * lax.rsqrt(fourth)
    return jnp.where(power < 0, -root, root) * (peak * (1.0 / TOP_POWER)), peak


def rounded_up(peak):
    return jnp.maximum(peak * (1.0 + 2.0**-6), LEAST_PEAK).astype(jnp.bfloat16).astype(jnp.float32)


def largest(value):
    return jnp.full((1, 1), jnp.max(jnp.abs(value)), jnp.float32)


def noted(peak, value, used):
    lane = lax.broadcasted_iota(jnp.int32, value.shape, value.ndim - 1)
    return jnp.where(lane < used, value, peak)


def added(keep, message):
    value, peak = decoded(message)
    return keep + value, peak + keep[0:1, keep.shape[1] - 1 : keep.shape[1]]


class Plan:
    def __init__(self, images, channels, rows, width, bands, strips):
        self.images, self.channels, self.rows, self.width = images, channels, rows, width
        self.bands, self.strips = bands, strips
        self.sizes = (bands, strips)
        self.depth = channels // bands
        self.cols = channels // strips
        self.blocks = bands // 2
        self.half = channels // 2
        self.strip_bits = strips.bit_length() - 1
        self.band_bits = bands.bit_length() - 1
        assert bands == 1 << self.band_bits and strips == 1 << self.strip_bits
        assert self.band_bits >= 3 and self.strip_bits >= 1
        self.top_strip = 1 << (self.strip_bits - 1)
        self.rest_strip = [1 << k for k in reversed(range(self.strip_bits - 1))]
        self.rest_band = [1 << k for k in range(3, self.band_bits)]
        self.inner = self.blocks // 4
        self.half_used = len(TAP_STEPS) * self.half
        self.half_lanes = padded_lanes(self.half_used)
        self.used = len(TAP_STEPS) * self.cols
        self.lanes = padded_lanes(self.used)
        self.block_rows = len(TAP_STEPS) * self.depth
        self.part_rows = self.inner * self.block_rows
        self.cells = 2 * images * rows * width
        by_row, by_next, by_col = (2, 0), (4, 0), (0, self.top_strip)
        self.term_masks = ((by_col, by_next), (by_row, by_col), (by_next, by_row))
        ones, others = (by_row, by_next) if ROW_FIRST else (by_next, by_row)
        self.gather_masks = ((ones, others), (others, by_col), (by_col, ones))

    def block_of(self, slot, by_next, by_row):
        bits = self.band_bits - 3
        turned = sum(((slot >> k) & 1) << (bits - 1 - k) for k in range(bits))
        return turned * 4 + by_next * 2 + by_row

    def chunks(self):
        return [(d, n, h) for d in range(2) for n in range(self.images) for h in range(self.rows)]


def place(plan):
    band, strip = lax.axis_index("band"), lax.axis_index("strip")
    return band % 2, (band // 2) % 2, (band // 4) % 2, strip // plan.top_strip


def mine(plan):
    core, by_row, by_next, by_col = place(plan)
    order = ((by_col, by_row, by_next), (by_next, by_col, by_row))
    return [jnp.where(core == 0, a, b) for a, b in zip(*order)]


def grad_row(plan, grad_ref, top_ref, bottom_ref, image, row, start, strip):
    if row < 0:
        piece = top_ref[image, pl.ds(start, plan.half), :]
        return jnp.where(strip > 0, piece, jnp.zeros_like(piece))
    if row >= plan.rows:
        piece = bottom_ref[image, pl.ds(start, plan.half), :]
        return jnp.where(strip < plan.strips - 1, piece, jnp.zeros_like(piece))
    return grad_ref[image, row, pl.ds(start, plan.half), :]


def moved(value, step):
    width = value.shape[-1]
    if step == 0:
        return value
    lane = lax.broadcasted_iota(jnp.int32, value.shape, value.ndim - 1)
    turned = pltpu.roll(value, (-step) % width, value.ndim - 1)
    inside = lane < width - step if step > 0 else lane >= -step
    return jnp.where(inside, turned, 0.0)


def acts_kernel(plan, act0, act1, out):
    core = lax.axis_index("band") % 2
    depth, width = plan.depth, plan.width
    for at, (d, n, h) in enumerate(plan.chunks()):
        cells = (act0, act1)[d][n, h].astype(jnp.float32)
        shifted = []
        for m in range(plan.blocks):
            begin = 2 * m * depth
            even, odd = cells[begin : begin + depth], cells[begin + depth : begin + 2 * depth]
            block = jnp.where(core == 0, even, odd)
            shifted.append([moved(block, step) for step in TAP_STEPS])
        for i in range(2):
            pieces = []
            for j in range(2):
                for slot in range(plan.inner):
                    here, there = shifted[plan.block_of(slot, j, i)], shifted[plan.block_of(slot, i, j)]
                    pieces += here if i == j else [jnp.where(core == 0, a, b) for a, b in zip(here, there)]
            out[i, :, at * width : (at + 1) * width] = jnp.concatenate(pieces, axis=0).astype(jnp.bfloat16)


def grads_kernel(plan, grad0, grad1, top0, top1, bottom0, bottom1, out):
    strip = lax.axis_index("strip")
    half, width = plan.half, plan.width
    sources = ((grad0, top0, bottom0), (grad1, top1, bottom1))
    for at, (d, n, h) in enumerate(plan.chunks()):
        cells = slice(at * width, (at + 1) * width)
        for x in range(2):
            for r, row_step in enumerate(TAP_STEPS):
                out[x, r * half : (r + 1) * half, cells] = grad_row(
                    plan, *sources[d], n, h - row_step, x * half, strip
                )
            out[x, plan.half_used :, cells] = jnp.zeros((plan.half_lanes - plan.half_used, width), jnp.bfloat16)


def pair_terms(plan, acts, grads, first, second):
    core = lax.axis_index("band") % 2
    i, x = jnp.where(core == 0, second, first), jnp.where(core == 0, first, second)
    return lax.dot_general(acts[i], grads[x], (((1,), (1,)), ((), ())), preferred_element_type=jnp.float32)


def send_kernel(plan, same, acts, grads, out):
    first, second, _ = mine(plan)
    total = pair_terms(plan, acts, grads, 1 - first, second if same else 1 - second)
    for k in range(2):
        half = total[k * plan.part_rows : (k + 1) * plan.part_rows]
        out[k] = encoded(rounded_up(largest(half)), half, plan.half_used)


def keep_kernel(plan, same, acts, grads, out):
    first, second, _ = mine(plan)
    total = pair_terms(plan, acts, grads, first, second if same else 1 - second)
    for k in range(2):
        half = total[k * plan.part_rows : (k + 1) * plan.part_rows]
        out[k] = noted(largest(half), half, plan.half_used)


def turn_kernel(plan, same, keep, message, out):
    for k in range(2):
        total, peak = added(keep[k], message[k])
        out[k] = noted(peak, total, plan.half_used) if same else encoded(rounded_up(peak), total, plan.half_used)


def part_kernel(plan, same, keep, message, out):
    third = mine(plan)[2]
    k = third if same else 1 - third
    total, peak = added(keep[k], message[k])
    out[...] = noted(peak, total, plan.half_used) if same else encoded(rounded_up(peak), total, plan.half_used)


def halve_kernel(plan, mask, used, same, keep, message, out):
    side = (lax.axis_index("band") // mask) % 2
    total, peak = added(keep[...], message[...])
    rows = total.shape[0] // 2
    lower, upper = total[:rows], total[rows:]
    if same:
        out[...] = noted(peak, jnp.where(side == 0, lower, upper), used)
    else:
        out[...] = encoded(rounded_up(peak), jnp.where(side == 0, upper, lower), used)


def pack_kernel(plan, kernel, out):
    rows = []
    for c in range(len(TAP_STEPS)):
        pieces = [kernel[r * len(TAP_STEPS) + c].astype(jnp.float32) for r in range(len(TAP_STEPS))]
        pieces.append(jnp.zeros((plan.depth, plan.lanes - plan.used), jnp.float32))
        rows.append(jnp.concatenate(pieces, axis=1))
    out[...] = jnp.concatenate(rows, axis=0).astype(jnp.bfloat16)


def halves(plan):
    core, row_bit, next_bit, _ = place(plan)
    by_row = (core == 0) != ROW_FIRST
    return jnp.where(by_row, row_bit, next_bit), jnp.where(by_row, next_bit, row_bit)


def ordered(plan, blocks):
    rest = lax.axis_index("band") // 8
    other_bit = halves(plan)[1]
    parts = [jnp.where(other_bit == 0, blocks[k], blocks[1 - k]).astype(jnp.float32) for k in range(2)]
    rows = []
    for c in range(len(TAP_STEPS)):
        for k in range(plan.inner):
            for part in parts:
                piece = None
                for at in range(plan.inner):
                    begin = at * plan.block_rows + c * plan.depth
                    here = part[begin : begin + plan.depth]
                    piece = here if piece is None else jnp.where((k ^ rest) == at, here, piece)
                rows.append(piece)
    return jnp.concatenate(rows, axis=0).astype(jnp.bfloat16)


def summed(plan, product):
    quarter = plan.half // 2
    total = None
    for c, col_step in enumerate(TAP_STEPS):
        term = moved(product[c * quarter : (c + 1) * quarter], -col_step)
        total = term if total is None else total + term
    return total.astype(jnp.bfloat16)


def groups(plan):
    rows = [(n, h) for n in range(plan.images) for h in range(plan.rows)]
    for d in range(2):
        for begin in range(0, len(rows), 2):
            part = rows[begin : begin + 2]
            at = (d * len(rows) + begin) * plan.width
            where = [(n, h, slice(k * plan.width, (k + 1) * plan.width)) for k, (n, h) in enumerate(part)]
            yield d, slice(at, at + len(part) * plan.width), where


def early_kernel(plan, own, third, last0, grads, out0, out1, rest):
    core, _, _, col = place(plan)
    near, far = ordered(plan, own), [ordered(plan, third), ordered(plan, last0)]
    beside = jnp.where(core == 0, far[1], far[0])
    below = jnp.where(core == 0, far[0], far[1])
    for d, cells, where in groups(plan):
        here, there = grads[col, :, cells], grads[1 - col, :, cells]
        product = jnp.dot(near, here, preferred_element_type=jnp.float32)
        product = product + jnp.dot(beside, there, preferred_element_type=jnp.float32)
        rest[:, cells] = jnp.dot(below, here, preferred_element_type=jnp.float32)
        for n, h, lanes in where:
            (out0, out1)[d][n, h] = summed(plan, product[:, lanes])


def late_of(plan, image, left, grads, rest, out):
    col = place(plan)[3]
    for d, cells, where in groups(plan):
        if d == image:
            product = rest[:, cells]
            product = product + jnp.dot(left, grads[1 - col, :, cells], preferred_element_type=jnp.float32)
            for n, h, lanes in where:
                out[n, h] = summed(plan, product[:, lanes])


def given_kernel(plan, last1, grads, rest, out, left):
    left[...] = ordered(plan, last1)
    late_of(plan, 1, left[...], grads, rest, out)


def own_kernel(plan, left, grads, rest, out):
    late_of(plan, 0, left[...], grads, rest, out)


def pack_kernel(plan, kernel, out):
    rows = []
    for c in range(len(TAP_STEPS)):
        pieces = [kernel[r * len(TAP_STEPS) + c].astype(jnp.float32) for r in range(len(TAP_STEPS))]
        pieces.append(jnp.zeros((plan.depth, plan.lanes - plan.used), jnp.float32))
        rows.append(jnp.concatenate(pieces, axis=1))
    out[...] = jnp.concatenate(rows, axis=0).astype(jnp.bfloat16)


def halves(plan):
    core, row_bit, next_bit, _ = place(plan)
    by_row = (core == 0) != ROW_FIRST
    return jnp.where(by_row, row_bit, next_bit), jnp.where(by_row, next_bit, row_bit)


def ordered(plan, blocks):
    rest = lax.axis_index("band") // 8
    other_bit = halves(plan)[1]
    parts = [jnp.where(other_bit == 0, blocks[k], blocks[1 - k]).astype(jnp.float32) for k in range(2)]
    rows = []
    for c in range(len(TAP_STEPS)):
        for k in range(plan.inner):
            for part in parts:
                piece = None
                for at in range(plan.inner):
                    begin = at * plan.block_rows + c * plan.depth
                    here = part[begin : begin + plan.depth]
                    piece = here if piece is None else jnp.where((k ^ rest) == at, here, piece)
                rows.append(piece)
    return jnp.concatenate(rows, axis=0).astype(jnp.bfloat16)


def summed(plan, product):
    quarter = plan.half // 2
    total = None
    for c, col_step in enumerate(TAP_STEPS):
        term = moved(product[c * quarter : (c + 1) * quarter], -col_step)
        total = term if total is None else total + term
    return total.astype(jnp.bfloat16)


def groups(plan):
    rows = [(n, h) for n in range(plan.images) for h in range(plan.rows)]
    for d in range(2):
        for begin in range(0, len(rows), 2):
            part = rows[begin : begin + 2]
            at = (d * len(rows) + begin) * plan.width
            where = [(n, h, slice(k * plan.width, (k + 1) * plan.width)) for k, (n, h) in enumerate(part)]
            yield d, slice(at, at + len(part) * plan.width), where


def early_kernel(plan, own, third, last0, grads, out0, out1, rest):
    core, _, _, col = place(plan)
    near, far = ordered(plan, own), [ordered(plan, third), ordered(plan, last0)]
    beside = jnp.where(core == 0, far[1], far[0])
    below = jnp.where(core == 0, far[0], far[1])
    for d, cells, where in groups(plan):
        here, there = grads[col, :, cells], grads[1 - col, :, cells]
        product = jnp.dot(near, here, preferred_element_type=jnp.float32)
        product = product + jnp.dot(beside, there, preferred_element_type=jnp.float32)
        rest[:, cells] = jnp.dot(below, here, preferred_element_type=jnp.float32)
        for n, h, lanes in where:
            (out0, out1)[d][n, h] = summed(plan, product[:, lanes])


def late_of(plan, image, left, grads, rest, out):
    col = place(plan)[3]
    for d, cells, where in groups(plan):
        if d == image:
            product = rest[:, cells]
            product = product + jnp.dot(left, grads[1 - col, :, cells], preferred_element_type=jnp.float32)
            for n, h, lanes in where:
                out[n, h] = summed(plan, product[:, lanes])


def given_kernel(plan, last1, grads, rest, out, left):
    left[...] = ordered(plan, last1)
    late_of(plan, 1, left[...], grads, rest, out)


def own_kernel(plan, left, grads, rest, out):
    late_of(plan, 0, left[...], grads, rest, out)


def last_kernel(plan, scale, keep, message, out):
    total = added(keep[...], message[...])[0] * scale
    depth, cols = plan.depth, plan.cols
    for r in range(len(TAP_STEPS)):
        for c in range(len(TAP_STEPS)):
            out[r * len(TAP_STEPS) + c] = total[c * depth : (c + 1) * depth, r * cols : (r + 1) * cols]


def last_kernel(plan, scale, keep, message, out):
    total = added(keep[...], message[...])[0] * scale
    depth, cols = plan.depth, plan.cols
    for r in range(len(TAP_STEPS)):
        for c in range(len(TAP_STEPS)):
            out[r * len(TAP_STEPS) + c] = total[c * depth : (c + 1) * depth, r * cols : (r + 1) * cols]


def weave_kernel(plan, own0, own1, theirs0, theirs1, terms, far, far_terms, out, sems, sem):
    copies = [pltpu.make_async_copy(terms, far_terms, sem)]
    copies[0].start()
    core, row_bit, next_bit, _ = place(plan)
    depth = plan.depth
    for n in range(plan.images):
        for h in range(plan.rows):
            mine = [ref[n, h].astype(jnp.float32) for ref in (own0, own1)]
            others = [ref[n, h].astype(jnp.float32) for ref in (theirs0, theirs1)]
            pieces = []
            for m in range(plan.blocks):
                for p in range(2):
                    by_row = (p == 0) != ROW_FIRST
                    bit, other, ours = (m % 2, m // 2 % 2, row_bit) if by_row else (m // 2 % 2, m % 2, next_bit)
                    at = slice((m // 4 * 2 + other) * depth, (m // 4 * 2 + other + 1) * depth)
                    a = jnp.where(bit == ours, mine[0][at], mine[1][at])
                    b = jnp.where(bit == ours, others[0][at], others[1][at])
                    pieces.append(jnp.where(core == p, a, b))
            out[n, h] = jnp.concatenate(pieces, axis=0).astype(jnp.bfloat16)
            copies.append(pltpu.make_async_copy(out.at[n, h], far.at[n, h], sems.at[n, h]))
            copies[-1].start()
    for copy in copies:
        copy.wait()


def after(value, *others):
    return lax.optimization_barrier((value, *others))[0]


def pair_kernel(plan, *refs):
    blocks = [ref[k].astype(jnp.float32) for ref in refs[:-1] for k in range(ref.shape[0])]
    refs[-1][0] = jnp.concatenate(blocks, axis=0).astype(jnp.bfloat16)


def first_kernel(plan, kernel):
    shape = jax.ShapeDtypeStruct((plan.block_rows, plan.lanes), jnp.bfloat16)
    packed = call("pack", functools.partial(pack_kernel, plan), shape, [kernel])[None]
    for mask in plan.rest_band[:0:-1]:
        packed = jnp.concatenate([packed, swap(packed, plan.sizes, (mask, 0))], axis=0)
    return [packed] + [swap(packed, plan.sizes, (mask, 0)) for mask in plan.rest_band[:1]]


def more_kernel(plan, packed, start, end, last):
    sizes = plan.sizes
    packed = [*packed[:-1], after(packed[-1], start)]
    if plan.rest_strip:
        packed = jnp.concatenate(packed, axis=0)[None]
        for mask in reversed(plan.rest_strip):
            packed = jnp.concatenate([packed, swap(packed, sizes, (0, mask))], axis=0)
        count = packed.shape[0]
        order = jnp.arange(count) ^ (lax.axis_index("strip") % count)
        packed = jnp.take(packed, order, axis=0)[..., : plan.used]
        packed = packed.reshape(count, plan.inner, plan.block_rows, len(TAP_STEPS), plan.cols)
        packed = packed.transpose(1, 2, 3, 0, 4).reshape(plan.inner, plan.block_rows, plan.half_used)
        packed = [jnp.pad(packed, ((0, 0), (0, 0), (0, plan.half_lanes - plan.half_used)))]
    shape = jax.ShapeDtypeStruct((1, plan.part_rows, plan.half_lanes), jnp.bfloat16)
    packed = after(call("pair", functools.partial(pair_kernel, plan), shape, packed), start)
    come = after(swap(packed, sizes, *plan.gather_masks[0]), end)
    packed = after(jnp.concatenate([packed, come], axis=0), end)
    third = swap(packed, sizes, *plan.gather_masks[1])
    return packed, third, swap(after(packed, last), sizes, *plan.gather_masks[2])


def narrowed(plan, total):
    rows = total.shape[0]
    total = total[:, : plan.half_used].reshape(rows, len(TAP_STEPS), plan.half)
    for mask in plan.rest_strip:
        side = (lax.axis_index("strip") // mask) % 2
        parts = total.reshape(rows, len(TAP_STEPS), 2, total.shape[2] // 2)
        kept = jnp.where(side == 0, parts[:, :, 0], parts[:, :, 1])
        given = jnp.where(side == 0, parts[:, :, 1], parts[:, :, 0])
        total = kept + swap(given, plan.sizes, (0, mask))
    total = total.reshape(rows, plan.used)
    return noted(largest(total), jnp.pad(total, ((0, 0), (0, plan.lanes - plan.used))), plan.used)


def kernel_terms(plan, acts, grads, packed):
    sizes, f32 = plan.sizes, jnp.float32
    rows, lanes = plan.part_rows, plan.half_lanes

    def run(name, kernel, shape, kind, operands):
        return call(name, kernel, jax.ShapeDtypeStruct(shape, kind), operands)

    part = functools.partial
    b16 = jnp.bfloat16
    shape = (2, rows, lanes)
    send0 = run("send0", part(send_kernel, plan, False), shape, b16, [acts, grads])
    come0 = swap(send0, sizes, *plan.term_masks[0])
    send1 = run("send1", part(send_kernel, plan, True), shape, b16, [after(acts, send0), grads])
    come1 = swap(send1, sizes, *plan.term_masks[0])
    keep0 = run("keep0", part(keep_kernel, plan, False), shape, f32, [after(acts, send1), grads])
    send = run("turn0", part(turn_kernel, plan, False), shape, b16, [keep0, come0])
    come = swap(send, sizes, *plan.term_masks[1])
    keep1 = run("keep1", part(keep_kernel, plan, True), shape, f32, [after(acts, send), grads])
    keep = run("turn1", part(turn_kernel, plan, True), shape, f32, [keep1, come1])
    packed, third, last0 = more_kernel(plan, packed, keep0, send, keep1)
    shape = shape[1:]
    send = run("part0", part(part_kernel, plan, False), shape, b16, [keep, come])
    last1 = swap(after(third, send), sizes, *plan.gather_masks[2])
    keep = run("part1", part(part_kernel, plan, True), shape, f32, [after(keep, send), come])
    come = swap(send, sizes, *plan.term_masks[2])
    if plan.rest_strip:
        keep = narrowed(plan, added(keep, come)[0])
        come = jnp.zeros(keep.shape, b16)
    for mask in plan.rest_band:
        rows //= 2
        shape = (rows, plan.lanes)
        halve = part(halve_kernel, plan, mask, plan.used)
        send = run("halve0", part(halve, False), shape, b16, [keep, come])
        keep = run("halve1", part(halve, True), shape, f32, [after(keep, send, last0), come])
        come = swap(send, sizes, (mask, 0))
    return keep, come, (after(packed, keep), third, last0, last1)


def edge_kernel(plan, grad, out, copy):
    strip = lax.axis_index("strip")
    for n in range(plan.images):
        out[n] = jnp.where(strip == 0, grad[n, plan.rows - 1], grad[n, 0])
    copy[...] = grad[...]


def borders(plan, grad):
    if plan.strips == 2:
        shape = jax.ShapeDtypeStruct((plan.images, plan.channels, plan.width), grad.dtype)
        copy = jax.ShapeDtypeStruct(grad.shape, grad.dtype)
        edge, grad = call("edge", functools.partial(edge_kernel, plan), (shape, copy), [grad])
        come = [swap(edge, plan.sizes, (core, 1)) for core in range(2)]
        return grad, come, come
    first, last = grad[:, 0], grad[:, plan.rows - 1]
    tops, bottoms = [], []
    for core in range(2):
        down = []
        for b in range(plan.bands):
            down += [(b * plan.strips + s, (b ^ core) * plan.strips + s + 1) for s in range(plan.strips - 1)]
        tops.append(lax.ppermute(last, AXES, down))
        bottoms.append(lax.ppermute(first, AXES, [(b, a) for a, b in down]))
    return grad, tops, bottoms


def body(activations, out_grad, kernel):
    images, channels, rows, width = activations.shape
    bands, strips = lax.axis_size("band"), lax.axis_size("strip")
    plan = Plan(images, channels, rows, width, bands, strips)
    scale = 1.0 / math.sqrt(images * bands * rows * strips * width)
    act = activations.transpose(0, 2, 1, 3)
    grad = out_grad.transpose(0, 2, 1, 3)
    grad0, tops, bottoms = borders(plan, grad)
    act1 = swap(act, plan.sizes, (1, 0))
    grad1 = swap(grad, plan.sizes, (1, 0))
    packed = first_kernel(plan, kernel.transpose(1, 0, 2))
    shape = (2, 2 * plan.part_rows, plan.cells)
    acts = call("acts", functools.partial(acts_kernel, plan), jax.ShapeDtypeStruct(shape, act.dtype), [act, act1])
    shape = (2, plan.half_lanes, plan.cells)
    grads = call(
        "grads",
        functools.partial(grads_kernel, plan),
        jax.ShapeDtypeStruct(shape, grad.dtype),
        [grad0, grad1, *tops, *bottoms],
    )
    keep, come, packed = kernel_terms(plan, acts, grads, packed)
    packed, third, last0, last1 = packed
    shape = jax.ShapeDtypeStruct((images, rows, plan.half // 2, width), jnp.bfloat16)
    rest = jax.ShapeDtypeStruct((len(TAP_STEPS) * plan.half // 2, plan.cells), jnp.float32)
    own0, given0, rest = call(
        "early", functools.partial(early_kernel, plan), (shape, shape, rest), [packed, third, last0, grads]
    )
    theirs0 = swap(given0, plan.sizes, (1, 0))
    left = jax.ShapeDtypeStruct((len(TAP_STEPS) * plan.half // 2, plan.half_lanes), jnp.bfloat16)
    given1, left = call("given", functools.partial(given_kernel, plan), (shape, left), [last1, grads, rest])
    theirs1 = swap(given1, plan.sizes, (1, 0))
    own1 = call("own", functools.partial(own_kernel, plan), shape, [after(left, given1), grads, rest])
    shape = (images, rows, channels, width)
    terms = (len(TAP_STEPS) ** 2, plan.depth, plan.cols)
    total = call(
        "last", functools.partial(last_kernel, plan, scale), jax.ShapeDtypeStruct(terms, jnp.float32), [keep, come]
    )
    input_grad, kernel_grad = call(
        "weave",
        functools.partial(weave_kernel, plan),
        (jax.ShapeDtypeStruct(shape, jnp.bfloat16), jax.ShapeDtypeStruct(terms, jnp.float32)),
        [own0, own1, theirs0, theirs1, total],
        [
            pltpu.VMEM(shape, jnp.bfloat16),
            pltpu.SemaphoreType.DMA((images, rows)),
            pltpu.SemaphoreType.DMA(()),
        ],
        far=2,
    )
    return input_grad.transpose(0, 2, 1, 3), kernel_grad.transpose(1, 0, 2)


def solution(mesh):
    in_specs = (
        P("band", None, "strip", None),
        P("band", None, "strip", None),
        P("band", None, "strip"),
    )
    out_specs = (P("band", None, "strip", None), P("band", None, "strip"))
    return jax.shard_map(body, mesh=mesh, in_specs=in_specs, out_specs=out_specs, check_vma=False)
```

```python
import functools
import math

import jax
import jax.numpy as jnp
from jax import lax
from jax.experimental import pallas as pl
from jax.experimental.pallas import tpu as pltpu
from jax.sharding import PartitionSpec as P

AXES = ("band", "strip")
TAP_STEPS = (-1, 0, 1)
LANES = 128
TOP_POWER = 2.0**15.5
LEAST_POWER = 2.0**-126
LEAST_PEAK = 1e-30
ROW_FIRST = False
VMEM_BYTES = 40 * 2**20
HINTS = {
    "edge": 8.0,
    "pair": 0.2,
    "pack": 8.0,
    "acts": 0.6,
    "grads": 0.5,
    "send0": 1.4,
    "send1": 1.4,
    "keep0": 1.0,
    "keep1": 1.0,
    "turn0": 0.9,
    "turn1": 0.6,
    "part0": 0.5,
    "part1": 0.3,
    "halve0": 0.5,
    "halve1": 3.0,
    "early": 1.7,
    "given": 0.5,
    "own": 0.5,
    "last": 8.0,
    "weave": 0.9,
}
FLOPS_PER_US = 1.15e9


def padded_lanes(count):
    return (count // LANES + 1) * LANES


def swap(value, sizes, *masks):
    bands, strips = sizes
    pairs = []
    for b in range(bands):
        for s in range(strips):
            masks_here = masks[b % len(masks)]
            pairs.append((b * strips + s, (b ^ masks_here[0]) * strips + (s ^ masks_here[1])))
    return lax.ppermute(value, AXES, pairs)


def call(name, kernel, out_shape, operands, scratch=(), far=0):
    outs = jax.tree.map(lambda _: pl.BlockSpec(memory_space=pltpu.VMEM), out_shape)
    if far:
        outs = outs[:-far] + (pl.BlockSpec(memory_space=pl.ANY),) * far
    return pl.pallas_call(
        kernel,
        out_shape=out_shape,
        in_specs=[pl.BlockSpec(memory_space=pltpu.VMEM)] * len(operands),
        out_specs=outs,
        scratch_shapes=list(scratch),
        compiler_params=pltpu.CompilerParams(vmem_limit_bytes=VMEM_BYTES),
        cost_estimate=pl.CostEstimate(
            flops=int(HINTS[name] * FLOPS_PER_US), bytes_accessed=0, transcendentals=0
        ),
        name=name,
    )(*operands)


def encoded(peak, value, used):
    lane = lax.broadcasted_iota(jnp.int32, value.shape, value.ndim - 1)
    ratio = value * (TOP_POWER / peak)
    square = ratio * ratio
    power = ratio * jnp.abs(ratio) * square * (square * square)
    return jnp.where(lane < used, power, peak).astype(jnp.bfloat16)


def decoded(message):
    power = message.astype(jnp.float32)
    peak = power[0:1, message.shape[1] - 1 : message.shape[1]]
    size = jnp.maximum(jnp.abs(power), LEAST_POWER)
    fourth = lax.rsqrt(lax.rsqrt(size))
    root = fourth * lax.rsqrt(fourth)
    return jnp.where(power < 0, -root, root) * (peak * (1.0 / TOP_POWER)), peak


def rounded_up(peak):
    return jnp.maximum(peak * (1.0 + 2.0**-6), LEAST_PEAK).astype(jnp.bfloat16).astype(jnp.float32)


def largest(value):
    return jnp.full((1, 1), jnp.max(jnp.abs(value)), jnp.float32)


def noted(peak, value, used):
    lane = lax.broadcasted_iota(jnp.int32, value.shape, value.ndim - 1)
    return jnp.where(lane < used, value, peak)


def added(keep, message):
    value, peak = decoded(message)
    return keep + value, peak + keep[0:1, keep.shape[1] - 1 : keep.shape[1]]


class Plan:
    def __init__(self, images, channels, rows, width, bands, strips):
        self.images, self.channels, self.rows, self.width = images, channels, rows, width
        self.bands, self.strips = bands, strips
        self.sizes = (bands, strips)
        self.depth = channels // bands
        self.cols = channels // strips
        self.blocks = bands // 2
        self.half = channels // 2
        self.strip_bits = strips.bit_length() - 1
        self.band_bits = bands.bit_length() - 1
        assert bands == 1 << self.band_bits and strips == 1 << self.strip_bits
        assert self.band_bits >= 3 and self.strip_bits >= 1
        self.top_strip = 1 << (self.strip_bits - 1)
        self.rest_strip = [1 << k for k in reversed(range(self.strip_bits - 1))]
        self.rest_band = [1 << k for k in range(3, self.band_bits)]
        self.inner = self.blocks // 4
        self.half_used = len(TAP_STEPS) * self.half
        self.half_lanes = padded_lanes(self.half_used)
        self.used = len(TAP_STEPS) * self.cols
        self.lanes = padded_lanes(self.used)
        self.block_rows = len(TAP_STEPS) * self.depth
        self.part_rows = self.inner * self.block_rows
        self.cells = 2 * images * rows * width
        by_row, by_next, by_col = (2, 0), (4, 0), (0, self.top_strip)
        self.term_masks = ((by_col, by_next), (by_row, by_col), (by_next, by_row))
        ones, others = (by_row, by_next) if ROW_FIRST else (by_next, by_row)
        self.gather_masks = ((ones, others), (others, by_col), (by_col, ones))

    def turned(self, slot):
        bits = self.band_bits - 3
        return sum(((slot >> k) & 1) << (bits - 1 - k) for k in range(bits))

    def block_of(self, slot, by_next, by_row):
        return self.turned(slot) * 4 + by_next * 2 + by_row

    def chunks(self):
        return [(d, n, h) for d in range(2) for n in range(self.images) for h in range(self.rows)]


def place(plan):
    band, strip = lax.axis_index("band"), lax.axis_index("strip")
    return band % 2, (band // 2) % 2, (band // 4) % 2, strip // plan.top_strip


def mine(plan):
    core, by_row, by_next, by_col = place(plan)
    order = ((by_col, by_row, by_next), (by_next, by_col, by_row))
    return [jnp.where(core == 0, a, b) for a, b in zip(*order)]


def grad_row(plan, grad_ref, top_ref, bottom_ref, image, row, start, strip):
    if row < 0:
        piece = top_ref[image, pl.ds(start, plan.half), :]
        return jnp.where(strip > 0, piece, jnp.zeros_like(piece))
    if row >= plan.rows:
        piece = bottom_ref[image, pl.ds(start, plan.half), :]
        return jnp.where(strip < plan.strips - 1, piece, jnp.zeros_like(piece))
    return grad_ref[image, row, pl.ds(start, plan.half), :]


def moved(value, step):
    width = value.shape[-1]
    if step == 0:
        return value
    lane = lax.broadcasted_iota(jnp.int32, value.shape, value.ndim - 1)
    turned = pltpu.roll(value, (-step) % width, value.ndim - 1)
    inside = lane < width - step if step > 0 else lane >= -step
    return jnp.where(inside, turned, 0.0)


def acts_kernel(plan, act0, act1, out):
    core = lax.axis_index("band") % 2
    depth, width = plan.depth, plan.width
    for at, (d, n, h) in enumerate(plan.chunks()):
        cells = (act0, act1)[d][n, h].astype(jnp.float32)
        shifted = []
        for m in range(plan.blocks):
            begin = 2 * m * depth
            even, odd = cells[begin : begin + depth], cells[begin + depth : begin + 2 * depth]
            block = jnp.where(core == 0, even, odd)
            shifted.append([moved(block, step) for step in TAP_STEPS])
        for i in range(2):
            pieces = []
            for j in range(2):
                for slot in range(plan.inner):
                    here, there = shifted[plan.block_of(slot, j, i)], shifted[plan.block_of(slot, i, j)]
                    pieces += here if i == j else [jnp.where(core == 0, a, b) for a, b in zip(here, there)]
            out[i, :, at * width : (at + 1) * width] = jnp.concatenate(pieces, axis=0).astype(jnp.bfloat16)


def grads_kernel(plan, grad0, grad1, top0, top1, bottom0, bottom1, out):
    strip = lax.axis_index("strip")
    half, width = plan.half, plan.width
    sources = ((grad0, top0, bottom0), (grad1, top1, bottom1))
    for at, (d, n, h) in enumerate(plan.chunks()):
        cells = slice(at * width, (at + 1) * width)
        for x in range(2):
            for r, row_step in enumerate(TAP_STEPS):
                out[x, r * half : (r + 1) * half, cells] = grad_row(
                    plan, *sources[d], n, h - row_step, x * half, strip
                )
            out[x, plan.half_used :, cells] = jnp.zeros((plan.half_lanes - plan.half_used, width), jnp.bfloat16)


def pair_terms(plan, acts, grads, first, second):
    core = lax.axis_index("band") % 2
    i, x = jnp.where(core == 0, second, first), jnp.where(core == 0, first, second)
    return lax.dot_general(acts[i], grads[x], (((1,), (1,)), ((), ())), preferred_element_type=jnp.float32)


def send_kernel(plan, same, acts, grads, out):
    first, second, _ = mine(plan)
    total = pair_terms(plan, acts, grads, 1 - first, second if same else 1 - second)
    for k in range(2):
        half = total[k * plan.part_rows : (k + 1) * plan.part_rows]
        out[k] = encoded(rounded_up(largest(half)), half, plan.half_used)


def keep_kernel(plan, same, acts, grads, out):
    first, second, _ = mine(plan)
    total = pair_terms(plan, acts, grads, first, second if same else 1 - second)
    for k in range(2):
        half = total[k * plan.part_rows : (k + 1) * plan.part_rows]
        out[k] = noted(largest(half), half, plan.half_used)


def turn_kernel(plan, same, keep, message, out):
    for k in range(2):
        total, peak = added(keep[k], message[k])
        out[k] = noted(peak, total, plan.half_used) if same else encoded(rounded_up(peak), total, plan.half_used)


def part_kernel(plan, same, keep, message, out):
    third = mine(plan)[2]
    k = third if same else 1 - third
    total, peak = added(keep[k], message[k])
    out[...] = noted(peak, total, plan.half_used) if same else encoded(rounded_up(peak), total, plan.half_used)


def halve_kernel(plan, mask, used, same, keep, message, out):
    side = (lax.axis_index("band") // mask) % 2
    total, peak = added(keep[...], message[...])
    rows = total.shape[0] // 2
    lower, upper = total[:rows], total[rows:]
    if same:
        out[...] = noted(peak, jnp.where(side == 0, lower, upper), used)
    else:
        out[...] = encoded(rounded_up(peak), jnp.where(side == 0, upper, lower), used)


def pack_kernel(plan, kernel, out):
    rows = []
    for c in range(len(TAP_STEPS)):
        pieces = [kernel[r * len(TAP_STEPS) + c].astype(jnp.float32) for r in range(len(TAP_STEPS))]
        pieces.append(jnp.zeros((plan.depth, plan.lanes - plan.used), jnp.float32))
        rows.append(jnp.concatenate(pieces, axis=1))
    out[...] = jnp.concatenate(rows, axis=0).astype(jnp.bfloat16)


def halves(plan):
    core, row_bit, next_bit, _ = place(plan)
    by_row = (core == 0) != ROW_FIRST
    return jnp.where(by_row, row_bit, next_bit), jnp.where(by_row, next_bit, row_bit)


def ordered(plan, blocks):
    rest = lax.axis_index("band") // 8
    other_bit = halves(plan)[1]
    parts = [jnp.where(other_bit == 0, blocks[k], blocks[1 - k]).astype(jnp.float32) for k in range(2)]
    rows = []
    for c in range(len(TAP_STEPS)):
        for k in range(plan.inner):
            for part in parts:
                piece = None
                for at in range(plan.inner):
                    begin = plan.turned(at) * plan.block_rows + c * plan.depth
                    here = part[begin : begin + plan.depth]
                    piece = here if piece is None else jnp.where((k ^ rest) == at, here, piece)
                rows.append(piece)
    return jnp.concatenate(rows, axis=0).astype(jnp.bfloat16)


def summed(plan, product):
    quarter = plan.half // 2
    total = None
    for c, col_step in enumerate(TAP_STEPS):
        term = moved(product[c * quarter : (c + 1) * quarter], -col_step)
        total = term if total is None else total + term
    return total.astype(jnp.bfloat16)


def groups(plan):
    rows = [(n, h) for n in range(plan.images) for h in range(plan.rows)]
    for d in range(2):
        for begin in range(0, len(rows), 2):
            part = rows[begin : begin + 2]
            at = (d * len(rows) + begin) * plan.width
            where = [(n, h, slice(k * plan.width, (k + 1) * plan.width)) for k, (n, h) in enumerate(part)]
            yield d, slice(at, at + len(part) * plan.width), where


def early_kernel(plan, own, third, last0, grads, out0, out1, rest):
    core, _, _, col = place(plan)
    near, far = ordered(plan, own), [ordered(plan, third), ordered(plan, last0)]
    beside = jnp.where(core == 0, far[1], far[0])
    below = jnp.where(core == 0, far[0], far[1])
    for d, cells, where in groups(plan):
        here, there = grads[col, :, cells], grads[1 - col, :, cells]
        product = jnp.dot(near, here, preferred_element_type=jnp.float32)
        product = product + jnp.dot(beside, there, preferred_element_type=jnp.float32)
        rest[:, cells] = jnp.dot(below, here, preferred_element_type=jnp.float32)
        for n, h, lanes in where:
            (out0, out1)[d][n, h] = summed(plan, product[:, lanes])


def late_of(plan, image, left, grads, rest, out):
    col = place(plan)[3]
    for d, cells, where in groups(plan):
        if d == image:
            product = rest[:, cells]
            product = product + jnp.dot(left, grads[1 - col, :, cells], preferred_element_type=jnp.float32)
            for n, h, lanes in where:
                out[n, h] = summed(plan, product[:, lanes])


def given_kernel(plan, last1, grads, rest, out, left):
    left[...] = ordered(plan, last1)
    late_of(plan, 1, left[...], grads, rest, out)


def own_kernel(plan, left, grads, rest, out):
    late_of(plan, 0, left[...], grads, rest, out)


def pack_kernel(plan, kernel, out):
    rows = []
    for c in range(len(TAP_STEPS)):
        pieces = [kernel[r * len(TAP_STEPS) + c].astype(jnp.float32) for r in range(len(TAP_STEPS))]
        pieces.append(jnp.zeros((plan.depth, plan.lanes - plan.used), jnp.float32))
        rows.append(jnp.concatenate(pieces, axis=1))
    out[...] = jnp.concatenate(rows, axis=0).astype(jnp.bfloat16)


def halves(plan):
    core, row_bit, next_bit, _ = place(plan)
    by_row = (core == 0) != ROW_FIRST
    return jnp.where(by_row, row_bit, next_bit), jnp.where(by_row, next_bit, row_bit)


def ordered(plan, blocks):
    rest = lax.axis_index("band") // 8
    other_bit = halves(plan)[1]
    parts = [jnp.where(other_bit == 0, blocks[k], blocks[1 - k]).astype(jnp.float32) for k in range(2)]
    rows = []
    for c in range(len(TAP_STEPS)):
        for k in range(plan.inner):
            for part in parts:
                piece = None
                for at in range(plan.inner):
                    begin = plan.turned(at) * plan.block_rows + c * plan.depth
                    here = part[begin : begin + plan.depth]
                    piece = here if piece is None else jnp.where((k ^ rest) == at, here, piece)
                rows.append(piece)
    return jnp.concatenate(rows, axis=0).astype(jnp.bfloat16)


def summed(plan, product):
    quarter = plan.half // 2
    total = None
    for c, col_step in enumerate(TAP_STEPS):
        term = moved(product[c * quarter : (c + 1) * quarter], -col_step)
        total = term if total is None else total + term
    return total.astype(jnp.bfloat16)


def groups(plan):
    rows = [(n, h) for n in range(plan.images) for h in range(plan.rows)]
    for d in range(2):
        for begin in range(0, len(rows), 2):
            part = rows[begin : begin + 2]
            at = (d * len(rows) + begin) * plan.width
            where = [(n, h, slice(k * plan.width, (k + 1) * plan.width)) for k, (n, h) in enumerate(part)]
            yield d, slice(at, at + len(part) * plan.width), where


def early_kernel(plan, own, third, last0, grads, out0, out1, rest):
    core, _, _, col = place(plan)
    near, far = ordered(plan, own), [ordered(plan, third), ordered(plan, last0)]
    beside = jnp.where(core == 0, far[1], far[0])
    below = jnp.where(core == 0, far[0], far[1])
    for d, cells, where in groups(plan):
        here, there = grads[col, :, cells], grads[1 - col, :, cells]
        product = jnp.dot(near, here, preferred_element_type=jnp.float32)
        product = product + jnp.dot(beside, there, preferred_element_type=jnp.float32)
        rest[:, cells] = jnp.dot(below, here, preferred_element_type=jnp.float32)
        for n, h, lanes in where:
            (out0, out1)[d][n, h] = summed(plan, product[:, lanes])


def late_of(plan, image, left, grads, rest, out):
    col = place(plan)[3]
    for d, cells, where in groups(plan):
        if d == image:
            product = rest[:, cells]
            product = product + jnp.dot(left, grads[1 - col, :, cells], preferred_element_type=jnp.float32)
            for n, h, lanes in where:
                out[n, h] = summed(plan, product[:, lanes])


def given_kernel(plan, last1, grads, rest, out, left):
    left[...] = ordered(plan, last1)
    late_of(plan, 1, left[...], grads, rest, out)


def own_kernel(plan, left, grads, rest, out):
    late_of(plan, 0, left[...], grads, rest, out)


def last_kernel(plan, scale, keep, message, out):
    total = added(keep[...], message[...])[0] * scale
    depth, cols = plan.depth, plan.cols
    for r in range(len(TAP_STEPS)):
        for c in range(len(TAP_STEPS)):
            out[r * len(TAP_STEPS) + c] = total[c * depth : (c + 1) * depth, r * cols : (r + 1) * cols]


def last_kernel(plan, scale, keep, message, out):
    total = added(keep[...], message[...])[0] * scale
    depth, cols = plan.depth, plan.cols
    for r in range(len(TAP_STEPS)):
        for c in range(len(TAP_STEPS)):
            out[r * len(TAP_STEPS) + c] = total[c * depth : (c + 1) * depth, r * cols : (r + 1) * cols]


def weave_kernel(plan, own0, own1, theirs0, theirs1, terms, far, far_terms, out, sems, sem):
    copies = [pltpu.make_async_copy(terms, far_terms, sem)]
    copies[0].start()
    core, row_bit, next_bit, _ = place(plan)
    depth = plan.depth
    for n in range(plan.images):
        for h in range(plan.rows):
            mine = [ref[n, h].astype(jnp.float32) for ref in (own0, own1)]
            others = [ref[n, h].astype(jnp.float32) for ref in (theirs0, theirs1)]
            pieces = []
            for m in range(plan.blocks):
                for p in range(2):
                    by_row = (p == 0) != ROW_FIRST
                    bit, other, ours = (m % 2, m // 2 % 2, row_bit) if by_row else (m // 2 % 2, m % 2, next_bit)
                    at = slice((m // 4 * 2 + other) * depth, (m // 4 * 2 + other + 1) * depth)
                    a = jnp.where(bit == ours, mine[0][at], mine[1][at])
                    b = jnp.where(bit == ours, others[0][at], others[1][at])
                    pieces.append(jnp.where(core == p, a, b))
            out[n, h] = jnp.concatenate(pieces, axis=0).astype(jnp.bfloat16)
            copies.append(pltpu.make_async_copy(out.at[n, h], far.at[n, h], sems.at[n, h]))
            copies[-1].start()
    for copy in copies:
        copy.wait()


def after(value, *others):
    return lax.optimization_barrier((value, *others))[0]


def pair_kernel(plan, *refs):
    blocks = [ref[k].astype(jnp.float32) for ref in refs[:-1] for k in range(ref.shape[0])]
    refs[-1][0] = jnp.concatenate(blocks, axis=0).astype(jnp.bfloat16)


def first_kernel(plan, kernel):
    shape = jax.ShapeDtypeStruct((plan.block_rows, plan.lanes), jnp.bfloat16)
    packed = call("pack", functools.partial(pack_kernel, plan), shape, [kernel])[None]
    for mask in plan.rest_band[:0:-1]:
        packed = jnp.concatenate([packed, swap(packed, plan.sizes, (mask, 0))], axis=0)
    return [packed] + [swap(packed, plan.sizes, (mask, 0)) for mask in plan.rest_band[:1]]


def more_kernel(plan, packed, start, end, last):
    sizes = plan.sizes
    packed = [*packed[:-1], after(packed[-1], start)]
    if plan.rest_strip:
        packed = jnp.concatenate(packed, axis=0)[None]
        for mask in reversed(plan.rest_strip):
            packed = jnp.concatenate([packed, swap(packed, sizes, (0, mask))], axis=0)
        count = packed.shape[0]
        order = jnp.arange(count) ^ (lax.axis_index("strip") % count)
        packed = jnp.take(packed, order, axis=0)[..., : plan.used]
        packed = packed.reshape(count, plan.inner, plan.block_rows, len(TAP_STEPS), plan.cols)
        packed = packed.transpose(1, 2, 3, 0, 4).reshape(plan.inner, plan.block_rows, plan.half_used)
        packed = [jnp.pad(packed, ((0, 0), (0, 0), (0, plan.half_lanes - plan.half_used)))]
    shape = jax.ShapeDtypeStruct((1, plan.part_rows, plan.half_lanes), jnp.bfloat16)
    packed = after(call("pair", functools.partial(pair_kernel, plan), shape, packed), start)
    come = after(swap(packed, sizes, *plan.gather_masks[0]), end)
    packed = after(jnp.concatenate([packed, come], axis=0), end)
    third = swap(packed, sizes, *plan.gather_masks[1])
    return packed, third, swap(after(packed, last), sizes, *plan.gather_masks[2])


def narrowed(plan, total):
    rows = total.shape[0]
    total = total[:, : plan.half_used].reshape(rows, len(TAP_STEPS), plan.half)
    for mask in plan.rest_strip:
        side = (lax.axis_index("strip") // mask) % 2
        parts = total.reshape(rows, len(TAP_STEPS), 2, total.shape[2] // 2)
        kept = jnp.where(side == 0, parts[:, :, 0], parts[:, :, 1])
        given = jnp.where(side == 0, parts[:, :, 1], parts[:, :, 0])
        total = kept + swap(given, plan.sizes, (0, mask))
    total = total.reshape(rows, plan.used)
    return noted(largest(total), jnp.pad(total, ((0, 0), (0, plan.lanes - plan.used))), plan.used)


def kernel_terms(plan, acts, grads, packed):
    sizes, f32 = plan.sizes, jnp.float32
    rows, lanes = plan.part_rows, plan.half_lanes

    def run(name, kernel, shape, kind, operands):
        return call(name, kernel, jax.ShapeDtypeStruct(shape, kind), operands)

    part = functools.partial
    b16 = jnp.bfloat16
    shape = (2, rows, lanes)
    send0 = run("send0", part(send_kernel, plan, False), shape, b16, [acts, grads])
    come0 = swap(send0, sizes, *plan.term_masks[0])
    send1 = run("send1", part(send_kernel, plan, True), shape, b16, [after(acts, send0), grads])
    come1 = swap(send1, sizes, *plan.term_masks[0])
    keep0 = run("keep0", part(keep_kernel, plan, False), shape, f32, [after(acts, send1), grads])
    send = run("turn0", part(turn_kernel, plan, False), shape, b16, [keep0, come0])
    come = swap(send, sizes, *plan.term_masks[1])
    keep1 = run("keep1", part(keep_kernel, plan, True), shape, f32, [after(acts, send), grads])
    keep = run("turn1", part(turn_kernel, plan, True), shape, f32, [keep1, come1])
    packed, third, last0 = more_kernel(plan, packed, keep0, send, keep1)
    shape = shape[1:]
    send = run("part0", part(part_kernel, plan, False), shape, b16, [keep, come])
    last1 = swap(after(third, send), sizes, *plan.gather_masks[2])
    keep = run("part1", part(part_kernel, plan, True), shape, f32, [after(keep, send), come])
    come = swap(send, sizes, *plan.term_masks[2])
    if plan.rest_strip:
        keep = narrowed(plan, added(keep, come)[0])
        come = jnp.zeros(keep.shape, b16)
    for mask in plan.rest_band:
        rows //= 2
        shape = (rows, plan.lanes)
        halve = part(halve_kernel, plan, mask, plan.used)
        send = run("halve0", part(halve, False), shape, b16, [keep, come])
        keep = run("halve1", part(halve, True), shape, f32, [after(keep, send, last0), come])
        come = swap(send, sizes, (mask, 0))
    return keep, come, (after(packed, keep), third, last0, last1)


def edge_kernel(plan, grad, out, copy):
    strip = lax.axis_index("strip")
    for n in range(plan.images):
        out[n] = jnp.where(strip == 0, grad[n, plan.rows - 1], grad[n, 0])
    copy[...] = grad[...]


def borders(plan, grad):
    if plan.strips == 2:
        shape = jax.ShapeDtypeStruct((plan.images, plan.channels, plan.width), grad.dtype)
        copy = jax.ShapeDtypeStruct(grad.shape, grad.dtype)
        edge, grad = call("edge", functools.partial(edge_kernel, plan), (shape, copy), [grad])
        come = [swap(edge, plan.sizes, (core, 1)) for core in range(2)]
        return grad, come, come
    first, last = grad[:, 0], grad[:, plan.rows - 1]
    tops, bottoms = [], []
    for core in range(2):
        down = []
        for b in range(plan.bands):
            down += [(b * plan.strips + s, (b ^ core) * plan.strips + s + 1) for s in range(plan.strips - 1)]
        tops.append(lax.ppermute(last, AXES, down))
        bottoms.append(lax.ppermute(first, AXES, [(b, a) for a, b in down]))
    return grad, tops, bottoms


def body(activations, out_grad, kernel):
    images, channels, rows, width = activations.shape
    bands, strips = lax.axis_size("band"), lax.axis_size("strip")
    plan = Plan(images, channels, rows, width, bands, strips)
    scale = 1.0 / math.sqrt(images * bands * rows * strips * width)
    act = activations.transpose(0, 2, 1, 3)
    grad = out_grad.transpose(0, 2, 1, 3)
    grad0, tops, bottoms = borders(plan, grad)
    act1 = swap(act, plan.sizes, (1, 0))
    grad1 = swap(grad, plan.sizes, (1, 0))
    packed = first_kernel(plan, kernel.transpose(1, 0, 2))
    shape = (2, 2 * plan.part_rows, plan.cells)
    acts = call("acts", functools.partial(acts_kernel, plan), jax.ShapeDtypeStruct(shape, act.dtype), [act, act1])
    shape = (2, plan.half_lanes, plan.cells)
    grads = call(
        "grads",
        functools.partial(grads_kernel, plan),
        jax.ShapeDtypeStruct(shape, grad.dtype),
        [grad0, grad1, *tops, *bottoms],
    )
    keep, come, packed = kernel_terms(plan, acts, grads, packed)
    packed, third, last0, last1 = packed
    shape = jax.ShapeDtypeStruct((images, rows, plan.half // 2, width), jnp.bfloat16)
    rest = jax.ShapeDtypeStruct((len(TAP_STEPS) * plan.half // 2, plan.cells), jnp.float32)
    own0, given0, rest = call(
        "early", functools.partial(early_kernel, plan), (shape, shape, rest), [packed, third, last0, grads]
    )
    theirs0 = swap(given0, plan.sizes, (1, 0))
    left = jax.ShapeDtypeStruct((len(TAP_STEPS) * plan.half // 2, plan.half_lanes), jnp.bfloat16)
    given1, left = call("given", functools.partial(given_kernel, plan), (shape, left), [last1, grads, rest])
    theirs1 = swap(given1, plan.sizes, (1, 0))
    own1 = call("own", functools.partial(own_kernel, plan), shape, [after(left, given1), grads, rest])
    shape = (images, rows, channels, width)
    terms = (len(TAP_STEPS) ** 2, plan.depth, plan.cols)
    total = call(
        "last", functools.partial(last_kernel, plan, scale), jax.ShapeDtypeStruct(terms, jnp.float32), [keep, come]
    )
    input_grad, kernel_grad = call(
        "weave",
        functools.partial(weave_kernel, plan),
        (jax.ShapeDtypeStruct(shape, jnp.bfloat16), jax.ShapeDtypeStruct(terms, jnp.float32)),
        [own0, own1, theirs0, theirs1, total],
        [
            pltpu.VMEM(shape, jnp.bfloat16),
            pltpu.SemaphoreType.DMA((images, rows)),
            pltpu.SemaphoreType.DMA(()),
        ],
        far=2,
    )
    return input_grad.transpose(0, 2, 1, 3), kernel_grad.transpose(1, 0, 2)


def solution(mesh):
    in_specs = (
        P("band", None, "strip", None),
        P("band", None, "strip", None),
        P("band", None, "strip"),
    )
    out_specs = (P("band", None, "strip", None), P("band", None, "strip"))
    return jax.shard_map(body, mesh=mesh, in_specs=in_specs, out_specs=out_specs, check_vma=False)
```

```python
import functools
import math

import jax
import jax.numpy as jnp
from jax import lax
from jax.experimental import pallas as pl
from jax.experimental.pallas import tpu as pltpu
from jax.sharding import PartitionSpec as P

AXES = ("band", "strip")
TAP_STEPS = (-1, 0, 1)
LANES = 128
TOP_POWER = 2.0**15.5
LEAST_POWER = 2.0**-126
LEAST_PEAK = 1e-30
ROW_FIRST = False
VMEM_BYTES = 40 * 2**20
HINTS = {
    "edge": 8.0,
    "pair": 0.2,
    "pack": 8.0,
    "acts": 0.6,
    "grads": 0.5,
    "send0": 1.4,
    "send1": 1.4,
    "keep0": 1.0,
    "keep1": 1.0,
    "turn0": 0.9,
    "turn1": 0.6,
    "part0": 0.5,
    "part1": 0.3,
    "halve0": 0.5,
    "halve1": 3.0,
    "early": 1.7,
    "given": 0.5,
    "own": 0.5,
    "last": 8.0,
    "weave": 0.9,
}
FLOPS_PER_US = 1.15e9


def padded_lanes(count):
    return (count // LANES + 1) * LANES


def swap(value, sizes, *masks):
    bands, strips = sizes
    pairs = []
    for b in range(bands):
        for s in range(strips):
            masks_here = masks[b % len(masks)]
            pairs.append((b * strips + s, (b ^ masks_here[0]) * strips + (s ^ masks_here[1])))
    return lax.ppermute(value, AXES, pairs)


def call(name, kernel, out_shape, operands, scratch=(), far=0):
    outs = jax.tree.map(lambda _: pl.BlockSpec(memory_space=pltpu.VMEM), out_shape)
    if far:
        outs = outs[:-far] + (pl.BlockSpec(memory_space=pl.ANY),) * far
    return pl.pallas_call(
        kernel,
        out_shape=out_shape,
        in_specs=[pl.BlockSpec(memory_space=pltpu.VMEM)] * len(operands),
        out_specs=outs,
        scratch_shapes=list(scratch),
        compiler_params=pltpu.CompilerParams(vmem_limit_bytes=VMEM_BYTES),
        cost_estimate=pl.CostEstimate(
            flops=int(HINTS[name] * FLOPS_PER_US), bytes_accessed=0, transcendentals=0
        ),
        name=name,
    )(*operands)


def encoded(peak, value, used):
    lane = lax.broadcasted_iota(jnp.int32, value.shape, value.ndim - 1)
    ratio = value * (TOP_POWER / peak)
    square = ratio * ratio
    power = ratio * jnp.abs(ratio) * square * (square * square)
    return jnp.where(lane < used, power, peak).astype(jnp.bfloat16)


def decoded(message):
    power = message.astype(jnp.float32)
    peak = power[0:1, message.shape[1] - 1 : message.shape[1]]
    size = jnp.maximum(jnp.abs(power), LEAST_POWER)
    fourth = lax.rsqrt(lax.rsqrt(size))
    root = fourth * lax.rsqrt(fourth)
    return jnp.where(power < 0, -root, root) * (peak * (1.0 / TOP_POWER)), peak


def rounded_up(peak):
    return jnp.maximum(peak * (1.0 + 2.0**-6), LEAST_PEAK).astype(jnp.bfloat16).astype(jnp.float32)


def largest(value):
    return jnp.full((1, 1), jnp.max(jnp.abs(value)), jnp.float32)


def noted(peak, value, used):
    lane = lax.broadcasted_iota(jnp.int32, value.shape, value.ndim - 1)
    return jnp.where(lane < used, value, peak)


def added(keep, message):
    value, peak = decoded(message)
    return keep + value, peak + keep[0:1, keep.shape[1] - 1 : keep.shape[1]]


class Plan:
    def __init__(self, images, channels, rows, width, bands, strips):
        self.images, self.channels, self.rows, self.width = images, channels, rows, width
        self.bands, self.strips = bands, strips
        self.sizes = (bands, strips)
        self.depth = channels // bands
        self.cols = channels // strips
        self.blocks = bands // 2
        self.half = channels // 2
        self.strip_bits = strips.bit_length() - 1
        self.band_bits = bands.bit_length() - 1
        assert bands == 1 << self.band_bits and strips == 1 << self.strip_bits
        assert self.band_bits >= 3 and self.strip_bits >= 1
        self.top_strip = 1 << (self.strip_bits - 1)
        self.rest_strip = [1 << k for k in reversed(range(self.strip_bits - 1))]
        self.rest_band = [1 << k for k in range(3, self.band_bits)]
        self.inner = self.blocks // 4
        self.half_used = len(TAP_STEPS) * self.half
        self.half_lanes = padded_lanes(self.half_used)
        self.used = len(TAP_STEPS) * self.cols
        self.lanes = padded_lanes(self.used)
        self.block_rows = len(TAP_STEPS) * self.depth
        self.part_rows = self.inner * self.block_rows
        self.cells = 2 * images * rows * width
        by_row, by_next, by_col = (2, 0), (4, 0), (0, self.top_strip)
        self.term_masks = ((by_col, by_next), (by_row, by_col), (by_next, by_row))
        ones, others = (by_row, by_next) if ROW_FIRST else (by_next, by_row)
        self.gather_masks = ((ones, others), (others, by_col), (by_col, ones))

    def turned(self, slot):
        bits = self.band_bits - 3
        return sum(((slot >> k) & 1) << (bits - 1 - k) for k in range(bits))

    def block_of(self, slot, by_next, by_row):
        return self.turned(slot) * 4 + by_next * 2 + by_row

    def chunks(self):
        return [(d, n, h) for d in range(2) for n in range(self.images) for h in range(self.rows)]


def place(plan):
    band, strip = lax.axis_index("band"), lax.axis_index("strip")
    return band % 2, (band // 2) % 2, (band // 4) % 2, strip // plan.top_strip


def mine(plan):
    core, by_row, by_next, by_col = place(plan)
    order = ((by_col, by_row, by_next), (by_next, by_col, by_row))
    return [jnp.where(core == 0, a, b) for a, b in zip(*order)]


def grad_row(plan, grad_ref, top_ref, bottom_ref, image, row, start, strip):
    if row < 0:
        piece = top_ref[image, pl.ds(start, plan.half), :]
        return jnp.where(strip > 0, piece, jnp.zeros_like(piece))
    if row >= plan.rows:
        piece = bottom_ref[image, pl.ds(start, plan.half), :]
        return jnp.where(strip < plan.strips - 1, piece, jnp.zeros_like(piece))
    return grad_ref[image, row, pl.ds(start, plan.half), :]


def moved(value, step):
    width = value.shape[-1]
    if step == 0:
        return value
    lane = lax.broadcasted_iota(jnp.int32, value.shape, value.ndim - 1)
    turned = pltpu.roll(value, (-step) % width, value.ndim - 1)
    inside = lane < width - step if step > 0 else lane >= -step
    return jnp.where(inside, turned, 0.0)


def acts_kernel(plan, act0, act1, out):
    core = lax.axis_index("band") % 2
    depth, width = plan.depth, plan.width
    for at, (d, n, h) in enumerate(plan.chunks()):
        cells = (act0, act1)[d][n, h].astype(jnp.float32)
        shifted = []
        for m in range(plan.blocks):
            begin = 2 * m * depth
            even, odd = cells[begin : begin + depth], cells[begin + depth : begin + 2 * depth]
            block = jnp.where(core == 0, even, odd)
            shifted.append([moved(block, step) for step in TAP_STEPS])
        for i in range(2):
            pieces = []
            for j in range(2):
                for slot in range(plan.inner):
                    here, there = shifted[plan.block_of(slot, j, i)], shifted[plan.block_of(slot, i, j)]
                    pieces += here if i == j else [jnp.where(core == 0, a, b) for a, b in zip(here, there)]
            out[i, :, at * width : (at + 1) * width] = jnp.concatenate(pieces, axis=0).astype(jnp.bfloat16)


def grads_kernel(plan, grad0, grad1, top0, top1, bottom0, bottom1, out):
    strip = lax.axis_index("strip")
    half, width = plan.half, plan.width
    sources = ((grad0, top0, bottom0), (grad1, top1, bottom1))
    for at, (d, n, h) in enumerate(plan.chunks()):
        cells = slice(at * width, (at + 1) * width)
        for x in range(2):
            for r, row_step in enumerate(TAP_STEPS):
                out[x, r * half : (r + 1) * half, cells] = grad_row(
                    plan, *sources[d], n, h - row_step, x * half, strip
                )
            out[x, plan.half_used :, cells] = jnp.zeros((plan.half_lanes - plan.half_used, width), jnp.bfloat16)


def pair_terms(plan, acts, grads, first, second):
    core = lax.axis_index("band") % 2
    i, x = jnp.where(core == 0, second, first), jnp.where(core == 0, first, second)
    return lax.dot_general(acts[i], grads[x], (((1,), (1,)), ((), ())), preferred_element_type=jnp.float32)


def send_kernel(plan, same, acts, grads, out):
    first, second, _ = mine(plan)
    total = pair_terms(plan, acts, grads, 1 - first, second if same else 1 - second)
    for k in range(2):
        half = total[k * plan.part_rows : (k + 1) * plan.part_rows]
        out[k] = encoded(rounded_up(largest(half)), half, plan.half_used)


def keep_kernel(plan, same, acts, grads, out):
    first, second, _ = mine(plan)
    total = pair_terms(plan, acts, grads, first, second if same else 1 - second)
    for k in range(2):
        half = total[k * plan.part_rows : (k + 1) * plan.part_rows]
        out[k] = noted(largest(half), half, plan.half_used)


def turn_kernel(plan, same, keep, message, out):
    for k in range(2):
        total, peak = added(keep[k], message[k])
        out[k] = noted(peak, total, plan.half_used) if same else encoded(rounded_up(peak), total, plan.half_used)


def part_kernel(plan, same, keep, message, out):
    third = mine(plan)[2]
    k = third if same else 1 - third
    total, peak = added(keep[k], message[k])
    out[...] = noted(peak, total, plan.half_used) if same else encoded(rounded_up(peak), total, plan.half_used)


def halve_kernel(plan, mask, used, same, keep, message, out):
    side = (lax.axis_index("band") // mask) % 2
    total, peak = added(keep[...], message[...])
    rows = total.shape[0] // 2
    lower, upper = total[:rows], total[rows:]
    if same:
        out[...] = noted(peak, jnp.where(side == 0, lower, upper), used)
    else:
        out[...] = encoded(rounded_up(peak), jnp.where(side == 0, upper, lower), used)


def pack_kernel(plan, kernel, out):
    rows = []
    for c in range(len(TAP_STEPS)):
        pieces = [kernel[r * len(TAP_STEPS) + c].astype(jnp.float32) for r in range(len(TAP_STEPS))]
        pieces.append(jnp.zeros((plan.depth, plan.lanes - plan.used), jnp.float32))
        rows.append(jnp.concatenate(pieces, axis=1))
    out[...] = jnp.concatenate(rows, axis=0).astype(jnp.bfloat16)


def halves(plan):
    core, row_bit, next_bit, _ = place(plan)
    by_row = (core == 0) != ROW_FIRST
    return jnp.where(by_row, row_bit, next_bit), jnp.where(by_row, next_bit, row_bit)


def ordered(plan, blocks):
    rest = lax.axis_index("band") // 8
    other_bit = halves(plan)[1]
    parts = [jnp.where(other_bit == 0, blocks[k], blocks[1 - k]).astype(jnp.float32) for k in range(2)]
    rows = []
    for c in range(len(TAP_STEPS)):
        for k in range(plan.inner):
            for part in parts:
                piece = None
                for at in range(plan.inner):
                    begin = plan.turned(at) * plan.block_rows + c * plan.depth
                    here = part[begin : begin + plan.depth]
                    piece = here if piece is None else jnp.where((k ^ rest) == at, here, piece)
                rows.append(piece)
    return jnp.concatenate(rows, axis=0).astype(jnp.bfloat16)


def summed(plan, product):
    quarter = plan.half // 2
    total = None
    for c, col_step in enumerate(TAP_STEPS):
        term = moved(product[c * quarter : (c + 1) * quarter], -col_step)
        total = term if total is None else total + term
    return total.astype(jnp.bfloat16)


def groups(plan):
    rows = [(n, h) for n in range(plan.images) for h in range(plan.rows)]
    for d in range(2):
        for begin in range(0, len(rows), 2):
            part = rows[begin : begin + 2]
            at = (d * len(rows) + begin) * plan.width
            where = [(n, h, slice(k * plan.width, (k + 1) * plan.width)) for k, (n, h) in enumerate(part)]
            yield d, slice(at, at + len(part) * plan.width), where


def early_kernel(plan, own, third, last0, grads, out0, out1, rest):
    core, _, _, col = place(plan)
    near, far = ordered(plan, own), [ordered(plan, third), ordered(plan, last0)]
    beside = jnp.where(core == 0, far[1], far[0])
    below = jnp.where(core == 0, far[0], far[1])
    for d, cells, where in groups(plan):
        here, there = grads[col, :, cells], grads[1 - col, :, cells]
        product = jnp.dot(near, here, preferred_element_type=jnp.float32)
        product = product + jnp.dot(beside, there, preferred_element_type=jnp.float32)
        rest[:, cells] = jnp.dot(below, here, preferred_element_type=jnp.float32)
        for n, h, lanes in where:
            (out0, out1)[d][n, h] = summed(plan, product[:, lanes])


def late_of(plan, image, left, grads, rest, out):
    col = place(plan)[3]
    for d, cells, where in groups(plan):
        if d == image:
            product = rest[:, cells]
            product = product + jnp.dot(left, grads[1 - col, :, cells], preferred_element_type=jnp.float32)
            for n, h, lanes in where:
                out[n, h] = summed(plan, product[:, lanes])


def given_kernel(plan, last1, grads, rest, out, left):
    left[...] = ordered(plan, last1)
    late_of(plan, 1, left[...], grads, rest, out)


def own_kernel(plan, left, grads, rest, out):
    late_of(plan, 0, left[...], grads, rest, out)


def pack_kernel(plan, kernel, out):
    rows = []
    for c in range(len(TAP_STEPS)):
        pieces = [kernel[r * len(TAP_STEPS) + c].astype(jnp.float32) for r in range(len(TAP_STEPS))]
        pieces.append(jnp.zeros((plan.depth, plan.lanes - plan.used), jnp.float32))
        rows.append(jnp.concatenate(pieces, axis=1))
    out[...] = jnp.concatenate(rows, axis=0).astype(jnp.bfloat16)


def halves(plan):
    core, row_bit, next_bit, _ = place(plan)
    by_row = (core == 0) != ROW_FIRST
    return jnp.where(by_row, row_bit, next_bit), jnp.where(by_row, next_bit, row_bit)


def ordered(plan, blocks):
    rest = lax.axis_index("band") // 8
    other_bit = halves(plan)[1]
    parts = [jnp.where(other_bit == 0, blocks[k], blocks[1 - k]).astype(jnp.float32) for k in range(2)]
    rows = []
    for c in range(len(TAP_STEPS)):
        for k in range(plan.inner):
            for part in parts:
                piece = None
                for at in range(plan.inner):
                    begin = plan.turned(at) * plan.block_rows + c * plan.depth
                    here = part[begin : begin + plan.depth]
                    piece = here if piece is None else jnp.where((k ^ rest) == at, here, piece)
                rows.append(piece)
    return jnp.concatenate(rows, axis=0).astype(jnp.bfloat16)


def summed(plan, product):
    quarter = plan.half // 2
    total = None
    for c, col_step in enumerate(TAP_STEPS):
        term = moved(product[c * quarter : (c + 1) * quarter], -col_step)
        total = term if total is None else total + term
    return total.astype(jnp.bfloat16)


def groups(plan):
    rows = [(n, h) for n in range(plan.images) for h in range(plan.rows)]
    for d in range(2):
        for begin in range(0, len(rows), 2):
            part = rows[begin : begin + 2]
            at = (d * len(rows) + begin) * plan.width
            where = [(n, h, slice(k * plan.width, (k + 1) * plan.width)) for k, (n, h) in enumerate(part)]
            yield d, slice(at, at + len(part) * plan.width), where


def early_kernel(plan, own, third, last0, grads, out0, out1, rest):
    core, _, _, col = place(plan)
    near, far = ordered(plan, own), [ordered(plan, third), ordered(plan, last0)]
    beside = jnp.where(core == 0, far[1], far[0])
    below = jnp.where(core == 0, far[0], far[1])
    for d, cells, where in groups(plan):
        here, there = grads[col, :, cells], grads[1 - col, :, cells]
        product = jnp.dot(near, here, preferred_element_type=jnp.float32)
        product = product + jnp.dot(beside, there, preferred_element_type=jnp.float32)
        rest[:, cells] = jnp.dot(below, here, preferred_element_type=jnp.float32)
        for n, h, lanes in where:
            (out0, out1)[d][n, h] = summed(plan, product[:, lanes])


def late_of(plan, image, left, grads, rest, out):
    col = place(plan)[3]
    for d, cells, where in groups(plan):
        if d == image:
            product = rest[:, cells]
            product = product + jnp.dot(left, grads[1 - col, :, cells], preferred_element_type=jnp.float32)
            for n, h, lanes in where:
                out[n, h] = summed(plan, product[:, lanes])


def given_kernel(plan, last1, grads, rest, out, left):
    left[...] = ordered(plan, last1)
    late_of(plan, 1, left[...], grads, rest, out)


def own_kernel(plan, left, grads, rest, out):
    late_of(plan, 0, left[...], grads, rest, out)


def last_kernel(plan, scale, keep, message, out):
    total = added(keep[...], message[...])[0] * scale
    depth, cols = plan.depth, plan.cols
    for r in range(len(TAP_STEPS)):
        for c in range(len(TAP_STEPS)):
            out[r * len(TAP_STEPS) + c] = total[c * depth : (c + 1) * depth, r * cols : (r + 1) * cols]


def last_kernel(plan, scale, keep, message, out):
    total = added(keep[...], message[...])[0] * scale
    depth, cols = plan.depth, plan.cols
    for r in range(len(TAP_STEPS)):
        for c in range(len(TAP_STEPS)):
            out[r * len(TAP_STEPS) + c] = total[c * depth : (c + 1) * depth, r * cols : (r + 1) * cols]


def weave_kernel(plan, own0, own1, theirs0, theirs1, terms, far, far_terms, out, sems, sem):
    copies = [pltpu.make_async_copy(terms, far_terms, sem)]
    copies[0].start()
    core, row_bit, next_bit, _ = place(plan)
    depth = plan.depth
    for n in range(plan.images):
        for h in range(plan.rows):
            mine = [ref[n, h].astype(jnp.float32) for ref in (own0, own1)]
            others = [ref[n, h].astype(jnp.float32) for ref in (theirs0, theirs1)]
            pieces = []
            for m in range(plan.blocks):
                for p in range(2):
                    by_row = (p == 0) != ROW_FIRST
                    bit, other, ours = (m % 2, m // 2 % 2, row_bit) if by_row else (m // 2 % 2, m % 2, next_bit)
                    at = slice((m // 4 * 2 + other) * depth, (m // 4 * 2 + other + 1) * depth)
                    a = jnp.where(bit == ours, mine[0][at], mine[1][at])
                    b = jnp.where(bit == ours, others[0][at], others[1][at])
                    pieces.append(jnp.where(core == p, a, b))
            out[n, h] = jnp.concatenate(pieces, axis=0).astype(jnp.bfloat16)
            copies.append(pltpu.make_async_copy(out.at[n, h], far.at[n, h], sems.at[n, h]))
            copies[-1].start()
    for copy in copies:
        copy.wait()


def after(value, *others):
    return lax.optimization_barrier((value, *others))[0]


def pair_kernel(plan, *refs):
    blocks = [ref[k].astype(jnp.float32) for ref in refs[:-1] for k in range(ref.shape[0])]
    refs[-1][0] = jnp.concatenate(blocks, axis=0).astype(jnp.bfloat16)


def first_kernel(plan, kernel):
    shape = jax.ShapeDtypeStruct((plan.block_rows, plan.lanes), jnp.bfloat16)
    packed = call("pack", functools.partial(pack_kernel, plan), shape, [kernel])[None]
    for mask in plan.rest_band[:0:-1]:
        packed = jnp.concatenate([packed, swap(packed, plan.sizes, (mask, 0))], axis=0)
    return [packed] + [swap(packed, plan.sizes, (mask, 0)) for mask in plan.rest_band[:1]]


def more_kernel(plan, packed, start, end, last):
    sizes = plan.sizes
    packed = [*packed[:-1], after(packed[-1], start)]
    if plan.rest_strip:
        packed = jnp.concatenate(packed, axis=0)[None]
        for mask in reversed(plan.rest_strip):
            packed = jnp.concatenate([packed, swap(packed, sizes, (0, mask))], axis=0)
        count = packed.shape[0]
        order = jnp.arange(count) ^ (lax.axis_index("strip") % count)
        packed = jnp.take(packed, order, axis=0)[..., : plan.used]
        packed = packed.reshape(count, plan.inner, plan.block_rows, len(TAP_STEPS), plan.cols)
        packed = packed.transpose(1, 2, 3, 0, 4).reshape(plan.inner, plan.block_rows, plan.half_used)
        packed = [jnp.pad(packed, ((0, 0), (0, 0), (0, plan.half_lanes - plan.half_used)))]
    shape = jax.ShapeDtypeStruct((1, plan.part_rows, plan.half_lanes), jnp.bfloat16)
    packed = after(call("pair", functools.partial(pair_kernel, plan), shape, packed), start)
    come = after(swap(packed, sizes, *plan.gather_masks[0]), end)
    packed = after(jnp.concatenate([packed, come], axis=0), end)
    third = swap(packed, sizes, *plan.gather_masks[1])
    return packed, third, swap(after(packed, last), sizes, *plan.gather_masks[2])


def narrowed(plan, total):
    rows = total.shape[0]
    total = total[:, : plan.half_used].reshape(rows, len(TAP_STEPS), plan.half)
    for mask in plan.rest_strip:
        side = (lax.axis_index("strip") // mask) % 2
        parts = total.reshape(rows, len(TAP_STEPS), 2, total.shape[2] // 2)
        kept = jnp.where(side == 0, parts[:, :, 0], parts[:, :, 1])
        given = jnp.where(side == 0, parts[:, :, 1], parts[:, :, 0])
        total = kept + swap(given, plan.sizes, (0, mask))
    total = total.reshape(rows, plan.used)
    return noted(largest(total), jnp.pad(total, ((0, 0), (0, plan.lanes - plan.used))), plan.used)


def kernel_terms(plan, acts, grads, packed):
    sizes, f32 = plan.sizes, jnp.float32
    rows, lanes = plan.part_rows, plan.half_lanes

    def run(name, kernel, shape, kind, operands):
        return call(name, kernel, jax.ShapeDtypeStruct(shape, kind), operands)

    part = functools.partial
    b16 = jnp.bfloat16
    shape = (2, rows, lanes)
    send0 = run("send0", part(send_kernel, plan, False), shape, b16, [acts, grads])
    come0 = swap(send0, sizes, *plan.term_masks[0])
    send1 = run("send1", part(send_kernel, plan, True), shape, b16, [after(acts, send0), grads])
    come1 = swap(send1, sizes, *plan.term_masks[0])
    keep0 = run("keep0", part(keep_kernel, plan, False), shape, f32, [after(acts, send1), grads])
    send = run("turn0", part(turn_kernel, plan, False), shape, b16, [keep0, come0])
    come = swap(send, sizes, *plan.term_masks[1])
    keep1 = run("keep1", part(keep_kernel, plan, True), shape, f32, [after(acts, send), grads])
    keep = run("turn1", part(turn_kernel, plan, True), shape, f32, [keep1, come1])
    packed, third, last0 = more_kernel(plan, packed, keep0, send, keep1)
    shape = shape[1:]
    send = run("part0", part(part_kernel, plan, False), shape, b16, [keep, come])
    last1 = swap(after(third, send), sizes, *plan.gather_masks[2])
    keep = run("part1", part(part_kernel, plan, True), shape, f32, [after(keep, send), come])
    come = swap(send, sizes, *plan.term_masks[2])
    if plan.rest_strip:
        keep = narrowed(plan, added(keep, come)[0])
        come = jnp.zeros(keep.shape, b16)
    for mask in plan.rest_band:
        rows //= 2
        shape = (rows, plan.lanes)
        halve = part(halve_kernel, plan, mask, plan.used)
        send = run("halve0", part(halve, False), shape, b16, [keep, come])
        keep = run("halve1", part(halve, True), shape, f32, [after(keep, send, last0), come])
        come = swap(send, sizes, (mask, 0))
    return keep, come, (after(packed, keep), third, last0, last1)


def edge_kernel(plan, grad, out, copy):
    strip = lax.axis_index("strip")
    for n in range(plan.images):
        out[n] = jnp.where(strip == 0, grad[n, plan.rows - 1], grad[n, 0])
    copy[...] = grad[...]


def borders(plan, grad):
    if plan.strips == 2:
        shape = jax.ShapeDtypeStruct((plan.images, plan.channels, plan.width), grad.dtype)
        copy = jax.ShapeDtypeStruct(grad.shape, grad.dtype)
        edge, grad = call("edge", functools.partial(edge_kernel, plan), (shape, copy), [grad])
        come = [swap(edge, plan.sizes, (core, 1)) for core in range(2)]
        return grad, come, come
    first, last = grad[:, 0], grad[:, plan.rows - 1]
    tops, bottoms = [], []
    for core in range(2):
        down = []
        for b in range(plan.bands):
            down += [(b * plan.strips + s, (b ^ core) * plan.strips + s + 1) for s in range(plan.strips - 1)]
        tops.append(lax.ppermute(last, AXES, down))
        bottoms.append(lax.ppermute(first, AXES, [(b, a) for a, b in down]))
    return grad, tops, bottoms


def body(activations, out_grad, kernel):
    images, channels, rows, width = activations.shape
    bands, strips = lax.axis_size("band"), lax.axis_size("strip")
    plan = Plan(images, channels, rows, width, bands, strips)
    scale = 1.0 / math.sqrt(images * bands * rows * strips * width)
    act = activations.transpose(0, 2, 1, 3)
    grad = out_grad.transpose(0, 2, 1, 3)
    grad0, tops, bottoms = borders(plan, grad)
    act1 = swap(act, plan.sizes, (1, 0))
    grad1 = swap(grad, plan.sizes, (1, 0))
    packed = first_kernel(plan, kernel.transpose(1, 0, 2))
    shape = (2, 2 * plan.part_rows, plan.cells)
    acts = call("acts", functools.partial(acts_kernel, plan), jax.ShapeDtypeStruct(shape, act.dtype), [act, act1])
    shape = (2, plan.half_lanes, plan.cells)
    grads = call(
        "grads",
        functools.partial(grads_kernel, plan),
        jax.ShapeDtypeStruct(shape, grad.dtype),
        [grad0, grad1, *tops, *bottoms],
    )
    keep, come, packed = kernel_terms(plan, acts, grads, packed)
    packed, third, last0, last1 = packed
    shape = jax.ShapeDtypeStruct((images, rows, plan.half // 2, width), jnp.bfloat16)
    rest = jax.ShapeDtypeStruct((len(TAP_STEPS) * plan.half // 2, plan.cells), jnp.float32)
    own0, given0, rest = call(
        "early", functools.partial(early_kernel, plan), (shape, shape, rest), [packed, third, last0, grads]
    )
    theirs0 = swap(given0, plan.sizes, (1, 0))
    left = jax.ShapeDtypeStruct((len(TAP_STEPS) * plan.half // 2, plan.half_lanes), jnp.bfloat16)
    given1, left = call("given", functools.partial(given_kernel, plan), (shape, left), [last1, grads, rest])
    theirs1 = swap(given1, plan.sizes, (1, 0))
    own1 = call("own", functools.partial(own_kernel, plan), shape, [after(left, given1), grads, rest])
    shape = (images, rows, channels, width)
    terms = (len(TAP_STEPS) ** 2, plan.depth, plan.cols)
    total = call(
        "last", functools.partial(last_kernel, plan, scale), jax.ShapeDtypeStruct(terms, jnp.float32), [after(keep, own1), come]
    )
    input_grad, kernel_grad = call(
        "weave",
        functools.partial(weave_kernel, plan),
        (jax.ShapeDtypeStruct(shape, jnp.bfloat16), jax.ShapeDtypeStruct(terms, jnp.float32)),
        [own0, own1, theirs0, theirs1, total],
        [
            pltpu.VMEM(shape, jnp.bfloat16),
            pltpu.SemaphoreType.DMA((images, rows)),
            pltpu.SemaphoreType.DMA(()),
        ],
        far=2,
    )
    return input_grad.transpose(0, 2, 1, 3), kernel_grad.transpose(1, 0, 2)


def solution(mesh):
    in_specs = (
        P("band", None, "strip", None),
        P("band", None, "strip", None),
        P("band", None, "strip"),
    )
    out_specs = (P("band", None, "strip", None), P("band", None, "strip"))
    return jax.shard_map(body, mesh=mesh, in_specs=in_specs, out_specs=out_specs, check_vma=False)
```

```python
import functools
import math

import jax
import jax.numpy as jnp
from jax import lax
from jax.experimental import pallas as pl
from jax.experimental.pallas import tpu as pltpu
from jax.sharding import PartitionSpec as P

AXES = ("band", "strip")
TAP_STEPS = (-1, 0, 1)
LANES = 128
TOP_POWER = 2.0**15.5
LEAST_POWER = 2.0**-126
LEAST_PEAK = 1e-30
ROW_FIRST = False
VMEM_BYTES = 40 * 2**20
HINTS = {
    "edge": 8.0,
    "pair": 0.2,
    "pack": 8.0,
    "acts": 0.6,
    "grads": 0.5,
    "send0": 1.4,
    "send1": 1.4,
    "keep0": 1.0,
    "keep1": 1.0,
    "turn0": 0.9,
    "turn1": 0.6,
    "part0": 0.5,
    "part1": 0.3,
    "halve0": 0.5,
    "halve1": 3.0,
    "early": 1.7,
    "given": 0.5,
    "own": 0.5,
    "last": 8.0,
    "weave": 0.9,
}
FLOPS_PER_US = 1.15e9


def padded_lanes(count):
    return (count // LANES + 1) * LANES


def swap(value, sizes, *masks):
    bands, strips = sizes
    pairs = []
    for b in range(bands):
        for s in range(strips):
            masks_here = masks[b % len(masks)]
            pairs.append((b * strips + s, (b ^ masks_here[0]) * strips + (s ^ masks_here[1])))
    return lax.ppermute(value, AXES, pairs)


def call(name, kernel, out_shape, operands, scratch=(), far=0):
    outs = jax.tree.map(lambda _: pl.BlockSpec(memory_space=pltpu.VMEM), out_shape)
    if far:
        outs = outs[:-far] + (pl.BlockSpec(memory_space=pl.ANY),) * far
    return pl.pallas_call(
        kernel,
        out_shape=out_shape,
        in_specs=[pl.BlockSpec(memory_space=pltpu.VMEM)] * len(operands),
        out_specs=outs,
        scratch_shapes=list(scratch),
        compiler_params=pltpu.CompilerParams(vmem_limit_bytes=VMEM_BYTES),
        cost_estimate=pl.CostEstimate(
            flops=int(HINTS[name] * FLOPS_PER_US), bytes_accessed=0, transcendentals=0
        ),
        name=name,
    )(*operands)


def encoded(peak, value, used):
    lane = lax.broadcasted_iota(jnp.int32, value.shape, value.ndim - 1)
    ratio = value * (TOP_POWER / peak)
    square = ratio * ratio
    power = ratio * jnp.abs(ratio) * square * (square * square)
    return jnp.where(lane < used, power, peak).astype(jnp.bfloat16)


def decoded(message):
    power = message.astype(jnp.float32)
    peak = power[0:1, message.shape[1] - 1 : message.shape[1]]
    size = jnp.maximum(jnp.abs(power), LEAST_POWER)
    fourth = lax.rsqrt(lax.rsqrt(size))
    root = fourth * lax.rsqrt(fourth)
    return jnp.where(power < 0, -root, root) * (peak * (1.0 / TOP_POWER)), peak


def rounded_up(peak):
    return jnp.maximum(peak * (1.0 + 2.0**-6), LEAST_PEAK).astype(jnp.bfloat16).astype(jnp.float32)


def largest(value):
    return jnp.full((1, 1), jnp.max(jnp.abs(value)), jnp.float32)


def noted(peak, value, used):
    lane = lax.broadcasted_iota(jnp.int32, value.shape, value.ndim - 1)
    return jnp.where(lane < used, value, peak)


def added(keep, message):
    value, peak = decoded(message)
    return keep + value, peak + keep[0:1, keep.shape[1] - 1 : keep.shape[1]]


class Plan:
    def __init__(self, images, channels, rows, width, bands, strips):
        self.images, self.channels, self.rows, self.width = images, channels, rows, width
        self.bands, self.strips = bands, strips
        self.sizes = (bands, strips)
        self.depth = channels // bands
        self.cols = channels // strips
        self.blocks = bands // 2
        self.half = channels // 2
        self.strip_bits = strips.bit_length() - 1
        self.band_bits = bands.bit_length() - 1
        assert bands == 1 << self.band_bits and strips == 1 << self.strip_bits
        assert self.band_bits >= 3 and self.strip_bits >= 1
        self.top_strip = 1 << (self.strip_bits - 1)
        self.rest_strip = [1 << k for k in reversed(range(self.strip_bits - 1))]
        self.rest_band = [1 << k for k in range(3, self.band_bits)]
        self.inner = self.blocks // 4
        self.half_used = len(TAP_STEPS) * self.half
        self.half_lanes = padded_lanes(self.half_used)
        self.used = len(TAP_STEPS) * self.cols
        self.lanes = padded_lanes(self.used)
        self.block_rows = len(TAP_STEPS) * self.depth
        self.part_rows = self.inner * self.block_rows
        self.cells = 2 * images * rows * width
        by_row, by_next, by_col = (2, 0), (4, 0), (0, self.top_strip)
        self.term_masks = ((by_col, by_next), (by_row, by_col), (by_next, by_row))
        ones, others = (by_row, by_next) if ROW_FIRST else (by_next, by_row)
        self.gather_masks = ((ones, others), (others, by_col), (by_col, ones))

    def turned(self, slot):
        bits = self.band_bits - 3
        return sum(((slot >> k) & 1) << (bits - 1 - k) for k in range(bits))

    def block_of(self, slot, by_next, by_row):
        return self.turned(slot) * 4 + by_next * 2 + by_row

    def chunks(self):
        return [(d, n, h) for d in range(2) for n in range(self.images) for h in range(self.rows)]


def place(plan):
    band, strip = lax.axis_index("band"), lax.axis_index("strip")
    return band % 2, (band // 2) % 2, (band // 4) % 2, strip // plan.top_strip


def mine(plan):
    core, by_row, by_next, by_col = place(plan)
    order = ((by_col, by_row, by_next), (by_next, by_col, by_row))
    return [jnp.where(core == 0, a, b) for a, b in zip(*order)]


def grad_row(plan, grad_ref, top_ref, bottom_ref, image, row, start, strip):
    if row < 0:
        piece = top_ref[image, pl.ds(start, plan.half), :]
        return jnp.where(strip > 0, piece, jnp.zeros_like(piece))
    if row >= plan.rows:
        piece = bottom_ref[image, pl.ds(start, plan.half), :]
        return jnp.where(strip < plan.strips - 1, piece, jnp.zeros_like(piece))
    return grad_ref[image, row, pl.ds(start, plan.half), :]


def moved(value, step):
    width = value.shape[-1]
    if step == 0:
        return value
    lane = lax.broadcasted_iota(jnp.int32, value.shape, value.ndim - 1)
    turned = pltpu.roll(value, (-step) % width, value.ndim - 1)
    inside = lane < width - step if step > 0 else lane >= -step
    return jnp.where(inside, turned, 0.0)


def acts_kernel(plan, act0, act1, out):
    core = lax.axis_index("band") % 2
    depth, width = plan.depth, plan.width
    for at, (d, n, h) in enumerate(plan.chunks()):
        cells = (act0, act1)[d][n, h].astype(jnp.float32)
        shifted = []
        for m in range(plan.blocks):
            begin = 2 * m * depth
            even, odd = cells[begin : begin + depth], cells[begin + depth : begin + 2 * depth]
            block = jnp.where(core == 0, even, odd)
            shifted.append([moved(block, step) for step in TAP_STEPS])
        for i in range(2):
            pieces = []
            for j in range(2):
                for slot in range(plan.inner):
                    here, there = shifted[plan.block_of(slot, j, i)], shifted[plan.block_of(slot, i, j)]
                    pieces += here if i == j else [jnp.where(core == 0, a, b) for a, b in zip(here, there)]
            out[i, :, at * width : (at + 1) * width] = jnp.concatenate(pieces, axis=0).astype(jnp.bfloat16)


def grads_kernel(plan, grad0, grad1, top0, top1, bottom0, bottom1, out):
    strip = lax.axis_index("strip")
    half, width = plan.half, plan.width
    sources = ((grad0, top0, bottom0), (grad1, top1, bottom1))
    for at, (d, n, h) in enumerate(plan.chunks()):
        cells = slice(at * width, (at + 1) * width)
        for x in range(2):
            for r, row_step in enumerate(TAP_STEPS):
                out[x, r * half : (r + 1) * half, cells] = grad_row(
                    plan, *sources[d], n, h - row_step, x * half, strip
                )
            out[x, plan.half_used :, cells] = jnp.zeros((plan.half_lanes - plan.half_used, width), jnp.bfloat16)


def pair_terms(plan, acts, grads, first, second):
    core = lax.axis_index("band") % 2
    i, x = jnp.where(core == 0, second, first), jnp.where(core == 0, first, second)
    return lax.dot_general(acts[i], grads[x], (((1,), (1,)), ((), ())), preferred_element_type=jnp.float32)


def send_kernel(plan, same, acts, grads, out):
    first, second, _ = mine(plan)
    total = pair_terms(plan, acts, grads, 1 - first, second if same else 1 - second)
    peak = rounded_up(largest(total))
    for k in range(2):
        out[k] = encoded(peak, total[k * plan.part_rows : (k + 1) * plan.part_rows], plan.half_used)


def keep_kernel(plan, same, acts, grads, out):
    first, second, _ = mine(plan)
    total = pair_terms(plan, acts, grads, first, second if same else 1 - second)
    peak = largest(total)
    for k in range(2):
        out[k] = noted(peak, total[k * plan.part_rows : (k + 1) * plan.part_rows], plan.half_used)


def turn_kernel(plan, same, keep, message, out):
    for k in range(2):
        total, peak = added(keep[k], message[k])
        out[k] = noted(peak, total, plan.half_used) if same else encoded(rounded_up(peak), total, plan.half_used)


def part_kernel(plan, same, keep, message, out):
    third = mine(plan)[2]
    k = third if same else 1 - third
    total, peak = added(keep[k], message[k])
    out[...] = noted(peak, total, plan.half_used) if same else encoded(rounded_up(peak), total, plan.half_used)


def halve_kernel(plan, mask, used, same, keep, message, out):
    side = (lax.axis_index("band") // mask) % 2
    total, peak = added(keep[...], message[...])
    rows = total.shape[0] // 2
    lower, upper = total[:rows], total[rows:]
    if same:
        out[...] = noted(peak, jnp.where(side == 0, lower, upper), used)
    else:
        out[...] = encoded(rounded_up(peak), jnp.where(side == 0, upper, lower), used)


def pack_kernel(plan, kernel, out):
    rows = []
    for c in range(len(TAP_STEPS)):
        pieces = [kernel[r * len(TAP_STEPS) + c].astype(jnp.float32) for r in range(len(TAP_STEPS))]
        pieces.append(jnp.zeros((plan.depth, plan.lanes - plan.used), jnp.float32))
        rows.append(jnp.concatenate(pieces, axis=1))
    out[...] = jnp.concatenate(rows, axis=0).astype(jnp.bfloat16)


def halves(plan):
    core, row_bit, next_bit, _ = place(plan)
    by_row = (core == 0) != ROW_FIRST
    return jnp.where(by_row, row_bit, next_bit), jnp.where(by_row, next_bit, row_bit)


def ordered(plan, blocks):
    rest = lax.axis_index("band") // 8
    other_bit = halves(plan)[1]
    parts = [jnp.where(other_bit == 0, blocks[k], blocks[1 - k]).astype(jnp.float32) for k in range(2)]
    rows = []
    for c in range(len(TAP_STEPS)):
        for k in range(plan.inner):
            for part in parts:
                piece = None
                for at in range(plan.inner):
                    begin = plan.turned(at) * plan.block_rows + c * plan.depth
                    here = part[begin : begin + plan.depth]
                    piece = here if piece is None else jnp.where((k ^ rest) == at, here, piece)
                rows.append(piece)
    return jnp.concatenate(rows, axis=0).astype(jnp.bfloat16)


def summed(plan, product):
    quarter = plan.half // 2
    total = None
    for c, col_step in enumerate(TAP_STEPS):
        term = moved(product[c * quarter : (c + 1) * quarter], -col_step)
        total = term if total is None else total + term
    return total.astype(jnp.bfloat16)


def groups(plan):
    rows = [(n, h) for n in range(plan.images) for h in range(plan.rows)]
    for d in range(2):
        for begin in range(0, len(rows), 2):
            part = rows[begin : begin + 2]
            at = (d * len(rows) + begin) * plan.width
            where = [(n, h, slice(k * plan.width, (k + 1) * plan.width)) for k, (n, h) in enumerate(part)]
            yield d, slice(at, at + len(part) * plan.width), where


def early_kernel(plan, own, third, last0, grads, out0, out1, rest):
    core, _, _, col = place(plan)
    near, far = ordered(plan, own), [ordered(plan, third), ordered(plan, last0)]
    beside = jnp.where(core == 0, far[1], far[0])
    below = jnp.where(core == 0, far[0], far[1])
    for d, cells, where in groups(plan):
        here, there = grads[col, :, cells], grads[1 - col, :, cells]
        product = jnp.dot(near, here, preferred_element_type=jnp.float32)
        product = product + jnp.dot(beside, there, preferred_element_type=jnp.float32)
        rest[:, cells] = jnp.dot(below, here, preferred_element_type=jnp.float32)
        for n, h, lanes in where:
            (out0, out1)[d][n, h] = summed(plan, product[:, lanes])


def late_of(plan, image, left, grads, rest, out):
    col = place(plan)[3]
    for d, cells, where in groups(plan):
        if d == image:
            product = rest[:, cells]
            product = product + jnp.dot(left, grads[1 - col, :, cells], preferred_element_type=jnp.float32)
            for n, h, lanes in where:
                out[n, h] = summed(plan, product[:, lanes])


def given_kernel(plan, last1, grads, rest, out, left):
    left[...] = ordered(plan, last1)
    late_of(plan, 1, left[...], grads, rest, out)


def own_kernel(plan, left, grads, rest, out):
    late_of(plan, 0, left[...], grads, rest, out)


def pack_kernel(plan, kernel, out):
    rows = []
    for c in range(len(TAP_STEPS)):
        pieces = [kernel[r * len(TAP_STEPS) + c].astype(jnp.float32) for r in range(len(TAP_STEPS))]
        pieces.append(jnp.zeros((plan.depth, plan.lanes - plan.used), jnp.float32))
        rows.append(jnp.concatenate(pieces, axis=1))
    out[...] = jnp.concatenate(rows, axis=0).astype(jnp.bfloat16)


def halves(plan):
    core, row_bit, next_bit, _ = place(plan)
    by_row = (core == 0) != ROW_FIRST
    return jnp.where(by_row, row_bit, next_bit), jnp.where(by_row, next_bit, row_bit)


def ordered(plan, blocks):
    rest = lax.axis_index("band") // 8
    other_bit = halves(plan)[1]
    parts = [jnp.where(other_bit == 0, blocks[k], blocks[1 - k]).astype(jnp.float32) for k in range(2)]
    rows = []
    for c in range(len(TAP_STEPS)):
        for k in range(plan.inner):
            for part in parts:
                piece = None
                for at in range(plan.inner):
                    begin = plan.turned(at) * plan.block_rows + c * plan.depth
                    here = part[begin : begin + plan.depth]
                    piece = here if piece is None else jnp.where((k ^ rest) == at, here, piece)
                rows.append(piece)
    return jnp.concatenate(rows, axis=0).astype(jnp.bfloat16)


def summed(plan, product):
    quarter = plan.half // 2
    total = None
    for c, col_step in enumerate(TAP_STEPS):
        term = moved(product[c * quarter : (c + 1) * quarter], -col_step)
        total = term if total is None else total + term
    return total.astype(jnp.bfloat16)


def groups(plan):
    rows = [(n, h) for n in range(plan.images) for h in range(plan.rows)]
    for d in range(2):
        for begin in range(0, len(rows), 2):
            part = rows[begin : begin + 2]
            at = (d * len(rows) + begin) * plan.width
            where = [(n, h, slice(k * plan.width, (k + 1) * plan.width)) for k, (n, h) in enumerate(part)]
            yield d, slice(at, at + len(part) * plan.width), where


def early_kernel(plan, own, third, last0, grads, out0, out1, rest):
    core, _, _, col = place(plan)
    near, far = ordered(plan, own), [ordered(plan, third), ordered(plan, last0)]
    beside = jnp.where(core == 0, far[1], far[0])
    below = jnp.where(core == 0, far[0], far[1])
    for d, cells, where in groups(plan):
        here, there = grads[col, :, cells], grads[1 - col, :, cells]
        product = jnp.dot(near, here, preferred_element_type=jnp.float32)
        product = product + jnp.dot(beside, there, preferred_element_type=jnp.float32)
        rest[:, cells] = jnp.dot(below, here, preferred_element_type=jnp.float32)
        for n, h, lanes in where:
            (out0, out1)[d][n, h] = summed(plan, product[:, lanes])


def late_of(plan, image, left, grads, rest, out):
    col = place(plan)[3]
    for d, cells, where in groups(plan):
        if d == image:
            product = rest[:, cells]
            product = product + jnp.dot(left, grads[1 - col, :, cells], preferred_element_type=jnp.float32)
            for n, h, lanes in where:
                out[n, h] = summed(plan, product[:, lanes])


def given_kernel(plan, last1, grads, rest, out, left):
    left[...] = ordered(plan, last1)
    late_of(plan, 1, left[...], grads, rest, out)


def own_kernel(plan, left, grads, rest, out):
    late_of(plan, 0, left[...], grads, rest, out)


def last_kernel(plan, scale, keep, message, out):
    total = added(keep[...], message[...])[0] * scale
    depth, cols = plan.depth, plan.cols
    for r in range(len(TAP_STEPS)):
        for c in range(len(TAP_STEPS)):
            out[r * len(TAP_STEPS) + c] = total[c * depth : (c + 1) * depth, r * cols : (r + 1) * cols]


def last_kernel(plan, scale, keep, message, out):
    total = added(keep[...], message[...])[0] * scale
    depth, cols = plan.depth, plan.cols
    for r in range(len(TAP_STEPS)):
        for c in range(len(TAP_STEPS)):
            out[r * len(TAP_STEPS) + c] = total[c * depth : (c + 1) * depth, r * cols : (r + 1) * cols]


def weave_kernel(plan, own0, own1, theirs0, theirs1, terms, far, far_terms, out, sems, sem):
    copies = [pltpu.make_async_copy(terms, far_terms, sem)]
    copies[0].start()
    core, row_bit, next_bit, _ = place(plan)
    depth = plan.depth
    for n in range(plan.images):
        for h in range(plan.rows):
            mine = [ref[n, h].astype(jnp.float32) for ref in (own0, own1)]
            others = [ref[n, h].astype(jnp.float32) for ref in (theirs0, theirs1)]
            pieces = []
            for m in range(plan.blocks):
                for p in range(2):
                    by_row = (p == 0) != ROW_FIRST
                    bit, other, ours = (m % 2, m // 2 % 2, row_bit) if by_row else (m // 2 % 2, m % 2, next_bit)
                    at = slice((m // 4 * 2 + other) * depth, (m // 4 * 2 + other + 1) * depth)
                    a = jnp.where(bit == ours, mine[0][at], mine[1][at])
                    b = jnp.where(bit == ours, others[0][at], others[1][at])
                    pieces.append(jnp.where(core == p, a, b))
            out[n, h] = jnp.concatenate(pieces, axis=0).astype(jnp.bfloat16)
            copies.append(pltpu.make_async_copy(out.at[n, h], far.at[n, h], sems.at[n, h]))
            copies[-1].start()
    for copy in copies:
        copy.wait()


def after(value, *others):
    return lax.optimization_barrier((value, *others))[0]


def pair_kernel(plan, *refs):
    blocks = [ref[k].astype(jnp.float32) for ref in refs[:-1] for k in range(ref.shape[0])]
    refs[-1][0] = jnp.concatenate(blocks, axis=0).astype(jnp.bfloat16)


def first_kernel(plan, kernel):
    shape = jax.ShapeDtypeStruct((plan.block_rows, plan.lanes), jnp.bfloat16)
    packed = call("pack", functools.partial(pack_kernel, plan), shape, [kernel])[None]
    for mask in plan.rest_band[:0:-1]:
        packed = jnp.concatenate([packed, swap(packed, plan.sizes, (mask, 0))], axis=0)
    return [packed] + [swap(packed, plan.sizes, (mask, 0)) for mask in plan.rest_band[:1]]


def more_kernel(plan, packed, start, end, last):
    sizes = plan.sizes
    packed = [*packed[:-1], after(packed[-1], start)]
    if plan.rest_strip:
        packed = jnp.concatenate(packed, axis=0)[None]
        for mask in reversed(plan.rest_strip):
            packed = jnp.concatenate([packed, swap(packed, sizes, (0, mask))], axis=0)
        count = packed.shape[0]
        order = jnp.arange(count) ^ (lax.axis_index("strip") % count)
        packed = jnp.take(packed, order, axis=0)[..., : plan.used]
        packed = packed.reshape(count, plan.inner, plan.block_rows, len(TAP_STEPS), plan.cols)
        packed = packed.transpose(1, 2, 3, 0, 4).reshape(plan.inner, plan.block_rows, plan.half_used)
        packed = [jnp.pad(packed, ((0, 0), (0, 0), (0, plan.half_lanes - plan.half_used)))]
    shape = jax.ShapeDtypeStruct((1, plan.part_rows, plan.half_lanes), jnp.bfloat16)
    packed = after(call("pair", functools.partial(pair_kernel, plan), shape, packed), start)
    come = after(swap(packed, sizes, *plan.gather_masks[0]), end)
    packed = after(jnp.concatenate([packed, come], axis=0), end)
    third = swap(packed, sizes, *plan.gather_masks[1])
    return packed, third, swap(after(packed, last), sizes, *plan.gather_masks[2])


def narrowed(plan, total):
    rows = total.shape[0]
    total = total[:, : plan.half_used].reshape(rows, len(TAP_STEPS), plan.half)
    for mask in plan.rest_strip:
        side = (lax.axis_index("strip") // mask) % 2
        parts = total.reshape(rows, len(TAP_STEPS), 2, total.shape[2] // 2)
        kept = jnp.where(side == 0, parts[:, :, 0], parts[:, :, 1])
        given = jnp.where(side == 0, parts[:, :, 1], parts[:, :, 0])
        total = kept + swap(given, plan.sizes, (0, mask))
    total = total.reshape(rows, plan.used)
    return noted(largest(total), jnp.pad(total, ((0, 0), (0, plan.lanes - plan.used))), plan.used)


def kernel_terms(plan, acts, grads, packed):
    sizes, f32 = plan.sizes, jnp.float32
    rows, lanes = plan.part_rows, plan.half_lanes

    def run(name, kernel, shape, kind, operands):
        return call(name, kernel, jax.ShapeDtypeStruct(shape, kind), operands)

    part = functools.partial
    b16 = jnp.bfloat16
    shape = (2, rows, lanes)
    send0 = run("send0", part(send_kernel, plan, False), shape, b16, [acts, grads])
    come0 = swap(send0, sizes, *plan.term_masks[0])
    send1 = run("send1", part(send_kernel, plan, True), shape, b16, [after(acts, send0), grads])
    come1 = swap(send1, sizes, *plan.term_masks[0])
    keep0 = run("keep0", part(keep_kernel, plan, False), shape, f32, [after(acts, send1), grads])
    send = run("turn0", part(turn_kernel, plan, False), shape, b16, [keep0, come0])
    come = swap(send, sizes, *plan.term_masks[1])
    keep1 = run("keep1", part(keep_kernel, plan, True), shape, f32, [after(acts, send), grads])
    keep = run("turn1", part(turn_kernel, plan, True), shape, f32, [keep1, come1])
    packed, third, last0 = more_kernel(plan, packed, keep0, send, keep1)
    shape = shape[1:]
    send = run("part0", part(part_kernel, plan, False), shape, b16, [keep, come])
    last1 = swap(after(third, send), sizes, *plan.gather_masks[2])
    keep = run("part1", part(part_kernel, plan, True), shape, f32, [after(keep, send), come])
    come = swap(send, sizes, *plan.term_masks[2])
    if plan.rest_strip:
        keep = narrowed(plan, added(keep, come)[0])
        come = jnp.zeros(keep.shape, b16)
    for mask in plan.rest_band:
        rows //= 2
        shape = (rows, plan.lanes)
        halve = part(halve_kernel, plan, mask, plan.used)
        send = run("halve0", part(halve, False), shape, b16, [keep, come])
        keep = run("halve1", part(halve, True), shape, f32, [after(keep, send, last0), come])
        come = swap(send, sizes, (mask, 0))
    return keep, come, (after(packed, keep), third, last0, last1)


def edge_kernel(plan, grad, out, copy):
    strip = lax.axis_index("strip")
    for n in range(plan.images):
        out[n] = jnp.where(strip == 0, grad[n, plan.rows - 1], grad[n, 0])
    copy[...] = grad[...]


def borders(plan, grad):
    if plan.strips == 2:
        shape = jax.ShapeDtypeStruct((plan.images, plan.channels, plan.width), grad.dtype)
        copy = jax.ShapeDtypeStruct(grad.shape, grad.dtype)
        edge, grad = call("edge", functools.partial(edge_kernel, plan), (shape, copy), [grad])
        come = [swap(edge, plan.sizes, (core, 1)) for core in range(2)]
        return grad, come, come
    first, last = grad[:, 0], grad[:, plan.rows - 1]
    tops, bottoms = [], []
    for core in range(2):
        down = []
        for b in range(plan.bands):
            down += [(b * plan.strips + s, (b ^ core) * plan.strips + s + 1) for s in range(plan.strips - 1)]
        tops.append(lax.ppermute(last, AXES, down))
        bottoms.append(lax.ppermute(first, AXES, [(b, a) for a, b in down]))
    return grad, tops, bottoms


def body(activations, out_grad, kernel):
    images, channels, rows, width = activations.shape
    bands, strips = lax.axis_size("band"), lax.axis_size("strip")
    plan = Plan(images, channels, rows, width, bands, strips)
    scale = 1.0 / math.sqrt(images * bands * rows * strips * width)
    act = activations.transpose(0, 2, 1, 3)
    grad = out_grad.transpose(0, 2, 1, 3)
    grad0, tops, bottoms = borders(plan, grad)
    act1 = swap(act, plan.sizes, (1, 0))
    grad1 = swap(grad, plan.sizes, (1, 0))
    packed = first_kernel(plan, kernel.transpose(1, 0, 2))
    shape = (2, 2 * plan.part_rows, plan.cells)
    acts = call("acts", functools.partial(acts_kernel, plan), jax.ShapeDtypeStruct(shape, act.dtype), [act, act1])
    shape = (2, plan.half_lanes, plan.cells)
    grads = call(
        "grads",
        functools.partial(grads_kernel, plan),
        jax.ShapeDtypeStruct(shape, grad.dtype),
        [grad0, grad1, *tops, *bottoms],
    )
    keep, come, packed = kernel_terms(plan, acts, grads, packed)
    packed, third, last0, last1 = packed
    shape = jax.ShapeDtypeStruct((images, rows, plan.half // 2, width), jnp.bfloat16)
    rest = jax.ShapeDtypeStruct((len(TAP_STEPS) * plan.half // 2, plan.cells), jnp.float32)
    own0, given0, rest = call(
        "early", functools.partial(early_kernel, plan), (shape, shape, rest), [packed, third, last0, grads]
    )
    theirs0 = swap(given0, plan.sizes, (1, 0))
    left = jax.ShapeDtypeStruct((len(TAP_STEPS) * plan.half // 2, plan.half_lanes), jnp.bfloat16)
    given1, left = call("given", functools.partial(given_kernel, plan), (shape, left), [last1, grads, rest])
    theirs1 = swap(given1, plan.sizes, (1, 0))
    own1 = call("own", functools.partial(own_kernel, plan), shape, [after(left, given1), grads, rest])
    shape = (images, rows, channels, width)
    terms = (len(TAP_STEPS) ** 2, plan.depth, plan.cols)
    total = call(
        "last", functools.partial(last_kernel, plan, scale), jax.ShapeDtypeStruct(terms, jnp.float32), [after(keep, own1), come]
    )
    input_grad, kernel_grad = call(
        "weave",
        functools.partial(weave_kernel, plan),
        (jax.ShapeDtypeStruct(shape, jnp.bfloat16), jax.ShapeDtypeStruct(terms, jnp.float32)),
        [own0, own1, theirs0, theirs1, total],
        [
            pltpu.VMEM(shape, jnp.bfloat16),
            pltpu.SemaphoreType.DMA((images, rows)),
            pltpu.SemaphoreType.DMA(()),
        ],
        far=2,
    )
    return input_grad.transpose(0, 2, 1, 3), kernel_grad.transpose(1, 0, 2)


def solution(mesh):
    in_specs = (
        P("band", None, "strip", None),
        P("band", None, "strip", None),
        P("band", None, "strip"),
    )
    out_specs = (P("band", None, "strip", None), P("band", None, "strip"))
    return jax.shard_map(body, mesh=mesh, in_specs=in_specs, out_specs=out_specs, check_vma=False)
```

```python
import functools
import math

import jax
import jax.numpy as jnp
from jax import lax
from jax.experimental import pallas as pl
from jax.experimental.pallas import tpu as pltpu
from jax.sharding import PartitionSpec as P

AXES = ("band", "strip")
TAP_STEPS = (-1, 0, 1)
LANES = 128
TOP_POWER = 2.0**15.5
LEAST_POWER = 2.0**-126
LEAST_PEAK = 1e-30
ROW_FIRST = False
VMEM_BYTES = 40 * 2**20
HINTS = {
    "edge": 8.0,
    "pair": 0.2,
    "pack": 8.0,
    "acts": 0.6,
    "grads": 0.5,
    "send0": 1.4,
    "send1": 1.4,
    "keep0": 1.0,
    "keep1": 1.0,
    "turn0": 0.9,
    "turn1": 0.6,
    "part0": 0.5,
    "part1": 0.3,
    "halve0": 0.5,
    "halve1": 3.0,
    "early": 1.7,
    "given": 0.5,
    "own": 0.5,
    "last": 8.0,
    "weave": 0.9,
}
FLOPS_PER_US = 1.15e9


def padded_lanes(count):
    return (count // LANES + 1) * LANES


def swap(value, sizes, *masks):
    bands, strips = sizes
    pairs = []
    for b in range(bands):
        for s in range(strips):
            masks_here = masks[b % len(masks)]
            pairs.append((b * strips + s, (b ^ masks_here[0]) * strips + (s ^ masks_here[1])))
    return lax.ppermute(value, AXES, pairs)


def call(name, kernel, out_shape, operands, scratch=(), far=0):
    outs = jax.tree.map(lambda _: pl.BlockSpec(memory_space=pltpu.VMEM), out_shape)
    if far:
        outs = outs[:-far] + (pl.BlockSpec(memory_space=pl.ANY),) * far
    return pl.pallas_call(
        kernel,
        out_shape=out_shape,
        in_specs=[pl.BlockSpec(memory_space=pltpu.VMEM)] * len(operands),
        out_specs=outs,
        scratch_shapes=list(scratch),
        compiler_params=pltpu.CompilerParams(vmem_limit_bytes=VMEM_BYTES),
        cost_estimate=pl.CostEstimate(
            flops=int(HINTS[name] * FLOPS_PER_US), bytes_accessed=0, transcendentals=0
        ),
        name=name,
    )(*operands)


def encoded(peak, value, used):
    lane = lax.broadcasted_iota(jnp.int32, value.shape, value.ndim - 1)
    ratio = value * (TOP_POWER / peak)
    square = ratio * ratio
    power = ratio * jnp.abs(ratio) * square * (square * square)
    return jnp.where(lane < used, power, peak).astype(jnp.bfloat16)


def decoded(message):
    power = message.astype(jnp.float32)
    peak = power[0:1, message.shape[1] - 1 : message.shape[1]]
    size = jnp.maximum(jnp.abs(power), LEAST_POWER)
    fourth = lax.rsqrt(lax.rsqrt(size))
    root = fourth * lax.rsqrt(fourth)
    return jnp.where(power < 0, -root, root) * (peak * (1.0 / TOP_POWER)), peak


def rounded_up(peak):
    return jnp.maximum(peak * (1.0 + 2.0**-6), LEAST_PEAK).astype(jnp.bfloat16).astype(jnp.float32)


def largest(value):
    return jnp.full((1, 1), jnp.max(jnp.abs(value)), jnp.float32)


def noted(peak, value, used):
    lane = lax.broadcasted_iota(jnp.int32, value.shape, value.ndim - 1)
    return jnp.where(lane < used, value, peak)


def added(keep, message):
    value, peak = decoded(message)
    return keep + value, peak + keep[0:1, keep.shape[1] - 1 : keep.shape[1]]


class Plan:
    def __init__(self, images, channels, rows, width, bands, strips):
        self.images, self.channels, self.rows, self.width = images, channels, rows, width
        self.bands, self.strips = bands, strips
        self.sizes = (bands, strips)
        self.depth = channels // bands
        self.cols = channels // strips
        self.blocks = bands // 2
        self.half = channels // 2
        self.strip_bits = strips.bit_length() - 1
        self.band_bits = bands.bit_length() - 1
        assert bands == 1 << self.band_bits and strips == 1 << self.strip_bits
        assert self.band_bits >= 3 and self.strip_bits >= 1
        self.top_strip = 1 << (self.strip_bits - 1)
        self.rest_strip = [1 << k for k in reversed(range(self.strip_bits - 1))]
        self.rest_band = [1 << k for k in range(3, self.band_bits)]
        self.inner = self.blocks // 4
        self.half_used = len(TAP_STEPS) * self.half
        self.half_lanes = padded_lanes(self.half_used)
        self.used = len(TAP_STEPS) * self.cols
        self.lanes = padded_lanes(self.used)
        self.block_rows = len(TAP_STEPS) * self.depth
        self.part_rows = self.inner * self.block_rows
        self.cells = 2 * images * rows * width
        by_row, by_next, by_col = (2, 0), (4, 0), (0, self.top_strip)
        self.term_masks = ((by_col, by_next), (by_row, by_col), (by_next, by_row))
        ones, others = (by_row, by_next) if ROW_FIRST else (by_next, by_row)
        self.gather_masks = ((ones, others), (others, by_col), (by_col, ones))

    def turned(self, slot):
        bits = self.band_bits - 3
        return sum(((slot >> k) & 1) << (bits - 1 - k) for k in range(bits))

    def block_of(self, slot, by_next, by_row):
        return self.turned(slot) * 4 + by_next * 2 + by_row

    def chunks(self):
        return [(d, n, h) for d in range(2) for n in range(self.images) for h in range(self.rows)]


def place(plan):
    band, strip = lax.axis_index("band"), lax.axis_index("strip")
    return band % 2, (band // 2) % 2, (band // 4) % 2, strip // plan.top_strip


def mine(plan):
    core, by_row, by_next, by_col = place(plan)
    order = ((by_col, by_row, by_next), (by_next, by_col, by_row))
    return [jnp.where(core == 0, a, b) for a, b in zip(*order)]


def grad_row(plan, grad_ref, top_ref, bottom_ref, image, row, start, strip):
    if row < 0:
        piece = top_ref[image, pl.ds(start, plan.half), :]
        return jnp.where(strip > 0, piece, jnp.zeros_like(piece))
    if row >= plan.rows:
        piece = bottom_ref[image, pl.ds(start, plan.half), :]
        return jnp.where(strip < plan.strips - 1, piece, jnp.zeros_like(piece))
    return grad_ref[image, row, pl.ds(start, plan.half), :]


def moved(value, step):
    width = value.shape[-1]
    if step == 0:
        return value
    lane = lax.broadcasted_iota(jnp.int32, value.shape, value.ndim - 1)
    turned = pltpu.roll(value, (-step) % width, value.ndim - 1)
    inside = lane < width - step if step > 0 else lane >= -step
    return jnp.where(inside, turned, 0.0)


def acts_kernel(plan, act0, act1, out):
    core = lax.axis_index("band") % 2
    depth, width = plan.depth, plan.width
    for at, (d, n, h) in enumerate(plan.chunks()):
        cells = (act0, act1)[d][n, h].astype(jnp.float32)
        shifted = []
        for m in range(plan.blocks):
            begin = 2 * m * depth
            even, odd = cells[begin : begin + depth], cells[begin + depth : begin + 2 * depth]
            block = jnp.where(core == 0, even, odd)
            shifted.append([moved(block, step) for step in TAP_STEPS])
        for i in range(2):
            pieces = []
            for j in range(2):
                for slot in range(plan.inner):
                    here, there = shifted[plan.block_of(slot, j, i)], shifted[plan.block_of(slot, i, j)]
                    pieces += here if i == j else [jnp.where(core == 0, a, b) for a, b in zip(here, there)]
            out[i, :, at * width : (at + 1) * width] = jnp.concatenate(pieces, axis=0).astype(jnp.bfloat16)


def grads_kernel(plan, grad0, grad1, top0, top1, bottom0, bottom1, out):
    strip = lax.axis_index("strip")
    half, width = plan.half, plan.width
    sources = ((grad0, top0, bottom0), (grad1, top1, bottom1))
    for at, (d, n, h) in enumerate(plan.chunks()):
        cells = slice(at * width, (at + 1) * width)
        for x in range(2):
            for r, row_step in enumerate(TAP_STEPS):
                out[x, r * half : (r + 1) * half, cells] = grad_row(
                    plan, *sources[d], n, h - row_step, x * half, strip
                )
            out[x, plan.half_used :, cells] = jnp.zeros((plan.half_lanes - plan.half_used, width), jnp.bfloat16)


def pair_terms(plan, acts, grads, first, second):
    core = lax.axis_index("band") % 2
    i, x = jnp.where(core == 0, second, first), jnp.where(core == 0, first, second)
    return lax.dot_general(acts[i], grads[x], (((1,), (1,)), ((), ())), preferred_element_type=jnp.float32)


def send_kernel(plan, same, acts, grads, out):
    first, second, _ = mine(plan)
    total = pair_terms(plan, acts, grads, 1 - first, second if same else 1 - second)
    peak = rounded_up(largest(total))
    for k in range(2):
        out[k] = encoded(peak, total[k * plan.part_rows : (k + 1) * plan.part_rows], plan.half_used)


def keep_kernel(plan, same, acts, grads, out):
    first, second, _ = mine(plan)
    total = pair_terms(plan, acts, grads, first, second if same else 1 - second)
    peak = largest(total)
    for k in range(2):
        out[k] = noted(peak, total[k * plan.part_rows : (k + 1) * plan.part_rows], plan.half_used)


def turn_kernel(plan, same, keep, message, out):
    for k in range(2):
        total, peak = added(keep[k], message[k])
        out[k] = noted(peak, total, plan.half_used) if same else encoded(rounded_up(peak), total, plan.half_used)


def part_kernel(plan, same, keep, message, out):
    third = mine(plan)[2]
    k = third if same else 1 - third
    total, peak = added(keep[k], message[k])
    out[...] = noted(peak, total, plan.half_used) if same else encoded(rounded_up(peak), total, plan.half_used)


def halve_kernel(plan, mask, used, same, keep, message, out):
    side = (lax.axis_index("band") // mask) % 2
    total, peak = added(keep[...], message[...])
    rows = total.shape[0] // 2
    lower, upper = total[:rows], total[rows:]
    if same:
        out[...] = noted(peak, jnp.where(side == 0, lower, upper), used)
    else:
        out[...] = encoded(rounded_up(peak), jnp.where(side == 0, upper, lower), used)


def pack_kernel(plan, kernel, out):
    rows = []
    for c in range(len(TAP_STEPS)):
        pieces = [kernel[r * len(TAP_STEPS) + c].astype(jnp.float32) for r in range(len(TAP_STEPS))]
        pieces.append(jnp.zeros((plan.depth, plan.lanes - plan.used), jnp.float32))
        rows.append(jnp.concatenate(pieces, axis=1))
    out[...] = jnp.concatenate(rows, axis=0).astype(jnp.bfloat16)


def halves(plan):
    core, row_bit, next_bit, _ = place(plan)
    by_row = (core == 0) != ROW_FIRST
    return jnp.where(by_row, row_bit, next_bit), jnp.where(by_row, next_bit, row_bit)


def ordered(plan, blocks):
    rest = lax.axis_index("band") // 8
    other_bit = halves(plan)[1]
    parts = [jnp.where(other_bit == 0, blocks[k], blocks[1 - k]).astype(jnp.float32) for k in range(2)]
    rows = []
    for c in range(len(TAP_STEPS)):
        for k in range(plan.inner):
            for part in parts:
                piece = None
                for at in range(plan.inner):
                    begin = plan.turned(at) * plan.block_rows + c * plan.depth
                    here = part[begin : begin + plan.depth]
                    piece = here if piece is None else jnp.where((k ^ rest) == at, here, piece)
                rows.append(piece)
    return jnp.concatenate(rows, axis=0).astype(jnp.bfloat16)


def summed(plan, product):
    quarter = plan.half // 2
    total = None
    for c, col_step in enumerate(TAP_STEPS):
        term = moved(product[c * quarter : (c + 1) * quarter], -col_step)
        total = term if total is None else total + term
    return total.astype(jnp.bfloat16)


def groups(plan):
    rows = [(n, h) for n in range(plan.images) for h in range(plan.rows)]
    for d in range(2):
        for begin in range(0, len(rows), 2):
            part = rows[begin : begin + 2]
            at = (d * len(rows) + begin) * plan.width
            where = [(n, h, slice(k * plan.width, (k + 1) * plan.width)) for k, (n, h) in enumerate(part)]
            yield d, slice(at, at + len(part) * plan.width), where


def early_kernel(plan, own, third, last0, grads, out0, out1, rest):
    core, _, _, col = place(plan)
    near, far = ordered(plan, own), [ordered(plan, third), ordered(plan, last0)]
    beside = jnp.where(core == 0, far[1], far[0])
    below = jnp.where(core == 0, far[0], far[1])
    for d, cells, where in groups(plan):
        here, there = grads[col, :, cells], grads[1 - col, :, cells]
        product = jnp.dot(near, here, preferred_element_type=jnp.float32)
        product = product + jnp.dot(beside, there, preferred_element_type=jnp.float32)
        rest[:, cells] = jnp.dot(below, here, preferred_element_type=jnp.float32)
        for n, h, lanes in where:
            (out0, out1)[d][n, h] = summed(plan, product[:, lanes])


def late_of(plan, image, left, grads, rest, out):
    col = place(plan)[3]
    for d, cells, where in groups(plan):
        if d == image:
            product = rest[:, cells]
            product = product + jnp.dot(left, grads[1 - col, :, cells], preferred_element_type=jnp.float32)
            for n, h, lanes in where:
                out[n, h] = summed(plan, product[:, lanes])


def given_kernel(plan, last1, grads, rest, out, left):
    left[...] = ordered(plan, last1)
    late_of(plan, 1, left[...], grads, rest, out)


def own_kernel(plan, left, grads, rest, out):
    late_of(plan, 0, left[...], grads, rest, out)


def pack_kernel(plan, kernel, out):
    rows = []
    for c in range(len(TAP_STEPS)):
        pieces = [kernel[r * len(TAP_STEPS) + c].astype(jnp.float32) for r in range(len(TAP_STEPS))]
        pieces.append(jnp.zeros((plan.depth, plan.lanes - plan.used), jnp.float32))
        rows.append(jnp.concatenate(pieces, axis=1))
    out[...] = jnp.concatenate(rows, axis=0).astype(jnp.bfloat16)


def halves(plan):
    core, row_bit, next_bit, _ = place(plan)
    by_row = (core == 0) != ROW_FIRST
    return jnp.where(by_row, row_bit, next_bit), jnp.where(by_row, next_bit, row_bit)


def ordered(plan, blocks):
    rest = lax.axis_index("band") // 8
    other_bit = halves(plan)[1]
    parts = [jnp.where(other_bit == 0, blocks[k], blocks[1 - k]).astype(jnp.float32) for k in range(2)]
    rows = []
    for c in range(len(TAP_STEPS)):
        for k in range(plan.inner):
            for part in parts:
                piece = None
                for at in range(plan.inner):
                    begin = plan.turned(at) * plan.block_rows + c * plan.depth
                    here = part[begin : begin + plan.depth]
                    piece = here if piece is None else jnp.where((k ^ rest) == at, here, piece)
                rows.append(piece)
    return jnp.concatenate(rows, axis=0).astype(jnp.bfloat16)


def summed(plan, product):
    quarter = plan.half // 2
    total = None
    for c, col_step in enumerate(TAP_STEPS):
        term = moved(product[c * quarter : (c + 1) * quarter], -col_step)
        total = term if total is None else total + term
    return total.astype(jnp.bfloat16)


def groups(plan):
    rows = [(n, h) for n in range(plan.images) for h in range(plan.rows)]
    for d in range(2):
        for begin in range(0, len(rows), 2):
            part = rows[begin : begin + 2]
            at = (d * len(rows) + begin) * plan.width
            where = [(n, h, slice(k * plan.width, (k + 1) * plan.width)) for k, (n, h) in enumerate(part)]
            yield d, slice(at, at + len(part) * plan.width), where


def early_kernel(plan, own, third, last0, grads, out0, out1, rest):
    core, _, _, col = place(plan)
    near, far = ordered(plan, own), [ordered(plan, third), ordered(plan, last0)]
    beside = jnp.where(core == 0, far[1], far[0])
    below = jnp.where(core == 0, far[0], far[1])
    for d, cells, where in groups(plan):
        here, there = grads[col, :, cells], grads[1 - col, :, cells]
        product = jnp.dot(near, here, preferred_element_type=jnp.float32)
        product = product + jnp.dot(beside, there, preferred_element_type=jnp.float32)
        rest[:, cells] = jnp.dot(below, here, preferred_element_type=jnp.float32)
        for n, h, lanes in where:
            (out0, out1)[d][n, h] = summed(plan, product[:, lanes])


def late_of(plan, image, left, grads, rest, out):
    col = place(plan)[3]
    for d, cells, where in groups(plan):
        if d == image:
            product = rest[:, cells]
            product = product + jnp.dot(left, grads[1 - col, :, cells], preferred_element_type=jnp.float32)
            for n, h, lanes in where:
                out[n, h] = summed(plan, product[:, lanes])


def given_kernel(plan, last1, grads, rest, out, left):
    left[...] = ordered(plan, last1)
    late_of(plan, 1, left[...], grads, rest, out)


def own_kernel(plan, left, grads, rest, out):
    late_of(plan, 0, left[...], grads, rest, out)


def last_kernel(plan, scale, keep, message, out):
    total = added(keep[...], message[...])[0] * scale
    depth, cols = plan.depth, plan.cols
    for r in range(len(TAP_STEPS)):
        for c in range(len(TAP_STEPS)):
            out[r * len(TAP_STEPS) + c] = total[c * depth : (c + 1) * depth, r * cols : (r + 1) * cols]


def last_kernel(plan, scale, keep, message, out):
    total = added(keep[...], message[...])[0] * scale
    depth, cols = plan.depth, plan.cols
    for r in range(len(TAP_STEPS)):
        for c in range(len(TAP_STEPS)):
            out[r * len(TAP_STEPS) + c] = total[c * depth : (c + 1) * depth, r * cols : (r + 1) * cols]


def weave_kernel(plan, own0, own1, theirs0, theirs1, terms, far, far_terms, out, sems, sem):
    copies = [pltpu.make_async_copy(terms, far_terms, sem)]
    copies[0].start()
    core, row_bit, next_bit, _ = place(plan)
    depth = plan.depth
    for n in range(plan.images):
        for h in range(plan.rows):
            mine = [ref[n, h].astype(jnp.float32) for ref in (own0, own1)]
            others = [ref[n, h].astype(jnp.float32) for ref in (theirs0, theirs1)]
            even = [jnp.where(core == 0, a, b) for a, b in zip(mine, others)]
            odd = [jnp.where(core == 0, b, a) for a, b in zip(mine, others)]
            pieces = []
            for m in range(plan.blocks):
                for p, here in enumerate((even, odd)):
                    by_row = (p == 0) != ROW_FIRST
                    bit, other, ours = (m % 2, m // 2 % 2, row_bit) if by_row else (m // 2 % 2, m % 2, next_bit)
                    at = slice((m // 4 * 2 + other) * depth, (m // 4 * 2 + other + 1) * depth)
                    pieces.append(jnp.where(bit == ours, here[0][at], here[1][at]))
            out[n, h] = jnp.concatenate(pieces, axis=0).astype(jnp.bfloat16)
            copies.append(pltpu.make_async_copy(out.at[n, h], far.at[n, h], sems.at[n, h]))
            copies[-1].start()
    for copy in copies:
        copy.wait()


def after(value, *others):
    return lax.optimization_barrier((value, *others))[0]


def pair_kernel(plan, *refs):
    blocks = [ref[k].astype(jnp.float32) for ref in refs[:-1] for k in range(ref.shape[0])]
    refs[-1][0] = jnp.concatenate(blocks, axis=0).astype(jnp.bfloat16)


def first_kernel(plan, kernel):
    shape = jax.ShapeDtypeStruct((plan.block_rows, plan.lanes), jnp.bfloat16)
    packed = call("pack", functools.partial(pack_kernel, plan), shape, [kernel])[None]
    for mask in plan.rest_band[:0:-1]:
        packed = jnp.concatenate([packed, swap(packed, plan.sizes, (mask, 0))], axis=0)
    return [packed] + [swap(packed, plan.sizes, (mask, 0)) for mask in plan.rest_band[:1]]


def more_kernel(plan, packed, start, end, last):
    sizes = plan.sizes
    packed = [*packed[:-1], after(packed[-1], start)]
    if plan.rest_strip:
        packed = jnp.concatenate(packed, axis=0)[None]
        for mask in reversed(plan.rest_strip):
            packed = jnp.concatenate([packed, swap(packed, sizes, (0, mask))], axis=0)
        count = packed.shape[0]
        order = jnp.arange(count) ^ (lax.axis_index("strip") % count)
        packed = jnp.take(packed, order, axis=0)[..., : plan.used]
        packed = packed.reshape(count, plan.inner, plan.block_rows, len(TAP_STEPS), plan.cols)
        packed = packed.transpose(1, 2, 3, 0, 4).reshape(plan.inner, plan.block_rows, plan.half_used)
        packed = [jnp.pad(packed, ((0, 0), (0, 0), (0, plan.half_lanes - plan.half_used)))]
    shape = jax.ShapeDtypeStruct((1, plan.part_rows, plan.half_lanes), jnp.bfloat16)
    packed = after(call("pair", functools.partial(pair_kernel, plan), shape, packed), start)
    come = after(swap(packed, sizes, *plan.gather_masks[0]), end)
    packed = after(jnp.concatenate([packed, come], axis=0), end)
    third = swap(packed, sizes, *plan.gather_masks[1])
    return packed, third, swap(after(packed, last), sizes, *plan.gather_masks[2])


def narrowed(plan, total):
    rows = total.shape[0]
    total = total[:, : plan.half_used].reshape(rows, len(TAP_STEPS), plan.half)
    for mask in plan.rest_strip:
        side = (lax.axis_index("strip") // mask) % 2
        parts = total.reshape(rows, len(TAP_STEPS), 2, total.shape[2] // 2)
        kept = jnp.where(side == 0, parts[:, :, 0], parts[:, :, 1])
        given = jnp.where(side == 0, parts[:, :, 1], parts[:, :, 0])
        total = kept + swap(given, plan.sizes, (0, mask))
    total = total.reshape(rows, plan.used)
    return noted(largest(total), jnp.pad(total, ((0, 0), (0, plan.lanes - plan.used))), plan.used)


def kernel_terms(plan, acts, grads, packed):
    sizes, f32 = plan.sizes, jnp.float32
    rows, lanes = plan.part_rows, plan.half_lanes

    def run(name, kernel, shape, kind, operands):
        return call(name, kernel, jax.ShapeDtypeStruct(shape, kind), operands)

    part = functools.partial
    b16 = jnp.bfloat16
    shape = (2, rows, lanes)
    send0 = run("send0", part(send_kernel, plan, False), shape, b16, [acts, grads])
    come0 = swap(send0, sizes, *plan.term_masks[0])
    send1 = run("send1", part(send_kernel, plan, True), shape, b16, [after(acts, send0), grads])
    come1 = swap(send1, sizes, *plan.term_masks[0])
    keep0 = run("keep0", part(keep_kernel, plan, False), shape, f32, [after(acts, send1), grads])
    send = run("turn0", part(turn_kernel, plan, False), shape, b16, [keep0, come0])
    come = swap(send, sizes, *plan.term_masks[1])
    keep1 = run("keep1", part(keep_kernel, plan, True), shape, f32, [after(acts, send), grads])
    keep = run("turn1", part(turn_kernel, plan, True), shape, f32, [keep1, come1])
    packed, third, last0 = more_kernel(plan, packed, keep0, send, keep1)
    shape = shape[1:]
    send = run("part0", part(part_kernel, plan, False), shape, b16, [keep, come])
    last1 = swap(after(third, send), sizes, *plan.gather_masks[2])
    keep = run("part1", part(part_kernel, plan, True), shape, f32, [after(keep, send), come])
    come = swap(send, sizes, *plan.term_masks[2])
    if plan.rest_strip:
        keep = narrowed(plan, added(keep, come)[0])
        come = jnp.zeros(keep.shape, b16)
    for mask in plan.rest_band:
        rows //= 2
        shape = (rows, plan.lanes)
        halve = part(halve_kernel, plan, mask, plan.used)
        send = run("halve0", part(halve, False), shape, b16, [keep, come])
        keep = run("halve1", part(halve, True), shape, f32, [after(keep, send, last0), come])
        come = swap(send, sizes, (mask, 0))
    return keep, come, (after(packed, keep), third, last0, last1)


def edge_kernel(plan, grad, out, copy):
    strip = lax.axis_index("strip")
    for n in range(plan.images):
        out[n] = jnp.where(strip == 0, grad[n, plan.rows - 1], grad[n, 0])
    copy[...] = grad[...]


def borders(plan, grad):
    if plan.strips == 2:
        shape = jax.ShapeDtypeStruct((plan.images, plan.channels, plan.width), grad.dtype)
        copy = jax.ShapeDtypeStruct(grad.shape, grad.dtype)
        edge, grad = call("edge", functools.partial(edge_kernel, plan), (shape, copy), [grad])
        come = [swap(edge, plan.sizes, (core, 1)) for core in range(2)]
        return grad, come, come
    first, last = grad[:, 0], grad[:, plan.rows - 1]
    tops, bottoms = [], []
    for core in range(2):
        down = []
        for b in range(plan.bands):
            down += [(b * plan.strips + s, (b ^ core) * plan.strips + s + 1) for s in range(plan.strips - 1)]
        tops.append(lax.ppermute(last, AXES, down))
        bottoms.append(lax.ppermute(first, AXES, [(b, a) for a, b in down]))
    return grad, tops, bottoms


def body(activations, out_grad, kernel):
    images, channels, rows, width = activations.shape
    bands, strips = lax.axis_size("band"), lax.axis_size("strip")
    plan = Plan(images, channels, rows, width, bands, strips)
    scale = 1.0 / math.sqrt(images * bands * rows * strips * width)
    act = activations.transpose(0, 2, 1, 3)
    grad = out_grad.transpose(0, 2, 1, 3)
    grad0, tops, bottoms = borders(plan, grad)
    act1 = swap(act, plan.sizes, (1, 0))
    grad1 = swap(grad, plan.sizes, (1, 0))
    packed = first_kernel(plan, kernel.transpose(1, 0, 2))
    shape = (2, 2 * plan.part_rows, plan.cells)
    acts = call("acts", functools.partial(acts_kernel, plan), jax.ShapeDtypeStruct(shape, act.dtype), [act, act1])
    shape = (2, plan.half_lanes, plan.cells)
    grads = call(
        "grads",
        functools.partial(grads_kernel, plan),
        jax.ShapeDtypeStruct(shape, grad.dtype),
        [grad0, grad1, *tops, *bottoms],
    )
    keep, come, packed = kernel_terms(plan, acts, grads, packed)
    packed, third, last0, last1 = packed
    shape = jax.ShapeDtypeStruct((images, rows, plan.half // 2, width), jnp.bfloat16)
    rest = jax.ShapeDtypeStruct((len(TAP_STEPS) * plan.half // 2, plan.cells), jnp.float32)
    own0, given0, rest = call(
        "early", functools.partial(early_kernel, plan), (shape, shape, rest), [packed, third, last0, grads]
    )
    theirs0 = swap(given0, plan.sizes, (1, 0))
    left = jax.ShapeDtypeStruct((len(TAP_STEPS) * plan.half // 2, plan.half_lanes), jnp.bfloat16)
    given1, left = call("given", functools.partial(given_kernel, plan), (shape, left), [last1, grads, rest])
    theirs1 = swap(given1, plan.sizes, (1, 0))
    own1 = call("own", functools.partial(own_kernel, plan), shape, [after(left, given1), grads, rest])
    shape = (images, rows, channels, width)
    terms = (len(TAP_STEPS) ** 2, plan.depth, plan.cols)
    total = call(
        "last", functools.partial(last_kernel, plan, scale), jax.ShapeDtypeStruct(terms, jnp.float32), [after(keep, own1), come]
    )
    input_grad, kernel_grad = call(
        "weave",
        functools.partial(weave_kernel, plan),
        (jax.ShapeDtypeStruct(shape, jnp.bfloat16), jax.ShapeDtypeStruct(terms, jnp.float32)),
        [own0, own1, theirs0, theirs1, total],
        [
            pltpu.VMEM(shape, jnp.bfloat16),
            pltpu.SemaphoreType.DMA((images, rows)),
            pltpu.SemaphoreType.DMA(()),
        ],
        far=2,
    )
    return input_grad.transpose(0, 2, 1, 3), kernel_grad.transpose(1, 0, 2)


def solution(mesh):
    in_specs = (
        P("band", None, "strip", None),
        P("band", None, "strip", None),
        P("band", None, "strip"),
    )
    out_specs = (P("band", None, "strip", None), P("band", None, "strip"))
    return jax.shard_map(body, mesh=mesh, in_specs=in_specs, out_specs=out_specs, check_vma=False)
```
